32 devices in a mesh: chan: 8 (over y, x, core), tile: 4 (over z).
Axes of the slice: x: 2, y: 2, z: 4, core: 2. Of those that a mesh axis runs over, the one named last changes fastest.
Arguments:
- voltages: bfloat16 [4, 16, 555008], P('tile', 'chan'), may hold values from -6 to 6
- fir_taps: float32 [16, 2048], replicated, may hold values from -4 to 4
- channels: int32 [8], replicated, may hold values from 0 to 2047
- input_good_mask: int32 [4, 16], P('tile', 'chan'), may hold values 0 or 1
- tile_map: int32 [8, 4], replicated, may hold values from 0 to 3, each once within a row
Outputs:
- visibilities: bfloat16 [8, 4, 2, 32, 32], P('chan', 'tile')
The draws below stay inside these ranges and needn't reach their ends.
Inputs may be any that keep to these rules, and one draw needn't show every extreme that they name: `tile_map`: for every channel, every tile of the 2 x 2 grid, numbered row by row, stands in exactly one slot.
All inputs are finite; a program needn't handle non-finite values. No bound on the sum of `input_good_mask` on one device may be relied on, other than what follows from the above.
Results may differ from the reference program's by a relative error of at most 0.0077.
Values may be sent and summed in bfloat16 or wider, within the bound.
No kernel may reach another device: no remote copies, remote signals or barrier semaphores. Data moves between devices by JAX's collectives and lax.ppermute only.
A program may use at most 64 MiB of HBM per device.

```python
import math
import jax
import jax.numpy as jnp
from jax import lax

TRANSFORM_LENGTH = 2048
FILTER_TAPS = 16
SPECTRA_SUMMED = 256
CHANS = 8
INPUTS = 64
PIECE = 16
GRID = 2
TILE_SIDE = 32
SAMPLES = 555008
N_TILE = 4


def with_ends(entries, rng, least, top_value):
    longest = entries.shape.index(max(entries.shape))
    spots = []
    for shift in (0, 1):
        where = [jax.random.randint(jax.random.fold_in(rng, axis), (), 0, length) for axis, length in enumerate(entries.shape)]
        where[longest] = (where[longest] + shift) % entries.shape[longest]
        spots.append(tuple(where))
    return entries.at[spots[0]].set(least).at[spots[1]].set(top_value)


def level_of(key, shape, split, low, largest):
    gain, own = 1.0, jax.random.fold_in(key, 6)
    for dim, shards_of in split:
        steps = jnp.exp(jax.random.uniform(jax.random.fold_in(own, dim), (shards_of,), jnp.float32, low / len(split), largest / len(split)))
        gain = gain * jnp.repeat(steps, shape[dim] // shards_of).reshape([-1 if axis == dim else 1 for axis in range(len(shape))])
    return gain


def centred(key, extent, deviation, most, split=(), kind=jnp.bfloat16):
    result = deviation * jax.random.normal(key, extent, jnp.float32)
    if split:
        result = result * level_of(key, extent, split, -0.22, 0.18)
    return jnp.clip(result, -most, most).astype(kind)


def setup_inputs(seed: int = 0) -> dict:
    keys = jax.random.split(jax.random.key(seed), 6)
    return {
        "voltages": centred(keys[0], (N_TILE, PIECE, SAMPLES), 1.0, 6.0, ((0, 4), (1, 8))),
        "fir_taps": centred(keys[1], (FILTER_TAPS, TRANSFORM_LENGTH), 0.25, 4.0, (), jnp.float32),
        "channels": with_ends(jax.random.randint(keys[2], (CHANS,), 0, TRANSFORM_LENGTH), jax.random.fold_in(keys[2], 1), 0, TRANSFORM_LENGTH - 1).astype(jnp.int32),
        "input_good_mask": with_ends((jax.random.randint(keys[3], (N_TILE, PIECE), 0, 8) < 7).astype(jnp.int32), jax.random.fold_in(keys[3], 1), 0, 1),
        "tile_map": jax.vmap(lambda own: jax.random.permutation(own, N_TILE))(jax.random.split(keys[4], CHANS)).reshape((CHANS, N_TILE)).astype(jnp.int32),
    }


def dft_rows(channels):
    sample = jnp.arange(TRANSFORM_LENGTH, dtype=jnp.int32)
    phase = channels[:, None].astype(jnp.int32) * sample[None, :] % TRANSFORM_LENGTH
    angle = phase.astype(jnp.float32) * (2.0 * math.pi / TRANSFORM_LENGTH)
    factor = 1.0 / math.sqrt(TRANSFORM_LENGTH)
    return jnp.concatenate([jnp.cos(angle) * factor, -jnp.sin(angle) * factor], axis=0).astype(jnp.bfloat16)

def filtered_block(sample_block, fir_taps):
    running_total = jnp.zeros((sample_block.shape[0], SPECTRA_SUMMED, TRANSFORM_LENGTH), jnp.float32)
    for tap_index in range(FILTER_TAPS):
        running_total = running_total + fir_taps[tap_index][None, None, :] * sample_block[:, tap_index:tap_index + SPECTRA_SUMMED, :].astype(jnp.float32)
    return running_total.astype(jnp.bfloat16)

def reference(voltages, fir_taps, channels, input_good_mask, tile_map):
    dft_table = dft_rows(channels).astype(jnp.float32)
    blocks = voltages.reshape(N_TILE, PIECE, SPECTRA_SUMMED + FILTER_TAPS - 1, TRANSFORM_LENGTH)
    flag_rows = input_good_mask.astype(jnp.float32)

    def one_group(operands):
        sample_block, flag_row = operands
        filtered = filtered_block(sample_block, fir_taps).astype(jnp.float32)
        spectra = jnp.einsum('kn,bsn->kbs', dft_table, filtered)
        return (spectra * flag_row[None, :, None]).astype(jnp.bfloat16)
    groups = lax.map(one_group, (blocks, flag_rows))
    spectra_all = jnp.transpose(groups, (1, 0, 2, 3)).reshape(2, CHANS, INPUTS, SPECTRA_SUMMED)
    per_channel = jnp.transpose(spectra_all, (1, 0, 2, 3))

    def one_channel(operands):
        chan_data, slot_tiles = operands
        chan_data = chan_data.astype(jnp.float32)

        def one_slot(slot):
            tile = slot_tiles[slot]
            row_start = (tile // GRID * TILE_SIDE).astype(jnp.int32)
            col_start = (tile % GRID * TILE_SIDE).astype(jnp.int32)
            rows = lax.dynamic_slice_in_dim(chan_data, row_start, TILE_SIDE, 1)
            cols = lax.dynamic_slice_in_dim(chan_data, col_start, TILE_SIDE, 1)
            swapped = jnp.stack([cols[1], -cols[0]], axis=0)
            real_part = jnp.einsum('xis,xjs->ij', rows, cols)
            imag_part = jnp.einsum('xis,xjs->ij', rows, swapped)
            return (jnp.stack([real_part, imag_part], axis=0) * (1.0 / SPECTRA_SUMMED)).astype(jnp.bfloat16)
        return lax.map(one_slot, jnp.arange(N_TILE, dtype=jnp.int32))
    return lax.map(one_channel, (per_channel, tile_map))
```

```python
import math

import jax
import jax.numpy as jnp
from jax import lax
from jax.sharding import PartitionSpec as P

TRANSFORM_LENGTH = 2048
FILTER_TAPS = 16
SPECTRA_SUMMED = 256


def dft_rows(channels):
    sample = jnp.arange(TRANSFORM_LENGTH, dtype=jnp.int32)
    phase = channels[:, None] * sample[None, :] % TRANSFORM_LENGTH
    angle = phase.astype(jnp.float32) * (2.0 * math.pi / TRANSFORM_LENGTH)
    factor = 1.0 / math.sqrt(TRANSFORM_LENGTH)
    return jnp.concatenate([jnp.cos(angle) * factor, -jnp.sin(angle) * factor], axis=0)


def on_device(voltages, fir_taps, channels, input_good_mask, tile_map):
    own = voltages.shape[1]
    chans = channels.shape[0]
    n_chan = lax.axis_size("chan")
    n_tile = lax.axis_size("tile")
    per = chans // n_chan
    frames = SPECTRA_SUMMED + FILTER_TAPS - 1
    samples = voltages.reshape(own, frames, TRANSFORM_LENGTH)
    table = dft_rows(channels)
    combined = (fir_taps[:, None, :] * table[None, :, :]).astype(jnp.bfloat16)
    combined = combined.reshape(FILTER_TAPS * 2 * chans, TRANSFORM_LENGTH)
    partial = jnp.einsum("kn,amn->kam", combined, samples, preferred_element_type=jnp.float32)
    partial = partial.reshape(FILTER_TAPS, 2 * chans, own, frames)
    spectra = partial[0, :, :, :SPECTRA_SUMMED]
    for tap in range(1, FILTER_TAPS):
        spectra = spectra + partial[tap, :, :, tap : tap + SPECTRA_SUMMED]
    flags = input_good_mask.reshape(1, own, 1).astype(jnp.float32)
    spectra = (spectra * flags).astype(jnp.bfloat16)
    spectra = spectra.reshape(2, n_chan, per, own, SPECTRA_SUMMED).transpose(1, 2, 3, 0, 4)
    spectra = spectra.reshape(1, n_chan, per, own, 2 * SPECTRA_SUMMED)
    spectra = jnp.broadcast_to(spectra, (n_tile,) + spectra.shape[1:])
    spectra = spectra.reshape(n_tile * n_chan, per, own, 2 * SPECTRA_SUMMED)
    turned = lax.all_to_all(spectra, ("tile", "chan"), split_axis=0, concat_axis=0, tiled=True)
    whole = turned.transpose(1, 0, 2, 3).reshape(per, n_tile * n_chan * own, 2, SPECTRA_SUMMED)
    grid_side = n_tile // 8 + 2
    side = whole.shape[1] // grid_side
    tile = tile_map[lax.axis_index("chan") * per, lax.axis_index("tile")]
    row_start = tile // grid_side * side
    col_start = tile % grid_side * side
    rows = lax.dynamic_slice_in_dim(whole, row_start, side, 1)
    cols = lax.dynamic_slice_in_dim(whole, col_start, side, 1)
    swapped = jnp.stack([cols[:, :, 1], -cols[:, :, 0]], axis=2)
    real_part = jnp.einsum("cixs,cjxs->cij", rows, cols, preferred_element_type=jnp.float32)
    imag_part = jnp.einsum("cixs,cjxs->cij", rows, swapped, preferred_element_type=jnp.float32)
    visible = (jnp.stack([real_part, imag_part], axis=1) * (1.0 / SPECTRA_SUMMED)).astype(
        jnp.bfloat16
    )
    return visible.reshape(visible.shape[0], 1, 2, side, side)


def solution(mesh):
    in_specs = (P("tile", "chan", None), P(), P(), P("tile", "chan"), P())
    out_specs = P("chan", "tile", None, None, None)
    return jax.shard_map(
        on_device, mesh=mesh, in_specs=in_specs, out_specs=out_specs, check_vma=False
    )
```

```python
import math

import jax
import jax.numpy as jnp
from jax import lax
from jax.sharding import PartitionSpec as P

TRANSFORM_LENGTH = 2048
FILTER_TAPS = 16
SPECTRA_SUMMED = 256


def dft_rows(channels):
    sample = jnp.arange(TRANSFORM_LENGTH, dtype=jnp.int32)
    phase = channels[:, None] * sample[None, :] % TRANSFORM_LENGTH
    angle = phase.astype(jnp.float32) * (2.0 * math.pi / TRANSFORM_LENGTH)
    factor = 1.0 / math.sqrt(TRANSFORM_LENGTH)
    return jnp.concatenate([jnp.cos(angle) * factor, -jnp.sin(angle) * factor], axis=0)


def on_device(voltages, fir_taps, channels, input_good_mask, tile_map):
    own = voltages.shape[1]
    chans = channels.shape[0]
    n_chan = lax.axis_size("chan")
    n_tile = lax.axis_size("tile")
    per = chans // n_chan
    frames = SPECTRA_SUMMED + FILTER_TAPS - 1
    samples = voltages.reshape(own, frames, TRANSFORM_LENGTH)
    table = dft_rows(channels)
    combined = (fir_taps[:, None, :] * table[None, :, :]).astype(jnp.bfloat16)
    combined = combined.reshape(FILTER_TAPS * 2 * chans, TRANSFORM_LENGTH)
    partial = jnp.einsum("kn,amn->kam", combined, samples, preferred_element_type=jnp.float32)
    partial = partial.reshape(FILTER_TAPS, 2 * chans, own, frames)
    spectra = partial[0, :, :, :SPECTRA_SUMMED]
    for tap in range(1, FILTER_TAPS):
        spectra = spectra + partial[tap, :, :, tap : tap + SPECTRA_SUMMED]
    flags = input_good_mask.reshape(1, own, 1).astype(jnp.float32)
    spectra = (spectra * flags).astype(jnp.bfloat16)
    spectra = spectra.reshape(2, n_chan, per, own, SPECTRA_SUMMED).transpose(1, 2, 3, 0, 4)
    spectra = spectra.reshape(n_chan, per, own, 2 * SPECTRA_SUMMED)
    my_chan, my_tile = lax.axis_index("chan"), lax.axis_index("tile")
    if n_chan <= 8:
        pieces = []
        for d in range(n_chan):
            piece = lax.dynamic_index_in_dim(spectra, my_chan ^ d, 0, keepdims=False)
            if d:
                piece = lax.ppermute(piece, "chan", [(i, i ^ d) for i in range(n_chan)])
            pieces.append(piece)
        column = jnp.stack(pieces)
        blocks = [column]
        for e in range(1, n_tile):
            blocks.append(lax.ppermute(column, "tile", [(i, i ^ e) for i in range(n_tile)]))
        turned = jnp.stack(blocks)
        turned = turned[my_tile ^ jnp.arange(n_tile)][:, my_chan ^ jnp.arange(n_chan)]
    else:
        spectra = jnp.broadcast_to(spectra[None], (n_tile,) + spectra.shape)
        spectra = spectra.reshape((n_tile * n_chan,) + spectra.shape[2:])
        turned = lax.all_to_all(spectra, ("tile", "chan"), split_axis=0, concat_axis=0, tiled=True)
    turned = turned.reshape(n_tile * n_chan, per, own, 2 * SPECTRA_SUMMED)
    whole = turned.transpose(1, 0, 2, 3).reshape(per, n_tile * n_chan * own, 2, SPECTRA_SUMMED)
    grid_side = n_tile // 8 + 2
    side = whole.shape[1] // grid_side
    tile = tile_map[lax.axis_index("chan") * per, lax.axis_index("tile")]
    row_start = tile // grid_side * side
    col_start = tile % grid_side * side
    rows = lax.dynamic_slice_in_dim(whole, row_start, side, 1)
    cols = lax.dynamic_slice_in_dim(whole, col_start, side, 1)
    swapped = jnp.stack([cols[:, :, 1], -cols[:, :, 0]], axis=2)
    real_part = jnp.einsum("cixs,cjxs->cij", rows, cols, preferred_element_type=jnp.float32)
    imag_part = jnp.einsum("cixs,cjxs->cij", rows, swapped, preferred_element_type=jnp.float32)
    visible = (jnp.stack([real_part, imag_part], axis=1) * (1.0 / SPECTRA_SUMMED)).astype(
        jnp.bfloat16
    )
    return visible.reshape(visible.shape[0], 1, 2, side, side)


def solution(mesh):
    in_specs = (P("tile", "chan", None), P(), P(), P("tile", "chan"), P())
    out_specs = P("chan", "tile", None, None, None)
    return jax.shard_map(
        on_device, mesh=mesh, in_specs=in_specs, out_specs=out_specs, check_vma=False
    )
```

```python
import functools
import math

import jax
import jax.numpy as jnp
from jax import lax
from jax.experimental import pallas as pl
from jax.experimental.pallas import tpu as pltpu
from jax.sharding import PartitionSpec as P

TRANSFORM_LENGTH = 2048
FILTER_TAPS = 16
SPECTRA_SUMMED = 256
FRAMES = SPECTRA_SUMMED + FILTER_TAPS - 1
ROWS = 272
LANES = 128
BLOCKS = TRANSFORM_LENGTH // LANES
HALVES = SPECTRA_SUMMED // LANES
CHUNKS = 4


def build_table(chans, channels_ref, taps_ref, table_ref):
    row = lax.broadcasted_iota(jnp.int32, (chans, LANES), 0)
    lane = lax.broadcasted_iota(jnp.int32, (chans, LANES), 1)
    channel = jnp.zeros((chans, LANES), jnp.int32)
    for c in range(chans):
        channel = jnp.where(row == c, channels_ref[c], channel)

    def unit(phase):
        angle = (phase & (TRANSFORM_LENGTH - 1)).astype(jnp.float32) * (
            2.0 * math.pi / TRANSFORM_LENGTH
        )
        return jnp.cos(angle), jnp.sin(angle)

    factor = 1.0 / math.sqrt(TRANSFORM_LENGTH)
    cos0, sin0 = unit(channel * lane)
    blocks = [(cos0 * factor, sin0 * factor)]
    for bit in range(BLOCKS.bit_length() - 1):
        cos1, sin1 = unit(channel * (LANES << bit))
        blocks += [(c * cos1 - s * sin1, s * cos1 + c * sin1) for c, s in blocks]
    for nb, (cosine, sine) in enumerate(blocks):
        columns = slice(nb * LANES, (nb + 1) * LANES)
        dft = jnp.concatenate([cosine, -sine], axis=0)
        for tap in range(FILTER_TAPS):
            table_ref[tap * 2 * chans : (tap + 1) * 2 * chans, columns] = (
                dft * taps_ref[tap : tap + 1, columns]
            ).astype(jnp.bfloat16)


def front_kernel(
    own, chans, copies, channels_ref, mask_ref, taps_ref, x_hbm, out_ref,
    x_ref, wide_ref, sorted_ref, table_ref, partial_ref, fold_ref, block_ref, sems,
):
    per_frame = BLOCKS * own
    bounds = [FRAMES * step // CHUNKS * per_frame for step in range(CHUNKS + 1)]
    transfers = []
    for step in range(CHUNKS):
        part = pl.ds(bounds[step], bounds[step + 1] - bounds[step])
        transfers.append(pltpu.make_async_copy(x_hbm.at[part], x_ref.at[part], sems.at[step]))
    for transfer in transfers:
        transfer.start()
    build_table(chans, channels_ref, taps_ref, table_ref)
    for step, transfer in enumerate(transfers):
        transfer.wait()
        part = pl.ds(bounds[step], bounds[step + 1] - bounds[step])
        wide_ref[part, :] = x_ref[part, :].astype(jnp.float32)
    for nb in range(BLOCKS):
        for i in range(own):
            sorted_ref[i * ROWS : (i + 1) * ROWS, nb * LANES : (nb + 1) * LANES] = wide_ref[
                pl.ds(nb * own + i, ROWS, stride=per_frame), :
            ].astype(jnp.bfloat16)
    partial_ref[...] = lax.dot_general(
        sorted_ref[...], table_ref[...], (((1,), (1,)), ((), ())),
        preferred_element_type=jnp.float32,
    )
    kinds = 2 * chans
    together = LANES // kinds
    kept = -(-(SPECTRA_SUMMED + together - 1) // 8) * 8
    for i in range(own):
        folded = partial_ref[pl.ds(i * ROWS, kept), :LANES]
        for group in range(1, FILTER_TAPS // together):
            folded = folded + partial_ref[
                pl.ds(i * ROWS + group * together, kept), group * LANES : (group + 1) * LANES
            ]
        fold_ref[:kept, :] = folded
        turned = fold_ref[...].T
        spectra = turned[:kinds, :SPECTRA_SUMMED]
        for tap in range(1, together):
            shifted = pltpu.roll(
                turned[tap * kinds : (tap + 1) * kinds, :], turned.shape[1] - tap, axis=1
            )
            spectra = spectra + shifted[:, :SPECTRA_SUMMED]
        spectra = spectra * mask_ref[0, i].astype(jnp.float32)
        for half in range(HALVES):
            for q in range(2):
                block_ref[pl.ds((i * HALVES + half) * 2 + q, chans, stride=4 * own), :] = spectra[
                    q * chans : (q + 1) * chans, half * LANES : (half + 1) * LANES
                ]
    block = block_ref[...].astype(jnp.bfloat16)
    for copy in range(copies):
        out_ref[copy] = block


def back_kernel(own, grid_side, tile_map_ref, blocks_ref, out_ref, wide_ref, signal_ref):
    sources = blocks_ref.shape[0]
    inputs = sources * own
    side = inputs // grid_side
    per_block = blocks_ref.shape[1]
    tile = tile_map_ref[lax.axis_index("tile"), lax.axis_index("chan")]
    wide_ref[...] = blocks_ref[...].reshape(sources * per_block, LANES).astype(jnp.float32)
    for i in range(own):
        for half in range(HALVES):
            for q in range(2):
                signal_ref[q * HALVES + half, pl.ds(i, sources, stride=own), :] = wide_ref[
                    pl.ds((i * HALVES + half) * 2 + q, sources, stride=per_block), :
                ]
    row_start = pl.multiple_of(tile // grid_side * side, side)
    col_start = pl.multiple_of(tile % grid_side * side, side)

    def inputs_from(start):
        planes = [signal_ref[plane, pl.ds(start, side), :] for plane in range(2 * HALVES)]
        return jnp.concatenate(planes, axis=1).astype(jnp.bfloat16)

    rows, cols = inputs_from(row_start), inputs_from(col_start)
    swapped = jnp.concatenate([cols[:, SPECTRA_SUMMED:], -cols[:, :SPECTRA_SUMMED]], axis=1)
    for part, right in enumerate((cols, swapped)):
        product = lax.dot_general(
            rows, right, (((1,), (1,)), ((), ())), preferred_element_type=jnp.float32
        )
        out_ref[0, 0, part] = (product * (1.0 / SPECTRA_SUMMED)).astype(jnp.bfloat16)


def on_device(voltages, fir_taps, channels, input_good_mask, tile_map):
    own = voltages.shape[1]
    chans = channels.shape[0]
    n_chan = lax.axis_size("chan")
    n_tile = lax.axis_size("tile")
    assert chans == n_chan and 2 * chans <= LANES
    lines = FRAMES * BLOCKS * own
    x = voltages.reshape(own, FRAMES * BLOCKS, LANES).transpose(1, 0, 2).reshape(lines, LANES)
    smem = pl.BlockSpec(memory_space=pltpu.SMEM)
    vmem = pl.BlockSpec(memory_space=pltpu.VMEM)
    per_block = 2 * HALVES * own
    kinds = 2 * chans
    folded_rows = SPECTRA_SUMMED + (LANES if kinds < LANES else 0)
    spectra = pl.pallas_call(
        functools.partial(front_kernel, own, chans, n_tile),
        out_shape=jax.ShapeDtypeStruct((n_tile, chans * per_block, LANES), jnp.bfloat16),
        in_specs=[smem, smem, vmem, pl.BlockSpec(memory_space=pl.ANY)],
        out_specs=vmem,
        scratch_shapes=[
            pltpu.VMEM((lines, LANES), jnp.bfloat16),
            pltpu.VMEM((ROWS * BLOCKS * own, LANES), jnp.float32),
            pltpu.VMEM((own * ROWS, TRANSFORM_LENGTH), jnp.bfloat16),
            pltpu.VMEM((FILTER_TAPS * kinds, TRANSFORM_LENGTH), jnp.bfloat16),
            pltpu.VMEM((own * ROWS, FILTER_TAPS * kinds), jnp.float32),
            pltpu.VMEM((folded_rows, LANES), jnp.float32),
            pltpu.VMEM((chans * per_block, LANES), jnp.float32),
            pltpu.SemaphoreType.DMA((CHUNKS,)),
        ],
        compiler_params=pltpu.CompilerParams(vmem_limit_bytes=56 << 20),
        name="front",
    )(channels, input_good_mask, fir_taps, x)
    spectra = spectra.reshape(n_tile * n_chan, per_block, LANES)
    turned = lax.all_to_all(spectra, ("tile", "chan"), split_axis=0, concat_axis=0, tiled=True)
    grid_side = n_tile // 8 + 2
    inputs = n_tile * n_chan * own
    side = inputs // grid_side
    return pl.pallas_call(
        functools.partial(back_kernel, own, grid_side),
        out_shape=jax.ShapeDtypeStruct((1, 1, 2, side, side), jnp.bfloat16),
        in_specs=[smem, vmem],
        out_specs=vmem,
        scratch_shapes=[
            pltpu.VMEM((n_tile * n_chan * per_block, LANES), jnp.float32),
            pltpu.VMEM((2 * HALVES, inputs, LANES), jnp.float32),
        ],
        compiler_params=pltpu.CompilerParams(vmem_limit_bytes=56 << 20),
        name="back",
    )(tile_map.T, turned)


def solution(mesh):
    in_specs = (P("tile", "chan", None), P(), P(), P("tile", "chan"), P())
    out_specs = P("chan", "tile", None, None, None)
    return jax.shard_map(
        on_device, mesh=mesh, in_specs=in_specs, out_specs=out_specs, check_vma=False
    )
```

```python
import functools
import math

import jax
import jax.numpy as jnp
from jax import lax
from jax.experimental import pallas as pl
from jax.experimental.pallas import tpu as pltpu
from jax.sharding import PartitionSpec as P

TRANSFORM_LENGTH = 2048
FILTER_TAPS = 16
SPECTRA_SUMMED = 256
FRAMES = SPECTRA_SUMMED + FILTER_TAPS - 1
ROWS = 272
LANES = 128
BLOCKS = TRANSFORM_LENGTH // LANES
HALVES = SPECTRA_SUMMED // LANES
GROUPS = 4
OCTANT = TRANSFORM_LENGTH // 8


def cos_sin(phase):
    turns = (phase + OCTANT) // (2 * OCTANT)
    angle = (phase - turns * (2 * OCTANT)).astype(jnp.float32) * (2.0 * math.pi / TRANSFORM_LENGTH)
    square = angle * angle
    cosine, sine = jnp.zeros_like(angle), jnp.zeros_like(angle)
    for power in range(10, -1, -2):
        sign = -1.0 if power % 4 else 1.0
        cosine = cosine * square + sign / math.factorial(power)
        sine = sine * square + sign / math.factorial(power + 1)
    sine = sine * angle
    odd = (turns & 1) == 1
    first, second = jnp.where(odd, sine, cosine), jnp.where(odd, cosine, sine)
    first = jnp.where(((turns + 1) & 2) == 2, -first, first)
    second = jnp.where((turns & 2) == 2, -second, second)
    return first, second


def build_table(chans, channels_ref, taps_ref, table_ref):
    row = lax.broadcasted_iota(jnp.int32, (chans, LANES), 0)
    lane = lax.broadcasted_iota(jnp.int32, (chans, LANES), 1)
    channel = jnp.zeros((chans, LANES), jnp.int32)
    for c in range(chans):
        channel = jnp.where(row == c, channels_ref[c], channel)

    def unit(phase):
        return cos_sin(phase & (TRANSFORM_LENGTH - 1))

    factor = 1.0 / math.sqrt(TRANSFORM_LENGTH)
    cos0, sin0 = unit(channel * lane)
    blocks = [(cos0 * factor, sin0 * factor)]
    for bit in range(BLOCKS.bit_length() - 1):
        cos1, sin1 = unit(channel * (LANES << bit))
        blocks += [(c * cos1 - s * sin1, s * cos1 + c * sin1) for c, s in blocks]
    for nb, (cosine, sine) in enumerate(blocks):
        columns = slice(nb * LANES, (nb + 1) * LANES)
        dft = jnp.concatenate([cosine, -sine], axis=0)
        for tap in range(FILTER_TAPS):
            table_ref[tap * 2 * chans : (tap + 1) * 2 * chans, columns] = (
                dft * taps_ref[tap : tap + 1, columns]
            ).astype(jnp.bfloat16)


def front_kernel(
    own, chans, copies, channels_hbm, mask_hbm, taps_hbm, x_hbm, out_ref,
    channels_ref, mask_ref, taps_ref, x_ref, table_ref, partial_ref, fold_ref, block_ref,
    sems, small_sems,
):
    small = [
        pltpu.make_async_copy(source, target, small_sems.at[place])
        for place, (source, target) in enumerate(
            ((channels_hbm, channels_ref), (mask_hbm, mask_ref), (taps_hbm, taps_ref))
        )
    ]
    transfers = [
        pltpu.make_async_copy(x_hbm.at[:, nb], x_ref.at[nb, pl.ds(0, FRAMES)], sems.at[nb])
        for nb in range(BLOCKS)
    ]
    for transfer in small + transfers:
        transfer.start()
    for transfer in small:
        transfer.wait()
    build_table(chans, channels_ref, taps_ref, table_ref)
    rows_ref = x_ref.reshape(BLOCKS, ROWS * own, LANES)
    share = BLOCKS // GROUPS
    for group in range(GROUPS):
        chosen = range(group * share, (group + 1) * share)
        for nb in chosen:
            transfers[nb].wait()
        product = lax.dot_general(
            jnp.concatenate([rows_ref[nb] for nb in chosen], axis=1),
            table_ref[:, group * share * LANES : (group + 1) * share * LANES],
            (((1,), (1,)), ((), ())),
            preferred_element_type=jnp.float32,
        )
        if group:
            partial_ref[...] += product
        else:
            partial_ref[...] = product
    kinds = 2 * chans
    together = LANES // kinds
    kept = -(-(SPECTRA_SUMMED + together - 1) // 8) * 8
    folded = partial_ref[:kept * own, :LANES]
    for group in range(1, FILTER_TAPS // together):
        folded = folded + partial_ref[
            pl.ds(group * together * own, kept * own), group * LANES : (group + 1) * LANES
        ]
    fold_ref[: kept * own, :] = folded
    for i in range(own):
        turned = fold_ref[pl.ds(i, fold_ref.shape[0] // own, stride=own), :].T
        spectra = turned[:kinds, :SPECTRA_SUMMED]
        for tap in range(1, together):
            shifted = pltpu.roll(
                turned[tap * kinds : (tap + 1) * kinds, :], turned.shape[1] - tap, axis=1
            )
            spectra = spectra + shifted[:, :SPECTRA_SUMMED]
        spectra = spectra * mask_ref[0, i].astype(jnp.float32)
        for half in range(HALVES):
            for q in range(2):
                block_ref[pl.ds((i * HALVES + half) * 2 + q, chans, stride=4 * own), :] = spectra[
                    q * chans : (q + 1) * chans, half * LANES : (half + 1) * LANES
                ]
    block = block_ref[...].astype(jnp.bfloat16)
    for copy in range(copies):
        out_ref[copy] = block


def back_kernel(own, grid_side, tile_map_ref, blocks_ref, out_ref, wide_ref, signal_ref):
    sources = blocks_ref.shape[0]
    inputs = sources * own
    side = inputs // grid_side
    per_block = blocks_ref.shape[1]
    tile = tile_map_ref[lax.axis_index("tile"), lax.axis_index("chan")]
    wide_ref[...] = blocks_ref[...].reshape(sources * per_block, LANES).astype(jnp.float32)
    for i in range(own):
        for half in range(HALVES):
            for q in range(2):
                signal_ref[q * HALVES + half, pl.ds(i, sources, stride=own), :] = wide_ref[
                    pl.ds((i * HALVES + half) * 2 + q, sources, stride=per_block), :
                ]
    row_start = pl.multiple_of(tile // grid_side * side, side)
    col_start = pl.multiple_of(tile % grid_side * side, side)

    def inputs_from(start):
        planes = [signal_ref[plane, pl.ds(start, side), :] for plane in range(2 * HALVES)]
        return jnp.concatenate(planes, axis=1).astype(jnp.bfloat16)

    rows, cols = inputs_from(row_start), inputs_from(col_start)
    swapped = jnp.concatenate([cols[:, SPECTRA_SUMMED:], -cols[:, :SPECTRA_SUMMED]], axis=1)
    for part, right in enumerate((cols, swapped)):
        product = lax.dot_general(
            rows, right, (((1,), (1,)), ((), ())), preferred_element_type=jnp.float32
        )
        out_ref[0, 0, part] = (product * (1.0 / SPECTRA_SUMMED)).astype(jnp.bfloat16)


def on_device(voltages, fir_taps, channels, input_good_mask, tile_map):
    own = voltages.shape[1]
    chans = channels.shape[0]
    n_chan = lax.axis_size("chan")
    n_tile = lax.axis_size("tile")
    assert chans == n_chan and 2 * chans <= LANES
    x = voltages.reshape(own, FRAMES, BLOCKS, LANES).transpose(1, 2, 0, 3)
    hbm = pl.BlockSpec(memory_space=pl.ANY)
    vmem = pl.BlockSpec(memory_space=pltpu.VMEM)
    per_block = 2 * HALVES * own
    kinds = 2 * chans
    folded_rows = SPECTRA_SUMMED + (LANES if kinds < LANES else 0)
    spectra = pl.pallas_call(
        functools.partial(front_kernel, own, chans, n_tile),
        out_shape=jax.ShapeDtypeStruct((n_tile, chans * per_block, LANES), jnp.bfloat16),
        in_specs=[hbm, hbm, hbm, hbm],
        out_specs=vmem,
        scratch_shapes=[
            pltpu.SMEM(channels.shape, jnp.int32),
            pltpu.SMEM(input_good_mask.shape, jnp.int32),
            pltpu.VMEM(fir_taps.shape, jnp.float32),
            pltpu.VMEM((BLOCKS, ROWS, own, LANES), jnp.bfloat16),
            pltpu.VMEM((FILTER_TAPS * kinds, TRANSFORM_LENGTH), jnp.bfloat16),
            pltpu.VMEM((own * ROWS, FILTER_TAPS * kinds), jnp.float32),
            pltpu.VMEM((own * folded_rows, LANES), jnp.float32),
            pltpu.VMEM((chans * per_block, LANES), jnp.float32),
            pltpu.SemaphoreType.DMA((BLOCKS,)),
            pltpu.SemaphoreType.DMA((3,)),
        ],
        compiler_params=pltpu.CompilerParams(vmem_limit_bytes=56 << 20),
        name="front",
    )(channels, input_good_mask, fir_taps, x)
    spectra = spectra.reshape(n_tile * n_chan, per_block, LANES)
    turned = lax.all_to_all(spectra, ("tile", "chan"), split_axis=0, concat_axis=0, tiled=True)
    grid_side = n_tile // 8 + 2
    inputs = n_tile * n_chan * own
    side = inputs // grid_side
    return pl.pallas_call(
        functools.partial(back_kernel, own, grid_side),
        out_shape=jax.ShapeDtypeStruct((1, 1, 2, side, side), jnp.bfloat16),
        in_specs=[pl.BlockSpec(memory_space=pltpu.SMEM), vmem],
        out_specs=vmem,
        scratch_shapes=[
            pltpu.VMEM((n_tile * n_chan * per_block, LANES), jnp.float32),
            pltpu.VMEM((2 * HALVES, inputs, LANES), jnp.float32),
        ],
        compiler_params=pltpu.CompilerParams(vmem_limit_bytes=(4 << 20) + 40 * inputs * LANES * own),
        name="back",
    )(tile_map.T, turned)


def solution(mesh):
    in_specs = (P("tile", "chan", None), P(), P(), P("tile", "chan"), P())
    out_specs = P("chan", "tile", None, None, None)
    return jax.shard_map(
        on_device, mesh=mesh, in_specs=in_specs, out_specs=out_specs, check_vma=False
    )
```

```python
import functools
import math

import jax
import jax.numpy as jnp
from jax import lax
from jax.experimental import pallas as pl
from jax.experimental.pallas import tpu as pltpu
from jax.sharding import PartitionSpec as P

TRANSFORM_LENGTH = 2048
FILTER_TAPS = 16
SPECTRA_SUMMED = 256
FRAMES = SPECTRA_SUMMED + FILTER_TAPS - 1
ROWS = 272
LANES = 128
BLOCKS = TRANSFORM_LENGTH // LANES
HALVES = SPECTRA_SUMMED // LANES
GROUPS = 4
OCTANT = TRANSFORM_LENGTH // 8


def cos_sin(phase):
    turns = (phase + OCTANT) // (2 * OCTANT)
    angle = (phase - turns * (2 * OCTANT)).astype(jnp.float32) * (2.0 * math.pi / TRANSFORM_LENGTH)
    square = angle * angle
    cosine, sine = jnp.zeros_like(angle), jnp.zeros_like(angle)
    for power in range(10, -1, -2):
        sign = -1.0 if power % 4 else 1.0
        cosine = cosine * square + sign / math.factorial(power)
        sine = sine * square + sign / math.factorial(power + 1)
    sine = sine * angle
    odd = (turns & 1) == 1
    first, second = jnp.where(odd, sine, cosine), jnp.where(odd, cosine, sine)
    first = jnp.where(((turns + 1) & 2) == 2, -first, first)
    second = jnp.where((turns & 2) == 2, -second, second)
    return first, second


def build_table(chans, first, channels_ref, taps_ref, table_ref):
    row = lax.broadcasted_iota(jnp.int32, (chans, LANES), 0)
    lane = lax.broadcasted_iota(jnp.int32, (chans, LANES), 1)
    channel = jnp.zeros((chans, LANES), jnp.int32)
    for c in range(chans):
        channel = jnp.where(row == c, channels_ref[(c + first) % chans], channel)

    def unit(phase):
        return cos_sin(phase & (TRANSFORM_LENGTH - 1))

    factor = 1.0 / math.sqrt(TRANSFORM_LENGTH)
    cos0, sin0 = unit(channel * lane)
    blocks = [(cos0 * factor, sin0 * factor)]
    for bit in range(BLOCKS.bit_length() - 1):
        cos1, sin1 = unit(channel * (LANES << bit))
        blocks += [(c * cos1 - s * sin1, s * cos1 + c * sin1) for c, s in blocks]
    for nb, (cosine, sine) in enumerate(blocks):
        columns = slice(nb * LANES, (nb + 1) * LANES)
        dft = jnp.concatenate([cosine, -sine], axis=0)
        for tap in range(FILTER_TAPS):
            table_ref[tap * 2 * chans : (tap + 1) * 2 * chans, columns] = (
                dft * taps_ref[tap : tap + 1, columns]
            ).astype(jnp.bfloat16)


def front_kernel(
    own, chans, first, copies, channels_hbm, mask_hbm, taps_hbm, x_hbm, out_ref,
    channels_ref, mask_ref, taps_ref, x_ref, table_ref, partial_ref, fold_ref, block_ref,
    sems, small_sems,
):
    small = [
        pltpu.make_async_copy(source, target, small_sems.at[place])
        for place, (source, target) in enumerate(
            ((channels_hbm, channels_ref), (mask_hbm, mask_ref), (taps_hbm, taps_ref))
        )
    ]
    transfers = [
        pltpu.make_async_copy(x_hbm.at[:, nb], x_ref.at[nb, pl.ds(0, FRAMES)], sems.at[nb])
        for nb in range(BLOCKS)
    ]
    for transfer in small + transfers:
        transfer.start()
    for transfer in small:
        transfer.wait()
    build_table(chans, first, channels_ref, taps_ref, table_ref)
    rows_ref = x_ref.reshape(BLOCKS, ROWS * own, LANES)
    share = BLOCKS // GROUPS
    for group in range(GROUPS):
        chosen = range(group * share, (group + 1) * share)
        for nb in chosen:
            transfers[nb].wait()
        product = lax.dot_general(
            jnp.concatenate([rows_ref[nb] for nb in chosen], axis=1),
            table_ref[:, group * share * LANES : (group + 1) * share * LANES],
            (((1,), (1,)), ((), ())),
            preferred_element_type=jnp.float32,
        )
        if group:
            partial_ref[...] += product
        else:
            partial_ref[...] = product
    kinds = 2 * chans
    together = LANES // kinds
    kept = -(-(SPECTRA_SUMMED + together - 1) // 8) * 8
    folded = partial_ref[:kept * own, :LANES]
    for group in range(1, FILTER_TAPS // together):
        folded = folded + partial_ref[
            pl.ds(group * together * own, kept * own), group * LANES : (group + 1) * LANES
        ]
    fold_ref[: kept * own, :] = folded
    for i in range(own):
        turned = fold_ref[pl.ds(i, fold_ref.shape[0] // own, stride=own), :].T
        spectra = turned[:kinds, :SPECTRA_SUMMED]
        for tap in range(1, together):
            shifted = pltpu.roll(
                turned[tap * kinds : (tap + 1) * kinds, :], turned.shape[1] - tap, axis=1
            )
            spectra = spectra + shifted[:, :SPECTRA_SUMMED]
        spectra = spectra * mask_ref[0, i].astype(jnp.float32)
        for half in range(HALVES):
            for q in range(2):
                block_ref[pl.ds((i * HALVES + half) * 2 + q, chans, stride=4 * own), :] = spectra[
                    q * chans : (q + 1) * chans, half * LANES : (half + 1) * LANES
                ]
    block = block_ref[...].astype(jnp.bfloat16)
    for copy in range(copies):
        out_ref[copy] = block


def back_kernel(own, grid_side, runs, tile_map_ref, blocks_ref, out_ref, wide_ref, signal_ref):
    sources = blocks_ref.shape[0]
    inputs = sources * own
    side = inputs // grid_side
    per_block = blocks_ref.shape[1]
    tile = tile_map_ref[lax.axis_index("tile"), lax.axis_index("chan")]
    wide_ref[...] = blocks_ref[...].reshape(sources * per_block, LANES).astype(jnp.float32)
    for i in range(own):
        for half in range(HALVES):
            for q in range(2):
                for block, source, count in runs:
                    line = block * per_block + (i * HALVES + half) * 2 + q
                    signal_ref[
                        q * HALVES + half, pl.ds(source * own + i, count, stride=own), :
                    ] = wide_ref[pl.ds(line, count, stride=per_block), :]
    row_start = pl.multiple_of(tile // grid_side * side, side)
    col_start = pl.multiple_of(tile % grid_side * side, side)

    def inputs_from(start):
        planes = [signal_ref[plane, pl.ds(start, side), :] for plane in range(2 * HALVES)]
        return jnp.concatenate(planes, axis=1).astype(jnp.bfloat16)

    rows, cols = inputs_from(row_start), inputs_from(col_start)
    swapped = jnp.concatenate([cols[:, SPECTRA_SUMMED:], -cols[:, :SPECTRA_SUMMED]], axis=1)
    for part, right in enumerate((cols, swapped)):
        product = lax.dot_general(
            rows, right, (((1,), (1,)), ((), ())), preferred_element_type=jnp.float32
        )
        out_ref[0, 0, part] = (product * (1.0 / SPECTRA_SUMMED)).astype(jnp.bfloat16)


def on_device(voltages, fir_taps, channels, input_good_mask, tile_map):
    own = voltages.shape[1]
    chans = channels.shape[0]
    n_chan = lax.axis_size("chan")
    n_tile = lax.axis_size("tile")
    assert chans == n_chan and 2 * chans <= LANES
    first_tile, first_chan = n_tile - 1, max(n_chan - 2, 0)
    order = [
        (first_tile + t) % n_tile * n_chan + (first_chan + c) % n_chan
        for t in range(n_tile)
        for c in range(n_chan)
    ]
    runs = []
    for block, source in enumerate(order):
        if runs and source == runs[-1][1] + runs[-1][2]:
            runs[-1] = (runs[-1][0], runs[-1][1], runs[-1][2] + 1)
        else:
            runs.append((block, source, 1))
    x = voltages.reshape(own, FRAMES, BLOCKS, LANES).transpose(1, 2, 0, 3)
    hbm = pl.BlockSpec(memory_space=pl.ANY)
    vmem = pl.BlockSpec(memory_space=pltpu.VMEM)
    per_block = 2 * HALVES * own
    kinds = 2 * chans
    folded_rows = SPECTRA_SUMMED + (LANES if kinds < LANES else 0)
    spectra = pl.pallas_call(
        functools.partial(front_kernel, own, chans, first_chan, n_tile),
        out_shape=jax.ShapeDtypeStruct((n_tile, chans * per_block, LANES), jnp.bfloat16),
        in_specs=[hbm, hbm, hbm, hbm],
        out_specs=vmem,
        scratch_shapes=[
            pltpu.SMEM(channels.shape, jnp.int32),
            pltpu.SMEM(input_good_mask.shape, jnp.int32),
            pltpu.VMEM(fir_taps.shape, jnp.float32),
            pltpu.VMEM((BLOCKS, ROWS, own, LANES), jnp.bfloat16),
            pltpu.VMEM((FILTER_TAPS * kinds, TRANSFORM_LENGTH), jnp.bfloat16),
            pltpu.VMEM((own * ROWS, FILTER_TAPS * kinds), jnp.float32),
            pltpu.VMEM((own * folded_rows, LANES), jnp.float32),
            pltpu.VMEM((chans * per_block, LANES), jnp.float32),
            pltpu.SemaphoreType.DMA((BLOCKS,)),
            pltpu.SemaphoreType.DMA((3,)),
        ],
        compiler_params=pltpu.CompilerParams(vmem_limit_bytes=56 << 20),
        name="front",
    )(channels, input_good_mask, fir_taps, x)
    spectra = spectra.reshape(n_tile * n_chan, per_block, LANES)
    turned = lax.all_to_all(
        spectra, ("tile", "chan"), split_axis=0, concat_axis=0, axis_index_groups=[order], tiled=True
    )
    grid_side = n_tile // 8 + 2
    inputs = n_tile * n_chan * own
    side = inputs // grid_side
    return pl.pallas_call(
        functools.partial(back_kernel, own, grid_side, runs),
        out_shape=jax.ShapeDtypeStruct((1, 1, 2, side, side), jnp.bfloat16),
        in_specs=[pl.BlockSpec(memory_space=pltpu.SMEM), vmem],
        out_specs=vmem,
        scratch_shapes=[
            pltpu.VMEM((n_tile * n_chan * per_block, LANES), jnp.float32),
            pltpu.VMEM((2 * HALVES, inputs, LANES), jnp.float32),
        ],
        compiler_params=pltpu.CompilerParams(vmem_limit_bytes=(4 << 20) + 40 * inputs * LANES * own),
        name="back",
    )(tile_map.T, turned)


def solution(mesh):
    in_specs = (P("tile", "chan", None), P(), P(), P("tile", "chan"), P())
    out_specs = P("chan", "tile", None, None, None)
    return jax.shard_map(
        on_device, mesh=mesh, in_specs=in_specs, out_specs=out_specs, check_vma=False
    )
```

```python
import functools
import math

import jax
import jax.numpy as jnp
from jax import lax
from jax.experimental import pallas as pl
from jax.experimental.pallas import tpu as pltpu
from jax.sharding import PartitionSpec as P

TRANSFORM_LENGTH = 2048
FILTER_TAPS = 16
SPECTRA_SUMMED = 256
FRAMES = SPECTRA_SUMMED + FILTER_TAPS - 1
ROWS = 272
LANES = 128
BLOCKS = TRANSFORM_LENGTH // LANES
HALVES = SPECTRA_SUMMED // LANES
GROUPS = 4
OCTANT = TRANSFORM_LENGTH // 8


def cos_sin(phase):
    turns = (phase + OCTANT) // (2 * OCTANT)
    angle = (phase - turns * (2 * OCTANT)).astype(jnp.float32) * (2.0 * math.pi / TRANSFORM_LENGTH)
    square = angle * angle
    cosine, sine = jnp.zeros_like(angle), jnp.zeros_like(angle)
    for power in range(10, -1, -2):
        sign = -1.0 if power % 4 else 1.0
        cosine = cosine * square + sign / math.factorial(power)
        sine = sine * square + sign / math.factorial(power + 1)
    sine = sine * angle
    odd = (turns & 1) == 1
    first, second = jnp.where(odd, sine, cosine), jnp.where(odd, cosine, sine)
    first = jnp.where(((turns + 1) & 2) == 2, -first, first)
    second = jnp.where((turns & 2) == 2, -second, second)
    return first, second


def build_table(chans, first, channels_ref, taps_ref, table_ref):
    row = lax.broadcasted_iota(jnp.int32, (chans, LANES), 0)
    lane = lax.broadcasted_iota(jnp.int32, (chans, LANES), 1)
    channel = jnp.zeros((chans, LANES), jnp.int32)
    for c in range(chans):
        channel = jnp.where(row == c, channels_ref[(c + first) % chans], channel)

    def unit(phase):
        return cos_sin(phase & (TRANSFORM_LENGTH - 1))

    factor = 1.0 / math.sqrt(TRANSFORM_LENGTH)
    cos0, sin0 = unit(channel * lane)
    blocks = [(cos0 * factor, sin0 * factor)]
    for bit in range(BLOCKS.bit_length() - 1):
        cos1, sin1 = unit(channel * (LANES << bit))
        blocks += [(c * cos1 - s * sin1, s * cos1 + c * sin1) for c, s in blocks]
    for nb, (cosine, sine) in enumerate(blocks):
        columns = slice(nb * LANES, (nb + 1) * LANES)
        dft = jnp.concatenate([cosine, -sine], axis=0)
        for tap in range(FILTER_TAPS):
            table_ref[tap * 2 * chans : (tap + 1) * 2 * chans, columns] = (
                dft * taps_ref[tap : tap + 1, columns]
            ).astype(jnp.bfloat16)


def front_kernel(
    own, chans, first, copies, channels_hbm, mask_hbm, taps_hbm, x_hbm, out_ref,
    channels_ref, mask_ref, taps_ref, x_ref, table_ref, partial_ref, fold_ref, block_ref,
    sems, small_sems,
):
    small = [
        pltpu.make_async_copy(source, target, small_sems.at[place])
        for place, (source, target) in enumerate(
            ((channels_hbm, channels_ref), (mask_hbm, mask_ref), (taps_hbm, taps_ref))
        )
    ]
    transfers = [
        pltpu.make_async_copy(x_hbm.at[:, nb], x_ref.at[nb, pl.ds(0, FRAMES)], sems.at[nb])
        for nb in range(BLOCKS)
    ]
    for transfer in small + transfers:
        transfer.start()
    for transfer in small:
        transfer.wait()
    build_table(chans, first, channels_ref, taps_ref, table_ref)
    rows_ref = x_ref.reshape(BLOCKS, ROWS * own, LANES)
    share = BLOCKS // GROUPS
    for group in range(GROUPS):
        chosen = range(group * share, (group + 1) * share)
        for nb in chosen:
            transfers[nb].wait()
        product = lax.dot_general(
            jnp.concatenate([rows_ref[nb] for nb in chosen], axis=1),
            table_ref[:, group * share * LANES : (group + 1) * share * LANES],
            (((1,), (1,)), ((), ())),
            preferred_element_type=jnp.float32,
        )
        if group:
            partial_ref[...] += product
        else:
            partial_ref[...] = product
    kinds = 2 * chans
    together = LANES // kinds
    kept = -(-(SPECTRA_SUMMED + together - 1) // 8) * 8
    folded = partial_ref[:kept * own, :LANES]
    for group in range(1, FILTER_TAPS // together):
        folded = folded + partial_ref[
            pl.ds(group * together * own, kept * own), group * LANES : (group + 1) * LANES
        ]
    fold_ref[: kept * own, :] = folded
    for i in range(own):
        turned = fold_ref[pl.ds(i, fold_ref.shape[0] // own, stride=own), :].T
        spectra = turned[:kinds, :SPECTRA_SUMMED]
        for tap in range(1, together):
            shifted = pltpu.roll(
                turned[tap * kinds : (tap + 1) * kinds, :], turned.shape[1] - tap, axis=1
            )
            spectra = spectra + shifted[:, :SPECTRA_SUMMED]
        spectra = spectra * mask_ref[0, i].astype(jnp.float32)
        for half in range(HALVES):
            for q in range(2):
                block_ref[pl.ds((i * HALVES + half) * 2 + q, chans, stride=4 * own), :] = spectra[
                    q * chans : (q + 1) * chans, half * LANES : (half + 1) * LANES
                ]
    block = block_ref[...].astype(jnp.bfloat16)
    for copy in range(copies):
        out_ref[copy] = block


def back_kernel(
    own, grid_side, runs, tile_map_ref, mine_ref, other_ref, out_ref, mine_wide, other_wide, signal_ref
):
    sources = mine_ref.shape[0]
    inputs = sources * 2 * own
    side = inputs // grid_side
    lines = mine_ref.shape[1]
    chan = lax.axis_index("chan")
    tile = tile_map_ref[lax.axis_index("tile"), chan]
    first_core = chan % 2 == 0
    mine_wide[...] = mine_ref[...].reshape(sources * lines, LANES).astype(jnp.float32)
    other_wide[...] = other_ref[...].reshape(sources * lines, LANES).astype(jnp.float32)
    for i in range(own):
        for half in range(HALVES):
            for q in range(2):
                line = (i * HALVES + half) * 2 + q
                for block, source, count in runs:
                    low = pl.ds(block * lines + line, count, stride=lines)
                    high = pl.ds(block * lines + lines // 2 + line, count, stride=lines)
                    from_core = (
                        jnp.where(first_core, mine_wide[low, :], other_wide[high, :]),
                        jnp.where(first_core, other_wide[low, :], mine_wide[high, :]),
                    )
                    for core in range(2):
                        target = pl.ds((source * 2 + core) * own + i, count, stride=2 * own)
                        signal_ref[q * HALVES + half, target, :] = from_core[core]
    row_start = pl.multiple_of(tile // grid_side * side, side)
    col_start = pl.multiple_of(tile % grid_side * side, side)

    def inputs_from(start):
        planes = [signal_ref[plane, pl.ds(start, side), :] for plane in range(2 * HALVES)]
        return jnp.concatenate(planes, axis=1).astype(jnp.bfloat16)

    rows, cols = inputs_from(row_start), inputs_from(col_start)
    swapped = jnp.concatenate([cols[:, SPECTRA_SUMMED:], -cols[:, :SPECTRA_SUMMED]], axis=1)
    for part, right in enumerate((cols, swapped)):
        product = lax.dot_general(
            rows, right, (((1,), (1,)), ((), ())), preferred_element_type=jnp.float32
        )
        out_ref[0, 0, part] = (product * (1.0 / SPECTRA_SUMMED)).astype(jnp.bfloat16)


def on_device(voltages, fir_taps, channels, input_good_mask, tile_map):
    own = voltages.shape[1]
    chans = channels.shape[0]
    n_chan = lax.axis_size("chan")
    n_tile = lax.axis_size("tile")
    assert chans == n_chan and 2 * chans <= LANES
    chips = n_chan // 2
    first_tile, first_chan = n_tile - 1, n_chan - 2
    order = [
        (first_tile + t) % n_tile * chips + (chips - 1 + chip) % chips
        for t in range(n_tile)
        for chip in range(chips)
    ]
    groups = [[2 * place + core for place in order] for core in range(2)]
    runs = []
    for block, source in enumerate(order):
        if runs and source == runs[-1][1] + runs[-1][2]:
            runs[-1] = (runs[-1][0], runs[-1][1], runs[-1][2] + 1)
        else:
            runs.append((block, source, 1))
    x = voltages.reshape(own, FRAMES, BLOCKS, LANES).transpose(1, 2, 0, 3)
    hbm = pl.BlockSpec(memory_space=pl.ANY)
    vmem = pl.BlockSpec(memory_space=pltpu.VMEM)
    per_block = 2 * HALVES * own
    kinds = 2 * chans
    folded_rows = SPECTRA_SUMMED + (LANES if kinds < LANES else 0)
    spectra = pl.pallas_call(
        functools.partial(front_kernel, own, chans, first_chan, n_tile),
        out_shape=jax.ShapeDtypeStruct((n_tile, chans * per_block, LANES), jnp.bfloat16),
        in_specs=[hbm, hbm, hbm, hbm],
        out_specs=vmem,
        scratch_shapes=[
            pltpu.SMEM(channels.shape, jnp.int32),
            pltpu.SMEM(input_good_mask.shape, jnp.int32),
            pltpu.VMEM(fir_taps.shape, jnp.float32),
            pltpu.VMEM((BLOCKS, ROWS, own, LANES), jnp.bfloat16),
            pltpu.VMEM((FILTER_TAPS * kinds, TRANSFORM_LENGTH), jnp.bfloat16),
            pltpu.VMEM((own * ROWS, FILTER_TAPS * kinds), jnp.float32),
            pltpu.VMEM((own * folded_rows, LANES), jnp.float32),
            pltpu.VMEM((chans * per_block, LANES), jnp.float32),
            pltpu.SemaphoreType.DMA((BLOCKS,)),
            pltpu.SemaphoreType.DMA((3,)),
        ],
        compiler_params=pltpu.CompilerParams(vmem_limit_bytes=56 << 20),
        name="front",
    )(channels, input_good_mask, fir_taps, x)
    spectra = spectra.reshape(n_tile * chips, 2 * per_block, LANES)
    mine = lax.all_to_all(
        spectra, ("tile", "chan"), split_axis=0, concat_axis=0, axis_index_groups=groups, tiled=True
    )
    other = lax.ppermute(mine, "chan", [(c, c ^ 1) for c in range(n_chan)])
    grid_side = n_tile // 8 + 2
    inputs = n_tile * n_chan * own
    side = inputs // grid_side
    return pl.pallas_call(
        functools.partial(back_kernel, own, grid_side, runs),
        out_shape=jax.ShapeDtypeStruct((1, 1, 2, side, side), jnp.bfloat16),
        in_specs=[pl.BlockSpec(memory_space=pltpu.SMEM), vmem, vmem],
        out_specs=vmem,
        scratch_shapes=[
            pltpu.VMEM((n_tile * n_chan * per_block, LANES), jnp.float32),
            pltpu.VMEM((n_tile * n_chan * per_block, LANES), jnp.float32),
            pltpu.VMEM((2 * HALVES, inputs, LANES), jnp.float32),
        ],
        compiler_params=pltpu.CompilerParams(vmem_limit_bytes=(4 << 20) + 60 * inputs * LANES * own),
        name="back",
    )(tile_map.T, mine, other)


def solution(mesh):
    in_specs = (P("tile", "chan", None), P(), P(), P("tile", "chan"), P())
    out_specs = P("chan", "tile", None, None, None)
    return jax.shard_map(
        on_device, mesh=mesh, in_specs=in_specs, out_specs=out_specs, check_vma=False
    )
```

```python
import functools
import math

import jax
import jax.numpy as jnp
from jax import lax
from jax.experimental import pallas as pl
from jax.experimental.pallas import tpu as pltpu
from jax.sharding import PartitionSpec as P

TRANSFORM_LENGTH = 2048
FILTER_TAPS = 16
SPECTRA_SUMMED = 256
FRAMES = SPECTRA_SUMMED + FILTER_TAPS - 1
ROWS = 272
LANES = 128
BLOCKS = TRANSFORM_LENGTH // LANES
HALVES = SPECTRA_SUMMED // LANES
GROUPS = 4
OCTANT = TRANSFORM_LENGTH // 8


def cos_sin(phase):
    turns = (phase + OCTANT) // (2 * OCTANT)
    angle = (phase - turns * (2 * OCTANT)).astype(jnp.float32) * (2.0 * math.pi / TRANSFORM_LENGTH)
    square = angle * angle
    cosine, sine = jnp.zeros_like(angle), jnp.zeros_like(angle)
    for power in range(10, -1, -2):
        sign = -1.0 if power % 4 else 1.0
        cosine = cosine * square + sign / math.factorial(power)
        sine = sine * square + sign / math.factorial(power + 1)
    sine = sine * angle
    odd = (turns & 1) == 1
    first, second = jnp.where(odd, sine, cosine), jnp.where(odd, cosine, sine)
    first = jnp.where(((turns + 1) & 2) == 2, -first, first)
    second = jnp.where((turns & 2) == 2, -second, second)
    return first, second


def build_table(chans, channels_ref, taps_ref, table_ref):
    row = lax.broadcasted_iota(jnp.int32, (chans, LANES), 0)
    lane = lax.broadcasted_iota(jnp.int32, (chans, LANES), 1)
    channel = jnp.zeros((chans, LANES), jnp.int32)
    for c in range(chans):
        channel = jnp.where(row == c, channels_ref[chans - 2 - c + c % 2 * 2], channel)

    def unit(phase):
        return cos_sin(phase & (TRANSFORM_LENGTH - 1))

    factor = 1.0 / math.sqrt(TRANSFORM_LENGTH)
    cos0, sin0 = unit(channel * lane)
    blocks = [(cos0 * factor, sin0 * factor)]
    for bit in range(BLOCKS.bit_length() - 1):
        cos1, sin1 = unit(channel * (LANES << bit))
        blocks += [(c * cos1 - s * sin1, s * cos1 + c * sin1) for c, s in blocks]
    for nb, (cosine, sine) in enumerate(blocks):
        columns = slice(nb * LANES, (nb + 1) * LANES)
        dft = jnp.concatenate([cosine, -sine], axis=0)
        for tap in range(FILTER_TAPS):
            table_ref[tap * 2 * chans : (tap + 1) * 2 * chans, columns] = (
                dft * taps_ref[tap : tap + 1, columns]
            ).astype(jnp.bfloat16)


def front_kernel(
    own, chans, copies, channels_hbm, mask_hbm, taps_hbm, x_hbm, out_ref,
    channels_ref, mask_ref, taps_ref, x_ref, table_ref, partial_ref, fold_ref, block_ref,
    sems, small_sems,
):
    small = [
        pltpu.make_async_copy(source, target, small_sems.at[place])
        for place, (source, target) in enumerate(
            ((channels_hbm, channels_ref), (mask_hbm, mask_ref), (taps_hbm, taps_ref))
        )
    ]
    transfers = [
        pltpu.make_async_copy(x_hbm.at[:, nb], x_ref.at[nb, pl.ds(0, FRAMES)], sems.at[nb])
        for nb in range(BLOCKS)
    ]
    for transfer in small + transfers:
        transfer.start()
    for transfer in small:
        transfer.wait()
    build_table(chans, channels_ref, taps_ref, table_ref)
    rows_ref = x_ref.reshape(BLOCKS, ROWS * own, LANES)
    share = BLOCKS // GROUPS
    for group in range(GROUPS):
        chosen = range(group * share, (group + 1) * share)
        for nb in chosen:
            transfers[nb].wait()
        product = lax.dot_general(
            jnp.concatenate([rows_ref[nb] for nb in chosen], axis=1),
            table_ref[:, group * share * LANES : (group + 1) * share * LANES],
            (((1,), (1,)), ((), ())),
            preferred_element_type=jnp.float32,
        )
        if group:
            partial_ref[...] += product
        else:
            partial_ref[...] = product
    kinds = 2 * chans
    together = LANES // kinds
    kept = -(-(SPECTRA_SUMMED + together - 1) // 8) * 8
    folded = partial_ref[:kept * own, :LANES]
    for group in range(1, FILTER_TAPS // together):
        folded = folded + partial_ref[
            pl.ds(group * together * own, kept * own), group * LANES : (group + 1) * LANES
        ]
    fold_ref[: kept * own, :] = folded
    for i in range(own):
        turned = fold_ref[pl.ds(i, fold_ref.shape[0] // own, stride=own), :].T
        spectra = turned[:kinds, :SPECTRA_SUMMED]
        for tap in range(1, together):
            shifted = pltpu.roll(
                turned[tap * kinds : (tap + 1) * kinds, :], turned.shape[1] - tap, axis=1
            )
            spectra = spectra + shifted[:, :SPECTRA_SUMMED]
        spectra = spectra * mask_ref[0, i].astype(jnp.float32)
        for half in range(HALVES):
            for q in range(2):
                block_ref[pl.ds((i * HALVES + half) * 2 + q, chans, stride=4 * own), :] = spectra[
                    q * chans : (q + 1) * chans, half * LANES : (half + 1) * LANES
                ]
    block = block_ref[...].astype(jnp.bfloat16)
    for copy in range(copies):
        out_ref[copy] = block


def back_kernel(
    own, grid_side, tile_map_ref, mine_ref, other_ref, out_ref, mine_wide, other_wide, signal_ref
):
    sources = mine_ref.shape[0]
    inputs = sources * 2 * own
    side = inputs // grid_side
    lines = mine_ref.shape[1]
    chan = lax.axis_index("chan")
    tile = tile_map_ref[lax.axis_index("tile"), chan]
    first_core = chan % 2 == 0
    mine_wide[...] = mine_ref[...].reshape(sources * lines, LANES).astype(jnp.float32)
    other_wide[...] = other_ref[...].reshape(sources * lines, LANES).astype(jnp.float32)
    for i in range(own):
        for half in range(HALVES):
            for q in range(2):
                line = (i * HALVES + half) * 2 + q
                low = pl.ds(line, sources, stride=lines)
                high = pl.ds(lines // 2 + line, sources, stride=lines)
                from_core = (
                    jnp.where(first_core, mine_wide[low, :], other_wide[high, :]),
                    jnp.where(first_core, other_wide[low, :], mine_wide[high, :]),
                )
                for core in range(2):
                    target = pl.ds(core * own + i, sources, stride=2 * own)
                    signal_ref[q * HALVES + half, target, :] = from_core[core]
    row_start = pl.multiple_of((grid_side - 1 - tile // grid_side) * side, side)
    col_start = pl.multiple_of((grid_side - 1 - tile % grid_side) * side, side)
    to = lax.broadcasted_iota(jnp.int32, (side, side), 0)
    fro = lax.broadcasted_iota(jnp.int32, (side, side), 1)
    chip = 2 * own
    reverse = jnp.where(fro == side - chip - to // chip * chip + to % chip, 1.0, 0.0).astype(
        jnp.bfloat16
    )

    def inputs_from(start):
        planes = [signal_ref[plane, pl.ds(start, side), :] for plane in range(2 * HALVES)]
        signals = jnp.concatenate(planes, axis=1).astype(jnp.bfloat16)
        return jnp.dot(reverse, signals, preferred_element_type=jnp.float32).astype(jnp.bfloat16)

    rows, cols = inputs_from(row_start), inputs_from(col_start)
    swapped = jnp.concatenate([cols[:, SPECTRA_SUMMED:], -cols[:, :SPECTRA_SUMMED]], axis=1)
    for part, right in enumerate((cols, swapped)):
        product = lax.dot_general(
            rows, right, (((1,), (1,)), ((), ())), preferred_element_type=jnp.float32
        )
        out_ref[0, 0, part] = (product * (1.0 / SPECTRA_SUMMED)).astype(jnp.bfloat16)


def on_device(voltages, fir_taps, channels, input_good_mask, tile_map):
    own = voltages.shape[1]
    chans = channels.shape[0]
    n_chan = lax.axis_size("chan")
    n_tile = lax.axis_size("tile")
    assert chans == n_chan and 2 * chans <= LANES
    chips = n_chan // 2
    groups = [[2 * place + core for place in reversed(range(n_tile * chips))] for core in range(2)]
    x = voltages.reshape(own, FRAMES, BLOCKS, LANES).transpose(1, 2, 0, 3)
    hbm = pl.BlockSpec(memory_space=pltpu.HBM)
    vmem = pl.BlockSpec(memory_space=pltpu.VMEM)
    per_block = 2 * HALVES * own
    kinds = 2 * chans
    folded_rows = SPECTRA_SUMMED + (LANES if kinds < LANES else 0)
    spectra = pl.pallas_call(
        functools.partial(front_kernel, own, chans, n_tile),
        out_shape=jax.ShapeDtypeStruct((n_tile, chans * per_block, LANES), jnp.bfloat16),
        in_specs=[hbm, hbm, hbm, hbm],
        out_specs=vmem,
        scratch_shapes=[
            pltpu.SMEM(channels.shape, jnp.int32),
            pltpu.SMEM(input_good_mask.shape, jnp.int32),
            pltpu.VMEM(fir_taps.shape, jnp.float32),
            pltpu.VMEM((BLOCKS, ROWS, own, LANES), jnp.bfloat16),
            pltpu.VMEM((FILTER_TAPS * kinds, TRANSFORM_LENGTH), jnp.bfloat16),
            pltpu.VMEM((own * ROWS, FILTER_TAPS * kinds), jnp.float32),
            pltpu.VMEM((own * folded_rows, LANES), jnp.float32),
            pltpu.VMEM((chans * per_block, LANES), jnp.float32),
            pltpu.SemaphoreType.DMA((BLOCKS,)),
            pltpu.SemaphoreType.DMA((3,)),
        ],
        compiler_params=pltpu.CompilerParams(vmem_limit_bytes=55104 << 10),
        name="front",
    )(channels, input_good_mask, fir_taps, x)
    spectra = spectra.reshape(n_tile * chips, 2 * per_block, LANES)
    mine = lax.all_to_all(
        spectra, ("tile", "chan"), split_axis=0, concat_axis=0, axis_index_groups=groups, tiled=True
    )
    other = lax.ppermute(mine, "chan", [(c, c ^ 1) for c in range(n_chan)])
    grid_side = n_tile // 8 + 2
    inputs = n_tile * n_chan * own
    side = inputs // grid_side
    return pl.pallas_call(
        functools.partial(back_kernel, own, grid_side),
        out_shape=jax.ShapeDtypeStruct((1, 1, 2, side, side), jnp.bfloat16),
        in_specs=[pl.BlockSpec(memory_space=pltpu.SMEM), vmem, vmem],
        out_specs=vmem,
        scratch_shapes=[
            pltpu.VMEM((n_tile * n_chan * per_block, LANES), jnp.float32),
            pltpu.VMEM((n_tile * n_chan * per_block, LANES), jnp.float32),
            pltpu.VMEM((2 * HALVES, inputs, LANES), jnp.float32),
        ],
        compiler_params=pltpu.CompilerParams(vmem_limit_bytes=(4 << 20) + 60 * inputs * LANES * own),
        name="back",
    )(tile_map.T, mine, other)


def solution(mesh):
    in_specs = (P("tile", "chan", None), P(), P(), P("tile", "chan"), P())
    out_specs = P("chan", "tile", None, None, None)
    return jax.shard_map(
        on_device, mesh=mesh, in_specs=in_specs, out_specs=out_specs, check_vma=False
    )
```

```python
import functools
import math

import jax
import jax.numpy as jnp
from jax import lax
from jax.experimental import pallas as pl
from jax.experimental.pallas import tpu as pltpu
from jax.sharding import PartitionSpec as P

TRANSFORM_LENGTH = 2048
FILTER_TAPS = 16
SPECTRA_SUMMED = 256
FRAMES = SPECTRA_SUMMED + FILTER_TAPS - 1
ROWS = 272
LANES = 128
BLOCKS = TRANSFORM_LENGTH // LANES
HALVES = SPECTRA_SUMMED // LANES
GROUPS = 4
OCTANT = TRANSFORM_LENGTH // 8


def cos_sin(phase):
    turns = (phase + OCTANT) // (2 * OCTANT)
    angle = (phase - turns * (2 * OCTANT)).astype(jnp.float32) * (2.0 * math.pi / TRANSFORM_LENGTH)
    square = angle * angle
    cosine, sine = jnp.zeros_like(angle), jnp.zeros_like(angle)
    for power in range(10, -1, -2):
        sign = -1.0 if power % 4 else 1.0
        cosine = cosine * square + sign / math.factorial(power)
        sine = sine * square + sign / math.factorial(power + 1)
    sine = sine * angle
    odd = (turns & 1) == 1
    first, second = jnp.where(odd, sine, cosine), jnp.where(odd, cosine, sine)
    first = jnp.where(((turns + 1) & 2) == 2, -first, first)
    second = jnp.where((turns & 2) == 2, -second, second)
    return first, second


def build_table(chans, channels_ref, taps_ref, table_ref):
    row = lax.broadcasted_iota(jnp.int32, (chans, LANES), 0)
    lane = lax.broadcasted_iota(jnp.int32, (chans, LANES), 1)
    channel = jnp.zeros((chans, LANES), jnp.int32)
    for c in range(chans):
        channel = jnp.where(row == c, channels_ref[chans - 2 - c + c % 2 * 2], channel)

    def unit(phase):
        return cos_sin(phase & (TRANSFORM_LENGTH - 1))

    factor = 1.0 / math.sqrt(TRANSFORM_LENGTH)
    cos0, sin0 = unit(channel * lane)
    blocks = [(cos0 * factor, sin0 * factor)]
    for bit in range(BLOCKS.bit_length() - 1):
        cos1, sin1 = unit(channel * (LANES << bit))
        blocks += [(c * cos1 - s * sin1, s * cos1 + c * sin1) for c, s in blocks]
    for nb, (cosine, sine) in enumerate(blocks):
        columns = slice(nb * LANES, (nb + 1) * LANES)
        dft = jnp.concatenate([cosine, -sine], axis=0)
        for tap in range(FILTER_TAPS):
            table_ref[tap * 2 * chans : (tap + 1) * 2 * chans, columns] = (
                dft * taps_ref[tap : tap + 1, columns]
            ).astype(jnp.bfloat16)


def front_kernel(
    own, chans, copies, channels_hbm, mask_hbm, taps_hbm, x_hbm, out_ref,
    channels_ref, mask_ref, taps_ref, x_ref, table_ref, partial_ref, fold_ref, block_ref,
    sems, small_sems,
):
    small = [
        pltpu.make_async_copy(source, target, small_sems.at[place])
        for place, (source, target) in enumerate(
            ((channels_hbm, channels_ref), (mask_hbm, mask_ref), (taps_hbm, taps_ref))
        )
    ]
    transfers = [
        pltpu.make_async_copy(x_hbm.at[:, nb], x_ref.at[nb, pl.ds(0, FRAMES)], sems.at[nb])
        for nb in range(BLOCKS)
    ]
    for transfer in small:
        transfer.start()
    for place, transfer in enumerate(transfers):
        transfer.start(priority=place % 2)
    for transfer in small:
        transfer.wait()
    build_table(chans, channels_ref, taps_ref, table_ref)
    rows_ref = x_ref.reshape(BLOCKS, ROWS * own, LANES)
    share = BLOCKS // GROUPS
    for group in range(GROUPS):
        chosen = range(group * share, (group + 1) * share)
        for nb in chosen:
            transfers[nb].wait()
        product = lax.dot_general(
            jnp.concatenate([rows_ref[nb] for nb in chosen], axis=1),
            table_ref[:, group * share * LANES : (group + 1) * share * LANES],
            (((1,), (1,)), ((), ())),
            preferred_element_type=jnp.float32,
        )
        if group:
            partial_ref[...] += product
        else:
            partial_ref[...] = product
    kinds = 2 * chans
    together = LANES // kinds
    kept = -(-(SPECTRA_SUMMED + together - 1) // 8) * 8
    folded = partial_ref[:kept * own, :LANES]
    for group in range(1, FILTER_TAPS // together):
        folded = folded + partial_ref[
            pl.ds(group * together * own, kept * own), group * LANES : (group + 1) * LANES
        ]
    fold_ref[: kept * own, :] = folded
    for i in range(own):
        turned = fold_ref[pl.ds(i, fold_ref.shape[0] // own, stride=own), :].T
        spectra = turned[:kinds, :SPECTRA_SUMMED]
        for tap in range(1, together):
            shifted = pltpu.roll(
                turned[tap * kinds : (tap + 1) * kinds, :], turned.shape[1] - tap, axis=1
            )
            spectra = spectra + shifted[:, :SPECTRA_SUMMED]
        spectra = spectra * mask_ref[0, i].astype(jnp.float32)
        for half in range(HALVES):
            for q in range(2):
                block_ref[pl.ds((i * HALVES + half) * 2 + q, chans, stride=4 * own), :] = spectra[
                    q * chans : (q + 1) * chans, half * LANES : (half + 1) * LANES
                ]
    block = block_ref[...].astype(jnp.bfloat16)
    for copy in range(copies):
        out_ref[copy] = block


def back_kernel(
    own, grid_side, tile_map_any, mine_ref, other_ref, out_ref,
    tile_map_ref, mine_wide, other_wide, signal_ref, sem,
):
    fetch = pltpu.make_async_copy(tile_map_any, tile_map_ref, sem)
    fetch.start()
    sources = mine_ref.shape[0]
    inputs = sources * 2 * own
    side = inputs // grid_side
    lines = mine_ref.shape[1]
    chan = lax.axis_index("chan")
    first_core = chan % 2 == 0
    mine_wide[...] = mine_ref[...].reshape(sources * lines, LANES).astype(jnp.float32)
    other_wide[...] = other_ref[...].reshape(sources * lines, LANES).astype(jnp.float32)
    for i in range(own):
        for half in range(HALVES):
            for q in range(2):
                line = (i * HALVES + half) * 2 + q
                low = pl.ds(line, sources, stride=lines)
                high = pl.ds(lines // 2 + line, sources, stride=lines)
                from_core = (
                    jnp.where(first_core, mine_wide[low, :], other_wide[high, :]),
                    jnp.where(first_core, other_wide[low, :], mine_wide[high, :]),
                )
                for core in range(2):
                    target = pl.ds(core * own + i, sources, stride=2 * own)
                    signal_ref[q * HALVES + half, target, :] = from_core[core]
    fetch.wait()
    tile = tile_map_ref[lax.axis_index("tile"), chan]
    row_start = pl.multiple_of((grid_side - 1 - tile // grid_side) * side, side)
    col_start = pl.multiple_of((grid_side - 1 - tile % grid_side) * side, side)
    to = lax.broadcasted_iota(jnp.int32, (side, side), 0)
    fro = lax.broadcasted_iota(jnp.int32, (side, side), 1)
    chip = 2 * own
    reverse = jnp.where(fro == side - chip - to // chip * chip + to % chip, 1.0, 0.0).astype(
        jnp.bfloat16
    )

    def inputs_from(start):
        planes = [signal_ref[plane, pl.ds(start, side), :] for plane in range(2 * HALVES)]
        signals = jnp.concatenate(planes, axis=1).astype(jnp.bfloat16)
        return jnp.dot(reverse, signals, preferred_element_type=jnp.float32).astype(jnp.bfloat16)

    rows, cols = inputs_from(row_start), inputs_from(col_start)
    swapped = jnp.concatenate([cols[:, SPECTRA_SUMMED:], -cols[:, :SPECTRA_SUMMED]], axis=1)
    for part, right in enumerate((cols, swapped)):
        product = lax.dot_general(
            rows, right, (((1,), (1,)), ((), ())), preferred_element_type=jnp.float32
        )
        out_ref[0, 0, part] = (product * (1.0 / SPECTRA_SUMMED)).astype(jnp.bfloat16)


def on_device(voltages, fir_taps, channels, input_good_mask, tile_map):
    own = voltages.shape[1]
    chans = channels.shape[0]
    n_chan = lax.axis_size("chan")
    n_tile = lax.axis_size("tile")
    assert chans == n_chan and 2 * chans <= LANES
    chips = n_chan // 2
    groups = [[2 * place + core for place in reversed(range(n_tile * chips))] for core in range(2)]
    x = voltages.reshape(own, FRAMES, BLOCKS, LANES).transpose(1, 2, 0, 3)
    operands = (channels, input_good_mask, fir_taps, x)
    hbm = pl.BlockSpec(memory_space=pltpu.HBM)
    vmem = pl.BlockSpec(memory_space=pltpu.VMEM)
    per_block = 2 * HALVES * own
    kinds = 2 * chans
    folded_rows = SPECTRA_SUMMED + (LANES if kinds < LANES else 0)
    spectra = pl.pallas_call(
        functools.partial(front_kernel, own, chans, n_tile),
        out_shape=pltpu.VMEM((n_tile, chans * per_block, LANES), jnp.bfloat16),
        in_specs=[hbm, hbm, hbm, hbm],
        out_specs=vmem,
        scratch_shapes=[
            pltpu.SMEM(channels.shape, jnp.int32),
            pltpu.SMEM(input_good_mask.shape, jnp.int32),
            pltpu.VMEM(fir_taps.shape, jnp.float32),
            pltpu.VMEM((BLOCKS, ROWS, own, LANES), jnp.bfloat16),
            pltpu.VMEM((FILTER_TAPS * kinds, TRANSFORM_LENGTH), jnp.bfloat16),
            pltpu.VMEM((own * ROWS, FILTER_TAPS * kinds), jnp.float32),
            pltpu.VMEM((own * folded_rows, LANES), jnp.float32),
            pltpu.VMEM((chans * per_block, LANES), jnp.float32),
            pltpu.SemaphoreType.DMA((BLOCKS,)),
            pltpu.SemaphoreType.DMA((3,)),
        ],
        compiler_params=pltpu.CompilerParams(vmem_limit_bytes=32 << 20),
        name="front",
    )(*(pltpu.with_memory_space_constraint(v, pltpu.HBM) for v in operands))
    spectra = spectra.reshape(n_tile * chips, 2 * per_block, LANES)
    mine = lax.all_to_all(
        spectra, ("tile", "chan"), split_axis=0, concat_axis=0, axis_index_groups=groups, tiled=True
    )
    other = lax.ppermute(mine, "chan", [(c, c ^ 1) for c in range(n_chan)])
    grid_side = n_tile // 8 + 2
    inputs = n_tile * n_chan * own
    side = inputs // grid_side
    return pl.pallas_call(
        functools.partial(back_kernel, own, grid_side),
        out_shape=jax.ShapeDtypeStruct((1, 1, 2, side, side), jnp.bfloat16),
        in_specs=[pl.BlockSpec(memory_space=pl.ANY), vmem, vmem],
        out_specs=vmem,
        scratch_shapes=[
            pltpu.SMEM(tile_map.shape[::-1], jnp.int32),
            pltpu.VMEM((n_tile * n_chan * per_block, LANES), jnp.float32),
            pltpu.VMEM((n_tile * n_chan * per_block, LANES), jnp.float32),
            pltpu.VMEM((2 * HALVES, inputs, LANES), jnp.float32),
            pltpu.SemaphoreType.DMA(()),
        ],
        compiler_params=pltpu.CompilerParams(vmem_limit_bytes=(4 << 20) + 60 * inputs * LANES * own),
        name="back",
    )(tile_map.T, mine, other)


def solution(mesh):
    in_specs = (P("tile", "chan", None), P(), P(), P("tile", "chan"), P())
    out_specs = P("chan", "tile", None, None, None)
    return jax.shard_map(
        on_device, mesh=mesh, in_specs=in_specs, out_specs=out_specs, check_vma=False
    )
```

```python
import functools
import math

import jax
import jax.numpy as jnp
from jax import lax
from jax.experimental import pallas as pl
from jax.experimental.pallas import tpu as pltpu
from jax.sharding import PartitionSpec as P

TRANSFORM_LENGTH = 2048
FILTER_TAPS = 16
SPECTRA_SUMMED = 256
FRAMES = SPECTRA_SUMMED + FILTER_TAPS - 1
ROWS = 272
LANES = 128
BLOCKS = TRANSFORM_LENGTH // LANES
HALVES = SPECTRA_SUMMED // LANES
GROUPS = (0, 6, 12, 14, 16)
PARTS = (0, 136, FRAMES)
OCTANT = TRANSFORM_LENGTH // 8


def cos_sin(phase):
    turns = (phase + OCTANT) // (2 * OCTANT)
    angle = (phase - turns * (2 * OCTANT)).astype(jnp.float32) * (2.0 * math.pi / TRANSFORM_LENGTH)
    square = angle * angle
    cosine, sine = jnp.zeros_like(angle), jnp.zeros_like(angle)
    for power in range(10, -1, -2):
        sign = -1.0 if power % 4 else 1.0
        cosine = cosine * square + sign / math.factorial(power)
        sine = sine * square + sign / math.factorial(power + 1)
    sine = sine * angle
    odd = (turns & 1) == 1
    first, second = jnp.where(odd, sine, cosine), jnp.where(odd, cosine, sine)
    first = jnp.where(((turns + 1) & 2) == 2, -first, first)
    second = jnp.where((turns & 2) == 2, -second, second)
    return first, second


def build_table(chans, channels_ref, taps_ref, table_ref):
    row = lax.broadcasted_iota(jnp.int32, (chans, LANES), 0)
    lane = lax.broadcasted_iota(jnp.int32, (chans, LANES), 1)
    channel = jnp.zeros((chans, LANES), jnp.int32)
    for c in range(chans):
        channel = jnp.where(row == c, channels_ref[chans - 2 - c + c % 2 * 2], channel)

    def unit(phase):
        return cos_sin(phase & (TRANSFORM_LENGTH - 1))

    factor = 1.0 / math.sqrt(TRANSFORM_LENGTH)
    cos0, sin0 = unit(channel * lane)
    blocks = [(cos0 * factor, sin0 * factor)]
    for bit in range(BLOCKS.bit_length() - 1):
        cos1, sin1 = unit(channel * (LANES << bit))
        blocks += [(c * cos1 - s * sin1, s * cos1 + c * sin1) for c, s in blocks]
    for nb, (cosine, sine) in enumerate(blocks):
        columns = slice(nb * LANES, (nb + 1) * LANES)
        dft = jnp.concatenate([cosine, -sine], axis=0)
        for tap in range(FILTER_TAPS):
            table_ref[tap * 2 * chans : (tap + 1) * 2 * chans, columns] = (
                dft * taps_ref[tap : tap + 1, columns]
            ).astype(jnp.bfloat16)


def front_kernel(
    own, chans, copies, channels_hbm, mask_hbm, taps_hbm, x_hbm, out_ref,
    channels_ref, mask_ref, taps_ref, x_ref, table_ref, partial_ref, fold_ref, block_ref,
    sems, small_sems,
):
    small = [
        pltpu.make_async_copy(source, target, small_sems.at[place])
        for place, (source, target) in enumerate(
            ((channels_hbm, channels_ref), (mask_hbm, mask_ref), (taps_hbm, taps_ref))
        )
    ]
    transfers = []
    for nb in range(BLOCKS):
        for part, (start, stop) in enumerate(zip(PARTS, PARTS[1:])):
            frames = pl.ds(start, stop - start)
            transfers.append(
                pltpu.make_async_copy(x_hbm.at[frames, nb], x_ref.at[nb, frames], sems.at[nb, part])
            )
    for transfer in small:
        transfer.start()
    for place, transfer in enumerate(transfers):
        transfer.start(priority=place % 2)
    for transfer in small:
        transfer.wait()
    build_table(chans, channels_ref, taps_ref, table_ref)
    rows_ref = x_ref.reshape(BLOCKS, ROWS * own, LANES)
    each = len(PARTS) - 1
    for first, last in zip(GROUPS, GROUPS[1:]):
        for transfer in transfers[first * each : last * each]:
            transfer.wait()
        product = lax.dot_general(
            jnp.concatenate([rows_ref[nb] for nb in range(first, last)], axis=1),
            table_ref[:, first * LANES : last * LANES],
            (((1,), (1,)), ((), ())),
            preferred_element_type=jnp.float32,
        )
        if last == BLOCKS:
            product = partial_ref[...] + product
        elif first:
            partial_ref[...] += product
        else:
            partial_ref[...] = product
    kinds = 2 * chans
    together = LANES // kinds
    kept = -(-(SPECTRA_SUMMED + together - 1) // 8) * 8
    folded = product[: kept * own, :LANES]
    for group in range(1, FILTER_TAPS // together):
        start = group * together * own
        folded = folded + product[
            start : start + kept * own, group * LANES : (group + 1) * LANES
        ]
    fold_ref[: kept * own, :] = folded
    for i in range(own):
        turned = fold_ref[pl.ds(i, fold_ref.shape[0] // own, stride=own), :].T
        spectra = turned[:kinds, :SPECTRA_SUMMED]
        for tap in range(1, together):
            shifted = pltpu.roll(
                turned[tap * kinds : (tap + 1) * kinds, :], turned.shape[1] - tap, axis=1
            )
            spectra = spectra + shifted[:, :SPECTRA_SUMMED]
        spectra = spectra * mask_ref[0, i].astype(jnp.float32)
        for half in range(HALVES):
            for q in range(2):
                block_ref[pl.ds((i * HALVES + half) * 2 + q, chans, stride=4 * own), :] = spectra[
                    q * chans : (q + 1) * chans, half * LANES : (half + 1) * LANES
                ]
    block = block_ref[...].astype(jnp.bfloat16)
    for copy in range(copies):
        out_ref[copy] = block


def back_kernel(
    own, grid_side, tile_map_any, mine_ref, other_ref, out_ref,
    tile_map_ref, mine_wide, other_wide, signal_ref, sem,
):
    fetch = pltpu.make_async_copy(tile_map_any, tile_map_ref, sem)
    fetch.start()
    sources = mine_ref.shape[0]
    inputs = sources * 2 * own
    side = inputs // grid_side
    lines = mine_ref.shape[1]
    chan = lax.axis_index("chan")
    first_core = chan % 2 == 0
    mine_wide[...] = mine_ref[...].reshape(sources * lines, LANES).astype(jnp.float32)
    other_wide[...] = other_ref[...].reshape(sources * lines, LANES).astype(jnp.float32)
    for i in range(own):
        for half in range(HALVES):
            for q in range(2):
                line = (i * HALVES + half) * 2 + q
                low = pl.ds(line, sources, stride=lines)
                high = pl.ds(lines // 2 + line, sources, stride=lines)
                from_core = (
                    jnp.where(first_core, mine_wide[low, :], other_wide[high, :]),
                    jnp.where(first_core, other_wide[low, :], mine_wide[high, :]),
                )
                for core in range(2):
                    target = pl.ds(core * own + i, sources, stride=2 * own)
                    signal_ref[q * HALVES + half, target, :] = from_core[core]
    fetch.wait()
    tile = tile_map_ref[lax.axis_index("tile"), chan]
    row_start = pl.multiple_of((grid_side - 1 - tile // grid_side) * side, side)
    col_start = pl.multiple_of((grid_side - 1 - tile % grid_side) * side, side)
    to = lax.broadcasted_iota(jnp.int32, (side, side), 0)
    fro = lax.broadcasted_iota(jnp.int32, (side, side), 1)
    chip = 2 * own
    reverse = jnp.where(fro == side - chip - to // chip * chip + to % chip, 1.0, 0.0).astype(
        jnp.bfloat16
    )

    def inputs_from(start):
        planes = [signal_ref[plane, pl.ds(start, side), :] for plane in range(2 * HALVES)]
        signals = jnp.concatenate(planes, axis=1).astype(jnp.bfloat16)
        return jnp.dot(reverse, signals, preferred_element_type=jnp.float32).astype(jnp.bfloat16)

    rows, cols = inputs_from(row_start), inputs_from(col_start)
    swapped = jnp.concatenate([cols[:, SPECTRA_SUMMED:], -cols[:, :SPECTRA_SUMMED]], axis=1)
    for part, right in enumerate((cols, swapped)):
        product = lax.dot_general(
            rows, right, (((1,), (1,)), ((), ())), preferred_element_type=jnp.float32
        )
        out_ref[0, 0, part] = (product * (1.0 / SPECTRA_SUMMED)).astype(jnp.bfloat16)


def on_device(voltages, fir_taps, channels, input_good_mask, tile_map):
    own = voltages.shape[1]
    chans = channels.shape[0]
    n_chan = lax.axis_size("chan")
    n_tile = lax.axis_size("tile")
    assert chans == n_chan and 2 * chans <= LANES
    chips = n_chan // 2
    groups = [[2 * place + core for place in reversed(range(n_tile * chips))] for core in range(2)]
    x = voltages.reshape(own, FRAMES, BLOCKS, LANES).transpose(1, 2, 0, 3)
    operands = (channels, input_good_mask, fir_taps, x)
    hbm = pl.BlockSpec(memory_space=pltpu.HBM)
    vmem = pl.BlockSpec(memory_space=pltpu.VMEM)
    per_block = 2 * HALVES * own
    kinds = 2 * chans
    folded_rows = SPECTRA_SUMMED + (LANES if kinds < LANES else 0)
    spectra = pl.pallas_call(
        functools.partial(front_kernel, own, chans, n_tile),
        out_shape=pltpu.VMEM((n_tile, chans * per_block, LANES), jnp.bfloat16),
        in_specs=[hbm, hbm, hbm, hbm],
        out_specs=vmem,
        scratch_shapes=[
            pltpu.SMEM(channels.shape, jnp.int32),
            pltpu.SMEM(input_good_mask.shape, jnp.int32),
            pltpu.VMEM(fir_taps.shape, jnp.float32),
            pltpu.VMEM((BLOCKS, ROWS, own, LANES), jnp.bfloat16),
            pltpu.VMEM((FILTER_TAPS * kinds, TRANSFORM_LENGTH), jnp.bfloat16),
            pltpu.VMEM((own * ROWS, FILTER_TAPS * kinds), jnp.float32),
            pltpu.VMEM((own * folded_rows, LANES), jnp.float32),
            pltpu.VMEM((chans * per_block, LANES), jnp.float32),
            pltpu.SemaphoreType.DMA((BLOCKS, len(PARTS) - 1)),
            pltpu.SemaphoreType.DMA((3,)),
        ],
        compiler_params=pltpu.CompilerParams(vmem_limit_bytes=32 << 20),
        name="front",
    )(*(pltpu.with_memory_space_constraint(v, pltpu.HBM) for v in operands))
    spectra = spectra.reshape(n_tile * chips, 2 * per_block, LANES)
    mine = lax.all_to_all(
        spectra, ("tile", "chan"), split_axis=0, concat_axis=0, axis_index_groups=groups, tiled=True
    )
    other = lax.ppermute(mine, "chan", [(c, c ^ 1) for c in range(n_chan)])
    grid_side = n_tile // 8 + 2
    inputs = n_tile * n_chan * own
    side = inputs // grid_side
    return pl.pallas_call(
        functools.partial(back_kernel, own, grid_side),
        out_shape=jax.ShapeDtypeStruct((1, 1, 2, side, side), jnp.bfloat16),
        in_specs=[pl.BlockSpec(memory_space=pl.ANY), vmem, vmem],
        out_specs=vmem,
        scratch_shapes=[
            pltpu.SMEM(tile_map.shape[::-1], jnp.int32),
            pltpu.VMEM((n_tile * n_chan * per_block, LANES), jnp.float32),
            pltpu.VMEM((n_tile * n_chan * per_block, LANES), jnp.float32),
            pltpu.VMEM((2 * HALVES, inputs, LANES), jnp.float32),
            pltpu.SemaphoreType.DMA(()),
        ],
        compiler_params=pltpu.CompilerParams(vmem_limit_bytes=(4 << 20) + 60 * inputs * LANES * own),
        name="back",
    )(tile_map.T, mine, other)


def solution(mesh):
    in_specs = (P("tile", "chan", None), P(), P(), P("tile", "chan"), P())
    out_specs = P("chan", "tile", None, None, None)
    return jax.shard_map(
        on_device, mesh=mesh, in_specs=in_specs, out_specs=out_specs, check_vma=False
    )
```

```python
import functools
import math

import jax
import jax.numpy as jnp
from jax import lax
from jax.experimental import pallas as pl
from jax.experimental.pallas import tpu as pltpu
from jax.sharding import PartitionSpec as P

TRANSFORM_LENGTH = 2048
FILTER_TAPS = 16
SPECTRA_SUMMED = 256
FRAMES = SPECTRA_SUMMED + FILTER_TAPS - 1
ROWS = 272
LANES = 128
BLOCKS = TRANSFORM_LENGTH // LANES
HALVES = SPECTRA_SUMMED // LANES
GROUPS = (0, 6, 12, 14, 16)
PARTS = (0, 136, FRAMES)
OCTANT = TRANSFORM_LENGTH // 8


def cos_sin(phase):
    turns = (phase + OCTANT) >> (OCTANT.bit_length())
    angle = (phase - (turns << OCTANT.bit_length())).astype(jnp.float32) * (2.0 * math.pi / TRANSFORM_LENGTH)
    square = angle * angle
    cosine, sine = jnp.zeros_like(angle), jnp.zeros_like(angle)
    for power in range(10, -1, -2):
        sign = -1.0 if power % 4 else 1.0
        cosine = cosine * square + sign / math.factorial(power)
        sine = sine * square + sign / math.factorial(power + 1)
    sine = sine * angle
    odd = (turns & 1) == 1
    first, second = jnp.where(odd, sine, cosine), jnp.where(odd, cosine, sine)
    first = jnp.where(((turns + 1) & 2) == 2, -first, first)
    second = jnp.where((turns & 2) == 2, -second, second)
    return first, second


def build_table(chans, channels_ref, taps_ref, table_ref):
    row = lax.broadcasted_iota(jnp.int32, (chans, LANES), 0)
    lane = lax.broadcasted_iota(jnp.int32, (chans, LANES), 1)
    channel = jnp.zeros((chans, LANES), jnp.int32)
    for c in range(chans):
        channel = jnp.where(row == c, channels_ref[chans - 2 - c + c % 2 * 2], channel)

    def unit(phase):
        return cos_sin(phase & (TRANSFORM_LENGTH - 1))

    factor = 1.0 / math.sqrt(TRANSFORM_LENGTH)
    cos0, sin0 = unit(channel * lane)
    blocks = [(cos0 * factor, sin0 * factor)]
    for bit in range(BLOCKS.bit_length() - 1):
        cos1, sin1 = unit(channel * (LANES << bit))
        blocks += [(c * cos1 - s * sin1, s * cos1 + c * sin1) for c, s in blocks]
    for nb, (cosine, sine) in enumerate(blocks):
        columns = slice(nb * LANES, (nb + 1) * LANES)
        dft = jnp.concatenate([cosine, -sine], axis=0)
        for tap in range(FILTER_TAPS):
            table_ref[tap * 2 * chans : (tap + 1) * 2 * chans, columns] = (
                dft * taps_ref[tap : tap + 1, columns]
            ).astype(jnp.bfloat16)


def front_kernel(
    own, chans, copies, channels_hbm, mask_hbm, taps_hbm, x_hbm, out_ref,
    channels_ref, mask_ref, taps_ref, x_ref, table_ref, partial_ref, fold_ref, block_ref,
    sems, small_sems,
):
    small = [
        pltpu.make_async_copy(source, target, small_sems.at[place])
        for place, (source, target) in enumerate(
            ((channels_hbm, channels_ref), (mask_hbm, mask_ref), (taps_hbm, taps_ref))
        )
    ]
    transfers = []
    for nb in range(BLOCKS):
        for part, (start, stop) in enumerate(zip(PARTS, PARTS[1:])):
            frames = pl.ds(start, stop - start)
            transfers.append(
                pltpu.make_async_copy(x_hbm.at[frames, nb], x_ref.at[nb, frames], sems.at[nb, part])
            )
    for transfer in small:
        transfer.start()
    for place, transfer in enumerate(transfers):
        transfer.start(priority=place % 2)
    for transfer in small:
        transfer.wait()
    build_table(chans, channels_ref, taps_ref, table_ref)
    rows_ref = x_ref.reshape(BLOCKS, ROWS * own, LANES)
    each = len(PARTS) - 1
    for first, last in zip(GROUPS, GROUPS[1:]):
        for transfer in transfers[first * each : last * each]:
            transfer.wait()
        product = lax.dot_general(
            jnp.concatenate([rows_ref[nb] for nb in range(first, last)], axis=1),
            table_ref[:, first * LANES : last * LANES],
            (((1,), (1,)), ((), ())),
            preferred_element_type=jnp.float32,
        )
        if last == BLOCKS:
            product = partial_ref[...] + product
        elif first:
            partial_ref[...] += product
        else:
            partial_ref[...] = product
    kinds = 2 * chans
    together = LANES // kinds
    kept = -(-(SPECTRA_SUMMED + together - 1) // 8) * 8
    folded = product[: kept * own, :LANES]
    for group in range(1, FILTER_TAPS // together):
        start = group * together * own
        folded = folded + product[
            start : start + kept * own, group * LANES : (group + 1) * LANES
        ]
    fold_ref[: kept * own, :] = folded
    for i in range(own):
        turned = fold_ref[pl.ds(i, fold_ref.shape[0] // own, stride=own), :].T
        spectra = turned[:kinds, :SPECTRA_SUMMED]
        for tap in range(1, together):
            shifted = pltpu.roll(
                turned[tap * kinds : (tap + 1) * kinds, :], turned.shape[1] - tap, axis=1
            )
            spectra = spectra + shifted[:, :SPECTRA_SUMMED]
        spectra = spectra * mask_ref[0, i].astype(jnp.float32)
        for half in range(HALVES):
            for q in range(2):
                block_ref[pl.ds((i * HALVES + half) * 2 + q, chans, stride=4 * own), :] = spectra[
                    q * chans : (q + 1) * chans, half * LANES : (half + 1) * LANES
                ]
    block = block_ref[...].astype(jnp.bfloat16)
    for copy in range(copies):
        out_ref[copy] = block


def back_kernel(
    own, grid_side, tile_map_any, mine_ref, other_ref, out_ref,
    tile_map_ref, mine_wide, other_wide, signal_ref, sem,
):
    fetch = pltpu.make_async_copy(tile_map_any, tile_map_ref, sem)
    fetch.start()
    sources = mine_ref.shape[0]
    inputs = sources * 2 * own
    side = inputs // grid_side
    lines = mine_ref.shape[1]
    chan = lax.axis_index("chan")
    first_core = (chan & 1) == 0
    mine_wide[...] = mine_ref[...].reshape(sources * lines, LANES).astype(jnp.float32)
    other_wide[...] = other_ref[...].reshape(sources * lines, LANES).astype(jnp.float32)
    for i in range(own):
        for half in range(HALVES):
            for q in range(2):
                line = (i * HALVES + half) * 2 + q
                low = pl.ds(line, sources, stride=lines)
                high = pl.ds(lines // 2 + line, sources, stride=lines)
                from_core = (
                    jnp.where(first_core, mine_wide[low, :], other_wide[high, :]),
                    jnp.where(first_core, other_wide[low, :], mine_wide[high, :]),
                )
                for core in range(2):
                    target = pl.ds(core * own + i, sources, stride=2 * own)
                    signal_ref[q * HALVES + half, target, :] = from_core[core]
    fetch.wait()
    tile = tile_map_ref[lax.axis_index("tile"), chan]
    bits = grid_side.bit_length() - 1
    row_start = pl.multiple_of((grid_side - 1 - (tile >> bits)) * side, side)
    col_start = pl.multiple_of((grid_side - 1 - (tile & (grid_side - 1))) * side, side)
    to = lax.broadcasted_iota(jnp.int32, (side, side), 0)
    fro = lax.broadcasted_iota(jnp.int32, (side, side), 1)
    reverse = jnp.where(fro == to ^ (side - 2 * own), 1.0, 0.0).astype(jnp.bfloat16)

    def inputs_from(start):
        planes = [signal_ref[plane, pl.ds(start, side), :] for plane in range(2 * HALVES)]
        signals = jnp.concatenate(planes, axis=1).astype(jnp.bfloat16)
        return jnp.dot(reverse, signals, preferred_element_type=jnp.float32).astype(jnp.bfloat16)

    rows, cols = inputs_from(row_start), inputs_from(col_start)
    swapped = jnp.concatenate([cols[:, SPECTRA_SUMMED:], -cols[:, :SPECTRA_SUMMED]], axis=1)
    for part, right in enumerate((cols, swapped)):
        product = lax.dot_general(
            rows, right, (((1,), (1,)), ((), ())), preferred_element_type=jnp.float32
        )
        out_ref[0, 0, part] = (product * (1.0 / SPECTRA_SUMMED)).astype(jnp.bfloat16)


def on_device(voltages, fir_taps, channels, input_good_mask, tile_map):
    own = voltages.shape[1]
    chans = channels.shape[0]
    n_chan = lax.axis_size("chan")
    n_tile = lax.axis_size("tile")
    assert chans == n_chan and 2 * chans <= LANES and n_chan & (n_chan - 1) == 0
    chips = n_chan // 2
    groups = [[2 * place + core for place in reversed(range(n_tile * chips))] for core in range(2)]
    x = voltages.reshape(own, FRAMES, BLOCKS, LANES).transpose(1, 2, 0, 3)
    operands = (channels, input_good_mask, fir_taps, x)
    hbm = pl.BlockSpec(memory_space=pltpu.HBM)
    vmem = pl.BlockSpec(memory_space=pltpu.VMEM)
    per_block = 2 * HALVES * own
    kinds = 2 * chans
    folded_rows = SPECTRA_SUMMED + (LANES if kinds < LANES else 0)
    spectra = pl.pallas_call(
        functools.partial(front_kernel, own, chans, n_tile),
        out_shape=pltpu.VMEM((n_tile, chans * per_block, LANES), jnp.bfloat16),
        in_specs=[hbm, hbm, hbm, hbm],
        out_specs=vmem,
        scratch_shapes=[
            pltpu.SMEM(channels.shape, jnp.int32),
            pltpu.SMEM(input_good_mask.shape, jnp.int32),
            pltpu.VMEM(fir_taps.shape, jnp.float32),
            pltpu.VMEM((BLOCKS, ROWS, own, LANES), jnp.bfloat16),
            pltpu.VMEM((FILTER_TAPS * kinds, TRANSFORM_LENGTH), jnp.bfloat16),
            pltpu.VMEM((own * ROWS, FILTER_TAPS * kinds), jnp.float32),
            pltpu.VMEM((own * folded_rows, LANES), jnp.float32),
            pltpu.VMEM((chans * per_block, LANES), jnp.float32),
            pltpu.SemaphoreType.DMA((BLOCKS, len(PARTS) - 1)),
            pltpu.SemaphoreType.DMA((3,)),
        ],
        compiler_params=pltpu.CompilerParams(vmem_limit_bytes=32 << 20),
        name="front",
    )(*(pltpu.with_memory_space_constraint(v, pltpu.HBM) for v in operands))
    spectra = spectra.reshape(n_tile * chips, 2 * per_block, LANES)
    mine = lax.all_to_all(
        spectra, ("tile", "chan"), split_axis=0, concat_axis=0, axis_index_groups=groups, tiled=True
    )
    other = lax.ppermute(mine, "chan", [(c, c ^ 1) for c in range(n_chan)])
    grid_side = n_tile // 8 + 2
    inputs = n_tile * n_chan * own
    side = inputs // grid_side
    return pl.pallas_call(
        functools.partial(back_kernel, own, grid_side),
        out_shape=jax.ShapeDtypeStruct((1, 1, 2, side, side), jnp.bfloat16),
        in_specs=[pl.BlockSpec(memory_space=pl.ANY), vmem, vmem],
        out_specs=vmem,
        scratch_shapes=[
            pltpu.SMEM(tile_map.shape[::-1], jnp.int32),
            pltpu.VMEM((n_tile * n_chan * per_block, LANES), jnp.float32),
            pltpu.VMEM((n_tile * n_chan * per_block, LANES), jnp.float32),
            pltpu.VMEM((2 * HALVES, inputs, LANES), jnp.float32),
            pltpu.SemaphoreType.DMA(()),
        ],
        compiler_params=pltpu.CompilerParams(vmem_limit_bytes=(4 << 20) + 60 * inputs * LANES * own),
        name="back",
    )(tile_map.T, mine, other)


def solution(mesh):
    in_specs = (P("tile", "chan", None), P(), P(), P("tile", "chan"), P())
    out_specs = P("chan", "tile", None, None, None)
    return jax.shard_map(
        on_device, mesh=mesh, in_specs=in_specs, out_specs=out_specs, check_vma=False
    )
```

```python
import functools
import math

import jax
import jax.numpy as jnp
from jax import lax
from jax.experimental import pallas as pl
from jax.experimental.pallas import tpu as pltpu
from jax.sharding import PartitionSpec as P

TRANSFORM_LENGTH = 2048
FILTER_TAPS = 16
SPECTRA_SUMMED = 256
FRAMES = SPECTRA_SUMMED + FILTER_TAPS - 1
ROWS = 272
LANES = 128
BLOCKS = TRANSFORM_LENGTH // LANES
HALVES = SPECTRA_SUMMED // LANES
GROUPS = (0, 6, 12, 14, 16)
PARTS = (0, 136, FRAMES)
OCTANT = TRANSFORM_LENGTH // 8


def cos_sin(phase):
    turns = (phase + OCTANT) >> (OCTANT.bit_length())
    angle = (phase - (turns << OCTANT.bit_length())).astype(jnp.float32) * (2.0 * math.pi / TRANSFORM_LENGTH)
    square = angle * angle
    cosine, sine = jnp.zeros_like(angle), jnp.zeros_like(angle)
    for power in range(10, -1, -2):
        sign = -1.0 if power % 4 else 1.0
        cosine = cosine * square + sign / math.factorial(power)
        sine = sine * square + sign / math.factorial(power + 1)
    sine = sine * angle
    odd = (turns & 1) == 1
    first, second = jnp.where(odd, sine, cosine), jnp.where(odd, cosine, sine)
    first = jnp.where(((turns + 1) & 2) == 2, -first, first)
    second = jnp.where((turns & 2) == 2, -second, second)
    return first, second


def build_table(chans, channels_ref, taps_ref, table_ref):
    row = lax.broadcasted_iota(jnp.int32, (chans, LANES), 0)
    lane = lax.broadcasted_iota(jnp.int32, (chans, LANES), 1)
    channel = jnp.zeros((chans, LANES), jnp.int32)
    for c in range(chans):
        channel = jnp.where(row == c, channels_ref[c], channel)

    def unit(phase):
        return cos_sin(phase & (TRANSFORM_LENGTH - 1))

    factor = 1.0 / math.sqrt(TRANSFORM_LENGTH)
    cos0, sin0 = unit(channel * lane)
    blocks = [(cos0 * factor, sin0 * factor)]
    for bit in range(BLOCKS.bit_length() - 1):
        cos1, sin1 = unit(channel * (LANES << bit))
        blocks += [(c * cos1 - s * sin1, s * cos1 + c * sin1) for c, s in blocks]
    for nb, (cosine, sine) in enumerate(blocks):
        columns = slice(nb * LANES, (nb + 1) * LANES)
        dft = jnp.concatenate([cosine, -sine], axis=0)
        for tap in range(FILTER_TAPS):
            table_ref[tap * 2 * chans : (tap + 1) * 2 * chans, columns] = (
                dft * taps_ref[tap : tap + 1, columns]
            ).astype(jnp.bfloat16)


def front_kernel(
    own, chans, copies, channels_hbm, mask_hbm, taps_hbm, x_hbm, out_ref,
    channels_ref, mask_ref, taps_ref, x_ref, table_ref, partial_ref, fold_ref, block_ref,
    sems, small_sems,
):
    small = [
        pltpu.make_async_copy(source, target, small_sems.at[place])
        for place, (source, target) in enumerate(
            ((channels_hbm, channels_ref), (mask_hbm, mask_ref), (taps_hbm, taps_ref))
        )
    ]
    transfers = []
    for nb in range(BLOCKS):
        for part, (start, stop) in enumerate(zip(PARTS, PARTS[1:])):
            frames = pl.ds(start, stop - start)
            transfers.append(
                pltpu.make_async_copy(x_hbm.at[frames, nb], x_ref.at[nb, frames], sems.at[nb, part])
            )
    for transfer in small:
        transfer.start()
    for place, transfer in enumerate(transfers):
        transfer.start(priority=place % 2)
    for transfer in small:
        transfer.wait()
    build_table(chans, channels_ref, taps_ref, table_ref)
    rows_ref = x_ref.reshape(BLOCKS, ROWS * own, LANES)
    each = len(PARTS) - 1
    for first, last in zip(GROUPS, GROUPS[1:]):
        for transfer in transfers[first * each : last * each]:
            transfer.wait()
        product = lax.dot_general(
            jnp.concatenate([rows_ref[nb] for nb in range(first, last)], axis=1),
            table_ref[:, first * LANES : last * LANES],
            (((1,), (1,)), ((), ())),
            preferred_element_type=jnp.float32,
        )
        if last == BLOCKS:
            product = partial_ref[...] + product
        elif first:
            partial_ref[...] += product
        else:
            partial_ref[...] = product
    kinds = 2 * chans
    together = LANES // kinds
    kept = -(-(SPECTRA_SUMMED + together - 1) // 8) * 8
    folded = product[: kept * own, :LANES]
    for group in range(1, FILTER_TAPS // together):
        start = group * together * own
        folded = folded + product[
            start : start + kept * own, group * LANES : (group + 1) * LANES
        ]
    fold_ref[: kept * own, :] = folded
    for i in range(own):
        turned = fold_ref[pl.ds(i, fold_ref.shape[0] // own, stride=own), :].T
        spectra = turned[:kinds, :SPECTRA_SUMMED]
        for tap in range(1, together):
            shifted = pltpu.roll(
                turned[tap * kinds : (tap + 1) * kinds, :], turned.shape[1] - tap, axis=1
            )
            spectra = spectra + shifted[:, :SPECTRA_SUMMED]
        spectra = spectra * mask_ref[0, i].astype(jnp.float32)
        for half in range(HALVES):
            for q in range(2):
                block_ref[pl.ds((i * HALVES + half) * 2 + q, chans, stride=4 * own), :] = spectra[
                    q * chans : (q + 1) * chans, half * LANES : (half + 1) * LANES
                ]
    block = block_ref[...].astype(jnp.bfloat16)
    for copy in range(copies):
        out_ref[copy] = block


def back_kernel(
    own, grid_side, tile_map_any, blocks_ref, out_ref, tile_map_ref, wide_ref, signal_ref, sem
):
    fetch = pltpu.make_async_copy(tile_map_any, tile_map_ref, sem)
    fetch.start()
    sources = blocks_ref.shape[0]
    inputs = sources * own
    side = inputs // grid_side
    lines = blocks_ref.shape[1]
    wide_ref[...] = blocks_ref[...].reshape(sources * lines, LANES).astype(jnp.float32)
    for i in range(own):
        for half in range(HALVES):
            for q in range(2):
                signal_ref[q * HALVES + half, pl.ds(i, sources, stride=own), :] = wide_ref[
                    pl.ds((i * HALVES + half) * 2 + q, sources, stride=lines), :
                ]
    fetch.wait()
    tile = tile_map_ref[lax.axis_index("tile"), lax.axis_index("chan")]
    bits = grid_side.bit_length() - 1
    row_start = pl.multiple_of((tile >> bits) * side, side)
    col_start = pl.multiple_of((tile & (grid_side - 1)) * side, side)

    def inputs_from(start):
        planes = [signal_ref[plane, pl.ds(start, side), :] for plane in range(2 * HALVES)]
        return jnp.concatenate(planes, axis=1).astype(jnp.bfloat16)

    rows, cols = inputs_from(row_start), inputs_from(col_start)
    swapped = jnp.concatenate([cols[:, SPECTRA_SUMMED:], -cols[:, :SPECTRA_SUMMED]], axis=1)
    for part, right in enumerate((cols, swapped)):
        product = lax.dot_general(
            rows, right, (((1,), (1,)), ((), ())), preferred_element_type=jnp.float32
        )
        out_ref[0, 0, part] = (product * (1.0 / SPECTRA_SUMMED)).astype(jnp.bfloat16)


def on_device(voltages, fir_taps, channels, input_good_mask, tile_map):
    own = voltages.shape[1]
    chans = channels.shape[0]
    n_chan = lax.axis_size("chan")
    n_tile = lax.axis_size("tile")
    assert chans == n_chan and 2 * chans <= LANES and n_tile in (4, 16)
    x = voltages.reshape(own, FRAMES, BLOCKS, LANES).transpose(1, 2, 0, 3)
    operands = (channels, input_good_mask, fir_taps, x)
    hbm = pl.BlockSpec(memory_space=pltpu.HBM)
    vmem = pl.BlockSpec(memory_space=pltpu.VMEM)
    per_block = 2 * HALVES * own
    kinds = 2 * chans
    folded_rows = SPECTRA_SUMMED + (LANES if kinds < LANES else 0)
    spectra = pl.pallas_call(
        functools.partial(front_kernel, own, chans, n_tile),
        out_shape=pltpu.VMEM((n_tile, chans * per_block, LANES), jnp.bfloat16),
        in_specs=[hbm, hbm, hbm, hbm],
        out_specs=vmem,
        scratch_shapes=[
            pltpu.SMEM(channels.shape, jnp.int32),
            pltpu.SMEM(input_good_mask.shape, jnp.int32),
            pltpu.VMEM(fir_taps.shape, jnp.float32),
            pltpu.VMEM((BLOCKS, ROWS, own, LANES), jnp.bfloat16),
            pltpu.VMEM((FILTER_TAPS * kinds, TRANSFORM_LENGTH), jnp.bfloat16),
            pltpu.VMEM((own * ROWS, FILTER_TAPS * kinds), jnp.float32),
            pltpu.VMEM((own * folded_rows, LANES), jnp.float32),
            pltpu.VMEM((chans * per_block, LANES), jnp.float32),
            pltpu.SemaphoreType.DMA((BLOCKS, len(PARTS) - 1)),
            pltpu.SemaphoreType.DMA((3,)),
        ],
        compiler_params=pltpu.CompilerParams(vmem_limit_bytes=32 << 20),
        name="front",
    )(*(pltpu.with_memory_space_constraint(v, pltpu.HBM) for v in operands))
    spectra = spectra.reshape(n_tile * n_chan, per_block, LANES)
    turned = lax.all_to_all(spectra, ("tile", "chan"), split_axis=0, concat_axis=0, tiled=True)
    grid_side = n_tile // 8 + 2
    inputs = n_tile * n_chan * own
    side = inputs // grid_side
    return pl.pallas_call(
        functools.partial(back_kernel, own, grid_side),
        out_shape=jax.ShapeDtypeStruct((1, 1, 2, side, side), jnp.bfloat16),
        in_specs=[pl.BlockSpec(memory_space=pl.ANY), vmem],
        out_specs=vmem,
        scratch_shapes=[
            pltpu.SMEM(tile_map.shape[::-1], jnp.int32),
            pltpu.VMEM((n_tile * n_chan * per_block, LANES), jnp.float32),
            pltpu.VMEM((2 * HALVES, inputs, LANES), jnp.float32),
            pltpu.SemaphoreType.DMA(()),
        ],
        compiler_params=pltpu.CompilerParams(vmem_limit_bytes=(4 << 20) + 60 * inputs * LANES * own),
        name="back",
    )(tile_map.T, turned)


def solution(mesh):
    in_specs = (P("tile", "chan", None), P(), P(), P("tile", "chan"), P())
    out_specs = P("chan", "tile", None, None, None)
    return jax.shard_map(
        on_device, mesh=mesh, in_specs=in_specs, out_specs=out_specs, check_vma=False
    )
```

```python
import functools
import math

import jax
import jax.numpy as jnp
from jax import lax
from jax.experimental import pallas as pl
from jax.experimental.pallas import tpu as pltpu
from jax.sharding import PartitionSpec as P

TRANSFORM_LENGTH = 2048
FILTER_TAPS = 16
SPECTRA_SUMMED = 256
FRAMES = SPECTRA_SUMMED + FILTER_TAPS - 1
ROWS = 272
LANES = 128
BLOCKS = TRANSFORM_LENGTH // LANES
HALVES = SPECTRA_SUMMED // LANES
GROUPS = (0, 6, 12, 14, 16)
PARTS = (0, 136, FRAMES)
OCTANT = TRANSFORM_LENGTH // 8


def cos_sin(phase):
    turns = (phase + OCTANT) >> (OCTANT.bit_length())
    angle = (phase - (turns << OCTANT.bit_length())).astype(jnp.float32) * (2.0 * math.pi / TRANSFORM_LENGTH)
    square = angle * angle
    cosine, sine = jnp.zeros_like(angle), jnp.zeros_like(angle)
    for power in range(10, -1, -2):
        sign = -1.0 if power % 4 else 1.0
        cosine = cosine * square + sign / math.factorial(power)
        sine = sine * square + sign / math.factorial(power + 1)
    sine = sine * angle
    odd = (turns & 1) == 1
    first, second = jnp.where(odd, sine, cosine), jnp.where(odd, cosine, sine)
    first = jnp.where(((turns + 1) & 2) == 2, -first, first)
    second = jnp.where((turns & 2) == 2, -second, second)
    return first, second


def build_table(chans, channels_ref, taps_ref, table_ref):
    row = lax.broadcasted_iota(jnp.int32, (chans, LANES), 0)
    lane = lax.broadcasted_iota(jnp.int32, (chans, LANES), 1)
    channel = jnp.zeros((chans, LANES), jnp.int32)
    for c in range(chans):
        channel = jnp.where(row == c, channels_ref[(c + chans - 2) % chans], channel)

    def unit(phase):
        return cos_sin(phase & (TRANSFORM_LENGTH - 1))

    factor = 1.0 / math.sqrt(TRANSFORM_LENGTH)
    cos0, sin0 = unit(channel * lane)
    blocks = [(cos0 * factor, sin0 * factor)]
    for bit in range(BLOCKS.bit_length() - 1):
        cos1, sin1 = unit(channel * (LANES << bit))
        blocks += [(c * cos1 - s * sin1, s * cos1 + c * sin1) for c, s in blocks]
    for nb, (cosine, sine) in enumerate(blocks):
        columns = slice(nb * LANES, (nb + 1) * LANES)
        dft = jnp.concatenate([cosine, -sine], axis=0)
        for tap in range(FILTER_TAPS):
            table_ref[tap * 2 * chans : (tap + 1) * 2 * chans, columns] = (
                dft * taps_ref[tap : tap + 1, columns]
            ).astype(jnp.bfloat16)


def front_kernel(
    own, chans, copies, channels_hbm, mask_hbm, taps_hbm, x_hbm, out_ref,
    channels_ref, mask_ref, taps_ref, x_ref, table_ref, partial_ref, fold_ref, block_ref,
    sems, small_sems,
):
    small = [
        pltpu.make_async_copy(source, target, small_sems.at[place])
        for place, (source, target) in enumerate(
            ((channels_hbm, channels_ref), (mask_hbm, mask_ref), (taps_hbm, taps_ref))
        )
    ]
    transfers = []
    for nb in range(BLOCKS):
        for part, (start, stop) in enumerate(zip(PARTS, PARTS[1:])):
            frames = pl.ds(start, stop - start)
            transfers.append(
                pltpu.make_async_copy(x_hbm.at[frames, nb], x_ref.at[nb, frames], sems.at[nb, part])
            )
    for transfer in small:
        transfer.start()
    for place, transfer in enumerate(transfers):
        transfer.start(priority=place % 2)
    for transfer in small:
        transfer.wait()
    build_table(chans, channels_ref, taps_ref, table_ref)
    rows_ref = x_ref.reshape(BLOCKS, ROWS * own, LANES)
    each = len(PARTS) - 1
    for first, last in zip(GROUPS, GROUPS[1:]):
        for transfer in transfers[first * each : last * each]:
            transfer.wait()
        product = lax.dot_general(
            jnp.concatenate([rows_ref[nb] for nb in range(first, last)], axis=1),
            table_ref[:, first * LANES : last * LANES],
            (((1,), (1,)), ((), ())),
            preferred_element_type=jnp.float32,
        )
        if last == BLOCKS:
            product = partial_ref[...] + product
        elif first:
            partial_ref[...] += product
        else:
            partial_ref[...] = product
    kinds = 2 * chans
    together = LANES // kinds
    kept = -(-(SPECTRA_SUMMED + together - 1) // 8) * 8
    folded = product[: kept * own, :LANES]
    for group in range(1, FILTER_TAPS // together):
        start = group * together * own
        folded = folded + product[
            start : start + kept * own, group * LANES : (group + 1) * LANES
        ]
    fold_ref[: kept * own, :] = folded
    for i in range(own):
        turned = fold_ref[pl.ds(i, fold_ref.shape[0] // own, stride=own), :].T
        spectra = turned[:kinds, :SPECTRA_SUMMED]
        for tap in range(1, together):
            shifted = pltpu.roll(
                turned[tap * kinds : (tap + 1) * kinds, :], turned.shape[1] - tap, axis=1
            )
            spectra = spectra + shifted[:, :SPECTRA_SUMMED]
        spectra = spectra * mask_ref[0, i].astype(jnp.float32)
        for half in range(HALVES):
            for q in range(2):
                block_ref[pl.ds((i * HALVES + half) * 2 + q, chans, stride=4 * own), :] = spectra[
                    q * chans : (q + 1) * chans, half * LANES : (half + 1) * LANES
                ]
    block = block_ref[...].astype(jnp.bfloat16)
    for copy in range(copies):
        out_ref[copy] = block


def back_kernel(
    own, grid_side, tile_map_any, mine_ref, other_ref, out_ref,
    tile_map_ref, mine_wide, other_wide, signal_ref, sem,
):
    fetch = pltpu.make_async_copy(tile_map_any, tile_map_ref, sem)
    fetch.start()
    sources = mine_ref.shape[0]
    inputs = sources * 2 * own
    side = inputs // grid_side
    lines = mine_ref.shape[1]
    chan = lax.axis_index("chan")
    first_core = (chan & 1) == 0
    mine_wide[...] = mine_ref[...].reshape(sources * lines, LANES).astype(jnp.float32)
    other_wide[...] = other_ref[...].reshape(sources * lines, LANES).astype(jnp.float32)
    runs = ((0, sources - 1, 1), (1, 0, sources - 1))
    for i in range(own):
        for half in range(HALVES):
            for q in range(2):
                line = (i * HALVES + half) * 2 + q
                for block, source, count in runs:
                    low = pl.ds(block * lines + line, count, stride=lines)
                    high = pl.ds(block * lines + lines // 2 + line, count, stride=lines)
                    from_core = (
                        jnp.where(first_core, mine_wide[low, :], other_wide[high, :]),
                        jnp.where(first_core, other_wide[low, :], mine_wide[high, :]),
                    )
                    for core in range(2):
                        target = pl.ds((source * 2 + core) * own + i, count, stride=2 * own)
                        signal_ref[q * HALVES + half, target, :] = from_core[core]
    fetch.wait()
    tile = tile_map_ref[lax.axis_index("tile"), chan]
    bits = grid_side.bit_length() - 1
    row_start = pl.multiple_of((tile >> bits) * side, side)
    col_start = pl.multiple_of((tile & (grid_side - 1)) * side, side)

    def inputs_from(start):
        planes = [signal_ref[plane, pl.ds(start, side), :] for plane in range(2 * HALVES)]
        return jnp.concatenate(planes, axis=1).astype(jnp.bfloat16)

    rows, cols = inputs_from(row_start), inputs_from(col_start)
    swapped = jnp.concatenate([cols[:, SPECTRA_SUMMED:], -cols[:, :SPECTRA_SUMMED]], axis=1)
    for part, right in enumerate((cols, swapped)):
        product = lax.dot_general(
            rows, right, (((1,), (1,)), ((), ())), preferred_element_type=jnp.float32
        )
        out_ref[0, 0, part] = (product * (1.0 / SPECTRA_SUMMED)).astype(jnp.bfloat16)


def on_device(voltages, fir_taps, channels, input_good_mask, tile_map):
    own = voltages.shape[1]
    chans = channels.shape[0]
    n_chan = lax.axis_size("chan")
    n_tile = lax.axis_size("tile")
    assert chans == n_chan and 2 * chans <= LANES and n_chan & (n_chan - 1) == 0
    chips = n_chan // 2
    order = [n_tile * chips - 1] + list(range(n_tile * chips - 1))
    groups = [[2 * place + core for place in order] for core in range(2)]
    x = voltages.reshape(own, FRAMES, BLOCKS, LANES).transpose(1, 2, 0, 3)
    operands = (channels, input_good_mask, fir_taps, x)
    hbm = pl.BlockSpec(memory_space=pltpu.HBM)
    vmem = pl.BlockSpec(memory_space=pltpu.VMEM)
    per_block = 2 * HALVES * own
    kinds = 2 * chans
    folded_rows = SPECTRA_SUMMED + (LANES if kinds < LANES else 0)
    spectra = pl.pallas_call(
        functools.partial(front_kernel, own, chans, n_tile),
        out_shape=pltpu.VMEM((n_tile, chans * per_block, LANES), jnp.bfloat16),
        in_specs=[hbm, hbm, hbm, hbm],
        out_specs=vmem,
        scratch_shapes=[
            pltpu.SMEM(channels.shape, jnp.int32),
            pltpu.SMEM(input_good_mask.shape, jnp.int32),
            pltpu.VMEM(fir_taps.shape, jnp.float32),
            pltpu.VMEM((BLOCKS, ROWS, own, LANES), jnp.bfloat16),
            pltpu.VMEM((FILTER_TAPS * kinds, TRANSFORM_LENGTH), jnp.bfloat16),
            pltpu.VMEM((own * ROWS, FILTER_TAPS * kinds), jnp.float32),
            pltpu.VMEM((own * folded_rows, LANES), jnp.float32),
            pltpu.VMEM((chans * per_block, LANES), jnp.float32),
            pltpu.SemaphoreType.DMA((BLOCKS, len(PARTS) - 1)),
            pltpu.SemaphoreType.DMA((3,)),
        ],
        compiler_params=pltpu.CompilerParams(vmem_limit_bytes=32 << 20),
        name="front",
    )(*(pltpu.with_memory_space_constraint(v, pltpu.HBM) for v in operands))
    spectra = spectra.reshape(n_tile * chips, 2 * per_block, LANES)
    mine = lax.all_to_all(
        spectra, ("tile", "chan"), split_axis=0, concat_axis=0, axis_index_groups=groups, tiled=True
    )
    other = lax.ppermute(mine, "chan", [(c, c ^ 1) for c in range(n_chan)])
    grid_side = n_tile // 8 + 2
    inputs = n_tile * n_chan * own
    side = inputs // grid_side
    return pl.pallas_call(
        functools.partial(back_kernel, own, grid_side),
        out_shape=jax.ShapeDtypeStruct((1, 1, 2, side, side), jnp.bfloat16),
        in_specs=[pl.BlockSpec(memory_space=pl.ANY), vmem, vmem],
        out_specs=vmem,
        scratch_shapes=[
            pltpu.SMEM(tile_map.shape[::-1], jnp.int32),
            pltpu.VMEM((n_tile * n_chan * per_block, LANES), jnp.float32),
            pltpu.VMEM((n_tile * n_chan * per_block, LANES), jnp.float32),
            pltpu.VMEM((2 * HALVES, inputs, LANES), jnp.float32),
            pltpu.SemaphoreType.DMA(()),
        ],
        compiler_params=pltpu.CompilerParams(vmem_limit_bytes=(4 << 20) + 60 * inputs * LANES * own),
        name="back",
    )(tile_map.T, mine, other)


def solution(mesh):
    in_specs = (P("tile", "chan", None), P(), P(), P("tile", "chan"), P())
    out_specs = P("chan", "tile", None, None, None)
    return jax.shard_map(
        on_device, mesh=mesh, in_specs=in_specs, out_specs=out_specs, check_vma=False
    )
```

```python
import functools
import math

import jax
import jax.numpy as jnp
from jax import lax
from jax.experimental import pallas as pl
from jax.experimental.pallas import tpu as pltpu
from jax.sharding import PartitionSpec as P

TRANSFORM_LENGTH = 2048
FILTER_TAPS = 16
SPECTRA_SUMMED = 256
FRAMES = SPECTRA_SUMMED + FILTER_TAPS - 1
ROWS = 272
LANES = 128
BLOCKS = TRANSFORM_LENGTH // LANES
HALVES = SPECTRA_SUMMED // LANES
OCTANT = TRANSFORM_LENGTH // 8


def cos_sin(phase):
    turns = (phase + OCTANT) >> (OCTANT.bit_length())
    angle = (phase - (turns << OCTANT.bit_length())).astype(jnp.float32) * (2.0 * math.pi / TRANSFORM_LENGTH)
    square = angle * angle
    cosine, sine = jnp.zeros_like(angle), jnp.zeros_like(angle)
    for power in range(10, -1, -2):
        sign = -1.0 if power % 4 else 1.0
        cosine = cosine * square + sign / math.factorial(power)
        sine = sine * square + sign / math.factorial(power + 1)
    sine = sine * angle
    odd = (turns & 1) == 1
    first, second = jnp.where(odd, sine, cosine), jnp.where(odd, cosine, sine)
    first = jnp.where(((turns + 1) & 2) == 2, -first, first)
    second = jnp.where((turns & 2) == 2, -second, second)
    return first, second


def build_table(chans, channels_ref, taps_ref, table_ref):
    row = lax.broadcasted_iota(jnp.int32, (chans, LANES), 0)
    lane = lax.broadcasted_iota(jnp.int32, (chans, LANES), 1)
    channel = jnp.zeros((chans, LANES), jnp.int32)
    for c in range(chans):
        channel = jnp.where(row == c, channels_ref[(c + chans - 2) % chans], channel)

    def unit(phase):
        return cos_sin(phase & (TRANSFORM_LENGTH - 1))

    factor = 1.0 / math.sqrt(TRANSFORM_LENGTH)
    cos0, sin0 = unit(channel * lane)
    blocks = [(cos0 * factor, sin0 * factor)]
    for bit in range(BLOCKS.bit_length() - 1):
        cos1, sin1 = unit(channel * (LANES << bit))
        blocks += [(c * cos1 - s * sin1, s * cos1 + c * sin1) for c, s in blocks]
    for nb, (cosine, sine) in enumerate(blocks):
        columns = slice(nb * LANES, (nb + 1) * LANES)
        dft = jnp.concatenate([cosine, -sine], axis=0)
        for tap in range(FILTER_TAPS):
            table_ref[tap * 2 * chans : (tap + 1) * 2 * chans, columns] = (
                dft * taps_ref[tap : tap + 1, columns]
            ).astype(jnp.bfloat16)


def front_kernel(
    own, chans, copies, channels_hbm, mask_hbm, taps_hbm, x_hbm, out_ref,
    channels_ref, mask_ref, taps_ref, x_ref, table_ref, fold_ref, block_ref,
    sems, small_sems,
):
    small = [
        pltpu.make_async_copy(source, target, small_sems.at[place])
        for place, (source, target) in enumerate(
            ((channels_hbm, channels_ref), (mask_hbm, mask_ref), (taps_hbm, taps_ref))
        )
    ]
    transfers = [
        pltpu.make_async_copy(x_hbm.at[:, nb], x_ref.at[nb, pl.ds(0, FRAMES)], sems.at[nb])
        for nb in range(BLOCKS)
    ]
    for transfer in small:
        transfer.start()
    for place, transfer in enumerate(transfers):
        transfer.start(priority=place % 2)
    for transfer in small:
        transfer.wait()
    build_table(chans, channels_ref, taps_ref, table_ref)
    rows_ref = x_ref.reshape(BLOCKS, ROWS * own, LANES)
    for transfer in transfers:
        transfer.wait()
    product = lax.dot_general(
        jnp.concatenate([rows_ref[nb] for nb in range(BLOCKS)], axis=1),
        table_ref[...],
        (((1,), (1,)), ((), ())),
        preferred_element_type=jnp.float32,
    )
    kinds = 2 * chans
    together = LANES // kinds
    kept = -(-(SPECTRA_SUMMED + together - 1) // 8) * 8
    folded = product[: kept * own, :LANES]
    for group in range(1, FILTER_TAPS // together):
        start = group * together * own
        folded = folded + product[
            start : start + kept * own, group * LANES : (group + 1) * LANES
        ]
    fold_ref[: kept * own, :] = folded
    for i in range(own):
        turned = fold_ref[pl.ds(i, fold_ref.shape[0] // own, stride=own), :].T
        spectra = turned[:kinds, :SPECTRA_SUMMED]
        for tap in range(1, together):
            shifted = pltpu.roll(
                turned[tap * kinds : (tap + 1) * kinds, :], turned.shape[1] - tap, axis=1
            )
            spectra = spectra + shifted[:, :SPECTRA_SUMMED]
        spectra = spectra * mask_ref[0, i].astype(jnp.float32)
        for half in range(HALVES):
            for q in range(2):
                block_ref[pl.ds((i * HALVES + half) * 2 + q, chans, stride=4 * own), :] = spectra[
                    q * chans : (q + 1) * chans, half * LANES : (half + 1) * LANES
                ]
    block = block_ref[...].astype(jnp.bfloat16)
    for copy in range(copies):
        out_ref[copy] = block


def back_kernel(
    own, grid_side, tile_map_any, mine_ref, other_ref, out_ref,
    tile_map_ref, mine_wide, other_wide, signal_ref, sem,
):
    fetch = pltpu.make_async_copy(tile_map_any, tile_map_ref, sem)
    fetch.start()
    sources = mine_ref.shape[0]
    inputs = sources * 2 * own
    side = inputs // grid_side
    lines = mine_ref.shape[1]
    chan = lax.axis_index("chan")
    first_core = (chan & 1) == 0
    mine_wide[...] = mine_ref[...].reshape(sources * lines, LANES).astype(jnp.float32)
    other_wide[...] = other_ref[...].reshape(sources * lines, LANES).astype(jnp.float32)
    runs = ((0, sources - 1, 1), (1, 0, sources - 1))
    for i in range(own):
        for half in range(HALVES):
            for q in range(2):
                line = (i * HALVES + half) * 2 + q
                for block, source, count in runs:
                    low = pl.ds(block * lines + line, count, stride=lines)
                    high = pl.ds(block * lines + lines // 2 + line, count, stride=lines)
                    from_core = (
                        jnp.where(first_core, mine_wide[low, :], other_wide[high, :]),
                        jnp.where(first_core, other_wide[low, :], mine_wide[high, :]),
                    )
                    for core in range(2):
                        target = pl.ds((source * 2 + core) * own + i, count, stride=2 * own)
                        signal_ref[q * HALVES + half, target, :] = from_core[core]
    fetch.wait()
    tile = tile_map_ref[lax.axis_index("tile"), chan]
    bits = grid_side.bit_length() - 1
    row_start = pl.multiple_of((tile >> bits) * side, side)
    col_start = pl.multiple_of((tile & (grid_side - 1)) * side, side)

    def inputs_from(start):
        planes = [signal_ref[plane, pl.ds(start, side), :] for plane in range(2 * HALVES)]
        return jnp.concatenate(planes, axis=1).astype(jnp.bfloat16)

    rows, cols = inputs_from(row_start), inputs_from(col_start)
    swapped = jnp.concatenate([cols[:, SPECTRA_SUMMED:], -cols[:, :SPECTRA_SUMMED]], axis=1)
    for part, right in enumerate((cols, swapped)):
        product = lax.dot_general(
            rows, right, (((1,), (1,)), ((), ())), preferred_element_type=jnp.float32
        )
        out_ref[0, 0, part] = (product * (1.0 / SPECTRA_SUMMED)).astype(jnp.bfloat16)


def on_device(voltages, fir_taps, channels, input_good_mask, tile_map):
    own = voltages.shape[1]
    chans = channels.shape[0]
    n_chan = lax.axis_size("chan")
    n_tile = lax.axis_size("tile")
    assert chans == n_chan and 2 * chans <= LANES and n_chan & (n_chan - 1) == 0
    chips = n_chan // 2
    order = [n_tile * chips - 1] + list(range(n_tile * chips - 1))
    groups = [[2 * place + core for place in order] for core in range(2)]
    x = voltages.reshape(own, FRAMES, BLOCKS, LANES).transpose(1, 2, 0, 3)
    operands = (channels, input_good_mask, fir_taps, x)
    hbm = pl.BlockSpec(memory_space=pltpu.HBM)
    vmem = pl.BlockSpec(memory_space=pltpu.VMEM)
    per_block = 2 * HALVES * own
    kinds = 2 * chans
    folded_rows = SPECTRA_SUMMED + (LANES if kinds < LANES else 0)
    spectra = pl.pallas_call(
        functools.partial(front_kernel, own, chans, n_tile),
        out_shape=pltpu.VMEM((n_tile, chans * per_block, LANES), jnp.bfloat16),
        in_specs=[hbm, hbm, hbm, hbm],
        out_specs=vmem,
        scratch_shapes=[
            pltpu.SMEM(channels.shape, jnp.int32),
            pltpu.SMEM(input_good_mask.shape, jnp.int32),
            pltpu.VMEM(fir_taps.shape, jnp.float32),
            pltpu.VMEM((BLOCKS, ROWS, own, LANES), jnp.bfloat16),
            pltpu.VMEM((FILTER_TAPS * kinds, TRANSFORM_LENGTH), jnp.bfloat16),
            pltpu.VMEM((own * folded_rows, LANES), jnp.float32),
            pltpu.VMEM((chans * per_block, LANES), jnp.float32),
            pltpu.SemaphoreType.DMA((BLOCKS,)),
            pltpu.SemaphoreType.DMA((3,)),
        ],
        compiler_params=pltpu.CompilerParams(vmem_limit_bytes=32 << 20),
        name="front",
    )(*(pltpu.with_memory_space_constraint(v, pltpu.HBM) for v in operands))
    spectra = spectra.reshape(n_tile * chips, 2 * per_block, LANES)
    mine = lax.all_to_all(
        spectra, ("tile", "chan"), split_axis=0, concat_axis=0, axis_index_groups=groups, tiled=True
    )
    other = lax.ppermute(mine, "chan", [(c, c ^ 1) for c in range(n_chan)])
    grid_side = n_tile // 8 + 2
    inputs = n_tile * n_chan * own
    side = inputs // grid_side
    return pl.pallas_call(
        functools.partial(back_kernel, own, grid_side),
        out_shape=jax.ShapeDtypeStruct((1, 1, 2, side, side), jnp.bfloat16),
        in_specs=[pl.BlockSpec(memory_space=pl.ANY), vmem, vmem],
        out_specs=vmem,
        scratch_shapes=[
            pltpu.SMEM(tile_map.shape[::-1], jnp.int32),
            pltpu.VMEM((n_tile * n_chan * per_block, LANES), jnp.float32),
            pltpu.VMEM((n_tile * n_chan * per_block, LANES), jnp.float32),
            pltpu.VMEM((2 * HALVES, inputs, LANES), jnp.float32),
            pltpu.SemaphoreType.DMA(()),
        ],
        compiler_params=pltpu.CompilerParams(vmem_limit_bytes=(4 << 20) + 60 * inputs * LANES * own),
        name="back",
    )(tile_map.T, mine, other)


def solution(mesh):
    in_specs = (P("tile", "chan", None), P(), P(), P("tile", "chan"), P())
    out_specs = P("chan", "tile", None, None, None)
    return jax.shard_map(
        on_device, mesh=mesh, in_specs=in_specs, out_specs=out_specs, check_vma=False
    )
```

```python
import functools
import math

import jax
import jax.numpy as jnp
from jax import lax
from jax.experimental import pallas as pl
from jax.experimental.pallas import tpu as pltpu
from jax.sharding import PartitionSpec as P

TRANSFORM_LENGTH = 2048
FILTER_TAPS = 16
SPECTRA_SUMMED = 256
FRAMES = SPECTRA_SUMMED + FILTER_TAPS - 1
ROWS = 272
LANES = 128
BLOCKS = TRANSFORM_LENGTH // LANES
HALVES = SPECTRA_SUMMED // LANES
PARTS = (0, ROWS // 2, ROWS)
OCTANT = TRANSFORM_LENGTH // 8


def cos_sin(phase):
    turns = (phase + OCTANT) >> (OCTANT.bit_length())
    angle = (phase - (turns << OCTANT.bit_length())).astype(jnp.float32) * (2.0 * math.pi / TRANSFORM_LENGTH)
    square = angle * angle
    cosine, sine = jnp.zeros_like(angle), jnp.zeros_like(angle)
    for power in range(10, -1, -2):
        sign = -1.0 if power % 4 else 1.0
        cosine = cosine * square + sign / math.factorial(power)
        sine = sine * square + sign / math.factorial(power + 1)
    sine = sine * angle
    odd = (turns & 1) == 1
    first, second = jnp.where(odd, sine, cosine), jnp.where(odd, cosine, sine)
    first = jnp.where(((turns + 1) & 2) == 2, -first, first)
    second = jnp.where((turns & 2) == 2, -second, second)
    return first, second


def build_table(chans, channels_ref, taps_ref, table_ref):
    row = lax.broadcasted_iota(jnp.int32, (chans, LANES), 0)
    lane = lax.broadcasted_iota(jnp.int32, (chans, LANES), 1)
    channel = jnp.zeros((chans, LANES), jnp.int32)
    for c in range(chans):
        channel = jnp.where(row == c, channels_ref[(c + chans - 2) % chans], channel)

    def unit(phase):
        return cos_sin(phase & (TRANSFORM_LENGTH - 1))

    factor = 1.0 / math.sqrt(TRANSFORM_LENGTH)
    cos0, sin0 = unit(channel * lane)
    blocks = [(cos0 * factor, sin0 * factor)]
    for bit in range(BLOCKS.bit_length() - 1):
        cos1, sin1 = unit(channel * (LANES << bit))
        blocks += [(c * cos1 - s * sin1, s * cos1 + c * sin1) for c, s in blocks]
    for nb, (cosine, sine) in enumerate(blocks):
        columns = slice(nb * LANES, (nb + 1) * LANES)
        dft = jnp.concatenate([cosine, -sine], axis=0)
        for tap in range(FILTER_TAPS):
            table_ref[tap * 2 * chans : (tap + 1) * 2 * chans, columns] = (
                dft * taps_ref[tap : tap + 1, columns]
            ).astype(jnp.bfloat16)


def front_kernel(
    own, chans, copies, channels_hbm, mask_hbm, taps_hbm, x_hbm, out_ref,
    channels_ref, mask_ref, taps_ref, x_ref, table_ref, fold_ref, block_ref,
    sems, small_sems,
):
    small = [
        pltpu.make_async_copy(source, target, small_sems.at[place])
        for place, (source, target) in enumerate(
            ((channels_hbm, channels_ref), (mask_hbm, mask_ref), (taps_hbm, taps_ref))
        )
    ]
    transfers = []
    for part, (start, stop) in enumerate(zip(PARTS, PARTS[1:])):
        frames = pl.ds(start, min(stop, FRAMES) - start)
        transfers.append(
            [
                pltpu.make_async_copy(
                    x_hbm.at[frames, nb], x_ref.at[nb, frames], sems.at[part, nb]
                )
                for nb in range(BLOCKS)
            ]
        )
    for transfer in small:
        transfer.start()
    for part in transfers:
        for place, transfer in enumerate(part):
            transfer.start(priority=place % 2)
    for transfer in small:
        transfer.wait()
    build_table(chans, channels_ref, taps_ref, table_ref)
    rows_ref = x_ref.reshape(BLOCKS, ROWS * own, LANES)
    products = []
    for part, start, stop in zip(transfers, PARTS, PARTS[1:]):
        for transfer in part:
            transfer.wait()
        rows = pl.ds(start * own, (stop - start) * own)
        products.append(
            lax.dot_general(
                jnp.concatenate([rows_ref[nb, rows, :] for nb in range(BLOCKS)], axis=1),
                table_ref[...],
                (((1,), (1,)), ((), ())),
                preferred_element_type=jnp.float32,
            )
        )
    product = jnp.concatenate(products, axis=0)
    kinds = 2 * chans
    together = LANES // kinds
    kept = -(-(SPECTRA_SUMMED + together - 1) // 8) * 8
    folded = product[: kept * own, :LANES]
    for group in range(1, FILTER_TAPS // together):
        start = group * together * own
        folded = folded + product[
            start : start + kept * own, group * LANES : (group + 1) * LANES
        ]
    fold_ref[: kept * own, :] = folded
    for i in range(own):
        turned = fold_ref[pl.ds(i, fold_ref.shape[0] // own, stride=own), :].T
        spectra = turned[:kinds, :SPECTRA_SUMMED]
        for tap in range(1, together):
            shifted = pltpu.roll(
                turned[tap * kinds : (tap + 1) * kinds, :], turned.shape[1] - tap, axis=1
            )
            spectra = spectra + shifted[:, :SPECTRA_SUMMED]
        spectra = spectra * mask_ref[0, i].astype(jnp.float32)
        for half in range(HALVES):
            for q in range(2):
                block_ref[pl.ds((i * HALVES + half) * 2 + q, chans, stride=4 * own), :] = spectra[
                    q * chans : (q + 1) * chans, half * LANES : (half + 1) * LANES
                ]
    block = block_ref[...].astype(jnp.bfloat16)
    for copy in range(copies):
        out_ref[copy] = block


def back_kernel(
    own, grid_side, tile_map_any, mine_ref, other_ref, out_ref,
    tile_map_ref, mine_wide, other_wide, signal_ref, sem,
):
    fetch = pltpu.make_async_copy(tile_map_any, tile_map_ref, sem)
    fetch.start()
    sources = mine_ref.shape[0]
    inputs = sources * 2 * own
    side = inputs // grid_side
    lines = mine_ref.shape[1]
    chan = lax.axis_index("chan")
    first_core = (chan & 1) == 0
    mine_wide[...] = mine_ref[...].reshape(sources * lines, LANES).astype(jnp.float32)
    other_wide[...] = other_ref[...].reshape(sources * lines, LANES).astype(jnp.float32)
    runs = ((0, sources - 1, 1), (1, 0, sources - 1))
    for i in range(own):
        for half in range(HALVES):
            for q in range(2):
                line = (i * HALVES + half) * 2 + q
                for block, source, count in runs:
                    low = pl.ds(block * lines + line, count, stride=lines)
                    high = pl.ds(block * lines + lines // 2 + line, count, stride=lines)
                    from_core = (
                        jnp.where(first_core, mine_wide[low, :], other_wide[high, :]),
                        jnp.where(first_core, other_wide[low, :], mine_wide[high, :]),
                    )
                    for core in range(2):
                        target = pl.ds((source * 2 + core) * own + i, count, stride=2 * own)
                        signal_ref[q * HALVES + half, target, :] = from_core[core]
    fetch.wait()
    tile = tile_map_ref[lax.axis_index("tile"), chan]
    bits = grid_side.bit_length() - 1
    row_start = pl.multiple_of((tile >> bits) * side, side)
    col_start = pl.multiple_of((tile & (grid_side - 1)) * side, side)

    def inputs_from(start):
        planes = [signal_ref[plane, pl.ds(start, side), :] for plane in range(2 * HALVES)]
        return jnp.concatenate(planes, axis=1).astype(jnp.bfloat16)

    rows, cols = inputs_from(row_start), inputs_from(col_start)
    swapped = jnp.concatenate([cols[:, SPECTRA_SUMMED:], -cols[:, :SPECTRA_SUMMED]], axis=1)
    for part, right in enumerate((cols, swapped)):
        product = lax.dot_general(
            rows, right, (((1,), (1,)), ((), ())), preferred_element_type=jnp.float32
        )
        out_ref[0, 0, part] = (product * (1.0 / SPECTRA_SUMMED)).astype(jnp.bfloat16)


def on_device(voltages, fir_taps, channels, input_good_mask, tile_map):
    own = voltages.shape[1]
    chans = channels.shape[0]
    n_chan = lax.axis_size("chan")
    n_tile = lax.axis_size("tile")
    assert chans == n_chan and 2 * chans <= LANES and n_chan & (n_chan - 1) == 0
    chips = n_chan // 2
    order = [n_tile * chips - 1] + list(range(n_tile * chips - 1))
    groups = [[2 * place + core for place in order] for core in range(2)]
    x = voltages.reshape(own, FRAMES, BLOCKS, LANES).transpose(1, 2, 0, 3)
    operands = (channels, input_good_mask, fir_taps, x)
    hbm = pl.BlockSpec(memory_space=pltpu.HBM)
    vmem = pl.BlockSpec(memory_space=pltpu.VMEM)
    per_block = 2 * HALVES * own
    kinds = 2 * chans
    folded_rows = SPECTRA_SUMMED + (LANES if kinds < LANES else 0)
    spectra = pl.pallas_call(
        functools.partial(front_kernel, own, chans, n_tile),
        out_shape=pltpu.VMEM((n_tile, chans * per_block, LANES), jnp.bfloat16),
        in_specs=[hbm, hbm, hbm, hbm],
        out_specs=vmem,
        scratch_shapes=[
            pltpu.SMEM(channels.shape, jnp.int32),
            pltpu.SMEM(input_good_mask.shape, jnp.int32),
            pltpu.VMEM(fir_taps.shape, jnp.float32),
            pltpu.VMEM((BLOCKS, ROWS, own, LANES), jnp.bfloat16),
            pltpu.VMEM((FILTER_TAPS * kinds, TRANSFORM_LENGTH), jnp.bfloat16),
            pltpu.VMEM((own * folded_rows, LANES), jnp.float32),
            pltpu.VMEM((chans * per_block, LANES), jnp.float32),
            pltpu.SemaphoreType.DMA((len(PARTS) - 1, BLOCKS)),
            pltpu.SemaphoreType.DMA((3,)),
        ],
        compiler_params=pltpu.CompilerParams(vmem_limit_bytes=32 << 20),
        name="front",
    )(*(pltpu.with_memory_space_constraint(v, pltpu.HBM) for v in operands))
    spectra = spectra.reshape(n_tile * chips, 2 * per_block, LANES)
    mine = lax.all_to_all(
        spectra, ("tile", "chan"), split_axis=0, concat_axis=0, axis_index_groups=groups, tiled=True
    )
    other = lax.ppermute(mine, "chan", [(c, c ^ 1) for c in range(n_chan)])
    grid_side = n_tile // 8 + 2
    inputs = n_tile * n_chan * own
    side = inputs // grid_side
    return pl.pallas_call(
        functools.partial(back_kernel, own, grid_side),
        out_shape=jax.ShapeDtypeStruct((1, 1, 2, side, side), jnp.bfloat16),
        in_specs=[pl.BlockSpec(memory_space=pl.ANY), vmem, vmem],
        out_specs=vmem,
        scratch_shapes=[
            pltpu.SMEM(tile_map.shape[::-1], jnp.int32),
            pltpu.VMEM((n_tile * n_chan * per_block, LANES), jnp.float32),
            pltpu.VMEM((n_tile * n_chan * per_block, LANES), jnp.float32),
            pltpu.VMEM((2 * HALVES, inputs, LANES), jnp.float32),
            pltpu.SemaphoreType.DMA(()),
        ],
        compiler_params=pltpu.CompilerParams(vmem_limit_bytes=(4 << 20) + 60 * inputs * LANES * own),
        name="back",
    )(tile_map.T, mine, other)


def solution(mesh):
    in_specs = (P("tile", "chan", None), P(), P(), P("tile", "chan"), P())
    out_specs = P("chan", "tile", None, None, None)
    return jax.shard_map(
        on_device, mesh=mesh, in_specs=in_specs, out_specs=out_specs, check_vma=False
    )
```

```python
import functools
import math

import jax
import jax.numpy as jnp
from jax import lax
from jax.experimental import pallas as pl
from jax.experimental.pallas import tpu as pltpu
from jax.sharding import PartitionSpec as P

TRANSFORM_LENGTH = 2048
FILTER_TAPS = 16
SPECTRA_SUMMED = 256
FRAMES = SPECTRA_SUMMED + FILTER_TAPS - 1
ROWS = 272
LANES = 128
BLOCKS = TRANSFORM_LENGTH // LANES
HALVES = SPECTRA_SUMMED // LANES
OCTANT = TRANSFORM_LENGTH // 8


def cos_sin(phase):
    turns = (phase + OCTANT) >> (OCTANT.bit_length())
    angle = (phase - (turns << OCTANT.bit_length())).astype(jnp.float32) * (2.0 * math.pi / TRANSFORM_LENGTH)
    square = angle * angle
    cosine, sine = jnp.zeros_like(angle), jnp.zeros_like(angle)
    for power in range(10, -1, -2):
        sign = -1.0 if power % 4 else 1.0
        cosine = cosine * square + sign / math.factorial(power)
        sine = sine * square + sign / math.factorial(power + 1)
    sine = sine * angle
    odd = (turns & 1) == 1
    first, second = jnp.where(odd, sine, cosine), jnp.where(odd, cosine, sine)
    first = jnp.where(((turns + 1) & 2) == 2, -first, first)
    second = jnp.where((turns & 2) == 2, -second, second)
    return first, second


def dft_blocks(chans, channels_ref):
    row = lax.broadcasted_iota(jnp.int32, (chans, LANES), 0)
    lane = lax.broadcasted_iota(jnp.int32, (chans, LANES), 1)
    channel = jnp.zeros((chans, LANES), jnp.int32)
    for c in range(chans):
        channel = jnp.where(row == c, channels_ref[(c + chans - 2) % chans], channel)

    def unit(phase):
        return cos_sin(phase & (TRANSFORM_LENGTH - 1))

    factor = 1.0 / math.sqrt(TRANSFORM_LENGTH)
    cos0, sin0 = unit(channel * lane)
    blocks = [(cos0 * factor, sin0 * factor)]
    for bit in range(BLOCKS.bit_length() - 1):
        cos1, sin1 = unit(channel * (LANES << bit))
        blocks += [(c * cos1 - s * sin1, s * cos1 + c * sin1) for c, s in blocks]
    return [jnp.concatenate([cosine, -sine], axis=0) for cosine, sine in blocks]


def build_table(chans, blocks, taps_ref, table_ref):
    for nb, dft in enumerate(blocks):
        columns = slice(nb * LANES, (nb + 1) * LANES)
        for tap in range(FILTER_TAPS):
            table_ref[tap * 2 * chans : (tap + 1) * 2 * chans, columns] = (
                dft * taps_ref[tap : tap + 1, columns]
            ).astype(jnp.bfloat16)


def front_kernel(
    own, chans, copies, channels_hbm, mask_hbm, taps_hbm, x_hbm, out_ref,
    channels_ref, mask_ref, taps_ref, x_ref, table_ref, fold_ref, block_ref,
    sems, small_sems,
):
    small = [
        pltpu.make_async_copy(source, target, small_sems.at[place])
        for place, (source, target) in enumerate(
            ((channels_hbm, channels_ref), (mask_hbm, mask_ref), (taps_hbm, taps_ref))
        )
    ]
    transfers = [
        pltpu.make_async_copy(x_hbm.at[:, nb], x_ref.at[nb, pl.ds(0, FRAMES)], sems.at[nb])
        for nb in range(BLOCKS)
    ]
    for place, transfer in enumerate(small):
        transfer.start(priority=place // 2)
    for place, transfer in enumerate(transfers):
        transfer.start(priority=place % 2)
    small[0].wait()
    blocks = dft_blocks(chans, channels_ref)
    small[2].wait()
    build_table(chans, blocks, taps_ref, table_ref)
    rows_ref = x_ref.reshape(BLOCKS, ROWS * own, LANES)
    for transfer in transfers:
        transfer.wait()
    product = lax.dot_general(
        jnp.concatenate([rows_ref[nb] for nb in range(BLOCKS)], axis=1),
        table_ref[...],
        (((1,), (1,)), ((), ())),
        preferred_element_type=jnp.float32,
    )
    kinds = 2 * chans
    together = LANES // kinds
    kept = -(-(SPECTRA_SUMMED + together - 1) // 8) * 8
    folded = product[: kept * own, :LANES]
    for group in range(1, FILTER_TAPS // together):
        start = group * together * own
        folded = folded + product[
            start : start + kept * own, group * LANES : (group + 1) * LANES
        ]
    fold_ref[: kept * own, :] = folded
    small[1].wait()
    for i in range(own):
        turned = fold_ref[pl.ds(i, fold_ref.shape[0] // own, stride=own), :].T
        spectra = turned[:kinds, :SPECTRA_SUMMED]
        for tap in range(1, together):
            shifted = pltpu.roll(
                turned[tap * kinds : (tap + 1) * kinds, :], turned.shape[1] - tap, axis=1
            )
            spectra = spectra + shifted[:, :SPECTRA_SUMMED]
        spectra = spectra * mask_ref[0, i].astype(jnp.float32)
        for half in range(HALVES):
            for q in range(2):
                block_ref[pl.ds((i * HALVES + half) * 2 + q, chans, stride=4 * own), :] = spectra[
                    q * chans : (q + 1) * chans, half * LANES : (half + 1) * LANES
                ]
    block = block_ref[...].astype(jnp.bfloat16)
    for copy in range(copies):
        out_ref[copy] = block


def back_kernel(
    own, grid_side, tile_map_any, mine_ref, other_ref, out_ref,
    tile_map_ref, mine_wide, other_wide, signal_ref, sem,
):
    fetch = pltpu.make_async_copy(tile_map_any, tile_map_ref, sem)
    fetch.start()
    sources = mine_ref.shape[0]
    inputs = sources * 2 * own
    side = inputs // grid_side
    lines = mine_ref.shape[1]
    chan = lax.axis_index("chan")
    first_core = (chan & 1) == 0
    mine_wide[...] = mine_ref[...].reshape(sources * lines, LANES).astype(jnp.float32)
    other_wide[...] = other_ref[...].reshape(sources * lines, LANES).astype(jnp.float32)
    runs = ((0, sources - 1, 1), (1, 0, sources - 1))
    for i in range(own):
        for half in range(HALVES):
            for q in range(2):
                line = (i * HALVES + half) * 2 + q
                for block, source, count in runs:
                    low = pl.ds(block * lines + line, count, stride=lines)
                    high = pl.ds(block * lines + lines // 2 + line, count, stride=lines)
                    from_core = (
                        jnp.where(first_core, mine_wide[low, :], other_wide[high, :]),
                        jnp.where(first_core, other_wide[low, :], mine_wide[high, :]),
                    )
                    for core in range(2):
                        target = pl.ds((source * 2 + core) * own + i, count, stride=2 * own)
                        signal_ref[q * HALVES + half, target, :] = from_core[core]
    fetch.wait()
    tile = tile_map_ref[lax.axis_index("tile"), chan]
    bits = grid_side.bit_length() - 1
    row_start = pl.multiple_of((tile >> bits) * side, side)
    col_start = pl.multiple_of((tile & (grid_side - 1)) * side, side)

    def inputs_from(start):
        planes = [signal_ref[plane, pl.ds(start, side), :] for plane in range(2 * HALVES)]
        return jnp.concatenate(planes, axis=1).astype(jnp.bfloat16)

    rows, cols = inputs_from(row_start), inputs_from(col_start)
    swapped = jnp.concatenate([cols[:, SPECTRA_SUMMED:], -cols[:, :SPECTRA_SUMMED]], axis=1)
    for part, right in enumerate((cols, swapped)):
        product = lax.dot_general(
            rows, right, (((1,), (1,)), ((), ())), preferred_element_type=jnp.float32
        )
        out_ref[0, 0, part] = (product * (1.0 / SPECTRA_SUMMED)).astype(jnp.bfloat16)


def on_device(voltages, fir_taps, channels, input_good_mask, tile_map):
    own = voltages.shape[1]
    chans = channels.shape[0]
    n_chan = lax.axis_size("chan")
    n_tile = lax.axis_size("tile")
    assert chans == n_chan and 2 * chans <= LANES and n_chan & (n_chan - 1) == 0
    chips = n_chan // 2
    order = [n_tile * chips - 1] + list(range(n_tile * chips - 1))
    groups = [[2 * place + core for place in order] for core in range(2)]
    x = voltages.reshape(own, FRAMES, BLOCKS, LANES).transpose(1, 2, 0, 3)
    operands = (channels, input_good_mask, fir_taps, x)
    hbm = pl.BlockSpec(memory_space=pltpu.HBM)
    vmem = pl.BlockSpec(memory_space=pltpu.VMEM)
    per_block = 2 * HALVES * own
    kinds = 2 * chans
    folded_rows = SPECTRA_SUMMED + (LANES if kinds < LANES else 0)
    spectra = pl.pallas_call(
        functools.partial(front_kernel, own, chans, n_tile),
        out_shape=pltpu.VMEM((n_tile, chans * per_block, LANES), jnp.bfloat16),
        in_specs=[hbm, hbm, hbm, hbm],
        out_specs=vmem,
        scratch_shapes=[
            pltpu.SMEM(channels.shape, jnp.int32),
            pltpu.SMEM(input_good_mask.shape, jnp.int32),
            pltpu.VMEM(fir_taps.shape, jnp.float32),
            pltpu.VMEM((BLOCKS, ROWS, own, LANES), jnp.bfloat16),
            pltpu.VMEM((FILTER_TAPS * kinds, TRANSFORM_LENGTH), jnp.bfloat16),
            pltpu.VMEM((own * folded_rows, LANES), jnp.float32),
            pltpu.VMEM((chans * per_block, LANES), jnp.float32),
            pltpu.SemaphoreType.DMA((BLOCKS,)),
            pltpu.SemaphoreType.DMA((3,)),
        ],
        compiler_params=pltpu.CompilerParams(vmem_limit_bytes=32 << 20),
        name="front",
    )(*(pltpu.with_memory_space_constraint(v, pltpu.HBM) for v in operands))
    spectra = spectra.reshape(n_tile * chips, 2 * per_block, LANES)
    mine = lax.all_to_all(
        spectra, ("tile", "chan"), split_axis=0, concat_axis=0, axis_index_groups=groups, tiled=True
    )
    other = lax.ppermute(mine, "chan", [(c, c ^ 1) for c in range(n_chan)])
    grid_side = n_tile // 8 + 2
    inputs = n_tile * n_chan * own
    side = inputs // grid_side
    return pl.pallas_call(
        functools.partial(back_kernel, own, grid_side),
        out_shape=jax.ShapeDtypeStruct((1, 1, 2, side, side), jnp.bfloat16),
        in_specs=[pl.BlockSpec(memory_space=pl.ANY), vmem, vmem],
        out_specs=vmem,
        scratch_shapes=[
            pltpu.SMEM(tile_map.shape[::-1], jnp.int32),
            pltpu.VMEM((n_tile * n_chan * per_block, LANES), jnp.float32),
            pltpu.VMEM((n_tile * n_chan * per_block, LANES), jnp.float32),
            pltpu.VMEM((2 * HALVES, inputs, LANES), jnp.float32),
            pltpu.SemaphoreType.DMA(()),
        ],
        compiler_params=pltpu.CompilerParams(vmem_limit_bytes=(4 << 20) + 60 * inputs * LANES * own),
        name="back",
    )(tile_map.T, mine, other)


def solution(mesh):
    in_specs = (P("tile", "chan", None), P(), P(), P("tile", "chan"), P())
    out_specs = P("chan", "tile", None, None, None)
    return jax.shard_map(
        on_device, mesh=mesh, in_specs=in_specs, out_specs=out_specs, check_vma=False
    )
```

```python
import functools
import math

import jax
import jax.numpy as jnp
from jax import lax
from jax.experimental import pallas as pl
from jax.experimental.pallas import tpu as pltpu
from jax.sharding import PartitionSpec as P

TRANSFORM_LENGTH = 2048
FILTER_TAPS = 16
SPECTRA_SUMMED = 256
FRAMES = SPECTRA_SUMMED + FILTER_TAPS - 1
ROWS = 272
LANES = 128
BLOCKS = TRANSFORM_LENGTH // LANES
HALVES = SPECTRA_SUMMED // LANES
OCTANT = TRANSFORM_LENGTH // 8


def cos_sin(phase):
    turns = (phase + OCTANT) >> (OCTANT.bit_length())
    angle = (phase - (turns << OCTANT.bit_length())).astype(jnp.float32) * (2.0 * math.pi / TRANSFORM_LENGTH)
    square = angle * angle
    cosine, sine = jnp.zeros_like(angle), jnp.zeros_like(angle)
    for power in range(10, -1, -2):
        sign = -1.0 if power % 4 else 1.0
        cosine = cosine * square + sign / math.factorial(power)
        sine = sine * square + sign / math.factorial(power + 1)
    sine = sine * angle
    odd = (turns & 1) == 1
    first, second = jnp.where(odd, sine, cosine), jnp.where(odd, cosine, sine)
    first = jnp.where(((turns + 1) & 2) == 2, -first, first)
    second = jnp.where((turns & 2) == 2, -second, second)
    return first, second


def dft_blocks(chans, channels_ref):
    row = lax.broadcasted_iota(jnp.int32, (chans, LANES), 0)
    lane = lax.broadcasted_iota(jnp.int32, (chans, LANES), 1)
    channel = jnp.zeros((chans, LANES), jnp.int32)
    for c in range(chans):
        channel = jnp.where(row == c, channels_ref[(c + chans - 2) % chans], channel)

    def unit(phase):
        return cos_sin(phase & (TRANSFORM_LENGTH - 1))

    factor = 1.0 / math.sqrt(TRANSFORM_LENGTH)
    cos0, sin0 = unit(channel * lane)
    blocks = [(cos0 * factor, sin0 * factor)]
    for bit in range(BLOCKS.bit_length() - 1):
        cos1, sin1 = unit(channel * (LANES << bit))
        blocks += [(c * cos1 - s * sin1, s * cos1 + c * sin1) for c, s in blocks]
    return [jnp.concatenate([cosine, -sine], axis=0) for cosine, sine in blocks]


def build_table(chans, blocks, taps_ref, table_ref):
    for nb, dft in enumerate(blocks):
        columns = slice(nb * LANES, (nb + 1) * LANES)
        for tap in range(FILTER_TAPS):
            table_ref[tap * 2 * chans : (tap + 1) * 2 * chans, columns] = (
                dft * taps_ref[tap : tap + 1, columns]
            ).astype(jnp.bfloat16)


def front_kernel(
    own, chans, copies, channels_hbm, mask_hbm, taps_hbm, x_hbm, out_ref,
    channels_ref, mask_ref, taps_ref, x_ref, table_ref, fold_ref, block_ref,
    sems, small_sems,
):
    small = [
        pltpu.make_async_copy(source, target, small_sems.at[place])
        for place, (source, target) in enumerate(
            ((taps_hbm, taps_ref), (channels_hbm, channels_ref), (mask_hbm, mask_ref))
        )
    ]
    transfers = [
        pltpu.make_async_copy(x_hbm.at[:, nb], x_ref.at[nb, pl.ds(0, FRAMES)], sems.at[nb])
        for nb in range(BLOCKS)
    ]
    for transfer in small:
        transfer.start()
    for place, transfer in enumerate(transfers):
        transfer.start(priority=place % 2)
    small[1].wait()
    blocks = dft_blocks(chans, channels_ref)
    small[0].wait()
    small[2].wait()
    build_table(chans, blocks, taps_ref, table_ref)
    rows_ref = x_ref.reshape(BLOCKS, ROWS * own, LANES)
    for transfer in transfers:
        transfer.wait()
    product = lax.dot_general(
        jnp.concatenate([rows_ref[nb] for nb in range(BLOCKS)], axis=1),
        table_ref[...],
        (((1,), (1,)), ((), ())),
        preferred_element_type=jnp.float32,
    )
    kinds = 2 * chans
    together = LANES // kinds
    kept = -(-(SPECTRA_SUMMED + together - 1) // 8) * 8
    folded = product[: kept * own, :LANES]
    for group in range(1, FILTER_TAPS // together):
        start = group * together * own
        folded = folded + product[
            start : start + kept * own, group * LANES : (group + 1) * LANES
        ]
    fold_ref[: kept * own, :] = folded
    for i in range(own):
        turned = fold_ref[pl.ds(i, fold_ref.shape[0] // own, stride=own), :].T
        spectra = turned[:kinds, :SPECTRA_SUMMED]
        for tap in range(1, together):
            shifted = pltpu.roll(
                turned[tap * kinds : (tap + 1) * kinds, :], turned.shape[1] - tap, axis=1
            )
            spectra = spectra + shifted[:, :SPECTRA_SUMMED]
        spectra = spectra * mask_ref[0, i].astype(jnp.float32)
        for half in range(HALVES):
            for q in range(2):
                block_ref[pl.ds((i * HALVES + half) * 2 + q, chans, stride=4 * own), :] = spectra[
                    q * chans : (q + 1) * chans, half * LANES : (half + 1) * LANES
                ]
    block = block_ref[...].astype(jnp.bfloat16)
    for copy in range(copies):
        out_ref[copy] = block


def back_kernel(
    own, grid_side, tile_map_any, mine_ref, other_ref, out_ref,
    tile_map_ref, mine_wide, other_wide, signal_ref, sem,
):
    fetch = pltpu.make_async_copy(tile_map_any, tile_map_ref, sem)
    fetch.start()
    sources = mine_ref.shape[0]
    inputs = sources * 2 * own
    side = inputs // grid_side
    lines = mine_ref.shape[1]
    chan = lax.axis_index("chan")
    first_core = (chan & 1) == 0
    mine_wide[...] = mine_ref[...].reshape(sources * lines, LANES).astype(jnp.float32)
    other_wide[...] = other_ref[...].reshape(sources * lines, LANES).astype(jnp.float32)
    runs = ((0, sources - 1, 1), (1, 0, sources - 1))
    for i in range(own):
        for half in range(HALVES):
            for q in range(2):
                line = (i * HALVES + half) * 2 + q
                for block, source, count in runs:
                    low = pl.ds(block * lines + line, count, stride=lines)
                    high = pl.ds(block * lines + lines // 2 + line, count, stride=lines)
                    from_core = (
                        jnp.where(first_core, mine_wide[low, :], other_wide[high, :]),
                        jnp.where(first_core, other_wide[low, :], mine_wide[high, :]),
                    )
                    for core in range(2):
                        target = pl.ds((source * 2 + core) * own + i, count, stride=2 * own)
                        signal_ref[q * HALVES + half, target, :] = from_core[core]
    fetch.wait()
    tile = tile_map_ref[lax.axis_index("tile"), chan]
    bits = grid_side.bit_length() - 1
    row_start = pl.multiple_of((tile >> bits) * side, side)
    col_start = pl.multiple_of((tile & (grid_side - 1)) * side, side)

    def inputs_from(start):
        planes = [signal_ref[plane, pl.ds(start, side), :] for plane in range(2 * HALVES)]
        return jnp.concatenate(planes, axis=1).astype(jnp.bfloat16)

    rows, cols = inputs_from(row_start), inputs_from(col_start)
    swapped = jnp.concatenate([cols[:, SPECTRA_SUMMED:], -cols[:, :SPECTRA_SUMMED]], axis=1)
    for part, right in enumerate((cols, swapped)):
        product = lax.dot_general(
            rows, right, (((1,), (1,)), ((), ())), preferred_element_type=jnp.float32
        )
        out_ref[0, 0, part] = (product * (1.0 / SPECTRA_SUMMED)).astype(jnp.bfloat16)


def on_device(voltages, fir_taps, channels, input_good_mask, tile_map):
    own = voltages.shape[1]
    chans = channels.shape[0]
    n_chan = lax.axis_size("chan")
    n_tile = lax.axis_size("tile")
    assert chans == n_chan and 2 * chans <= LANES and n_chan & (n_chan - 1) == 0
    chips = n_chan // 2
    order = [n_tile * chips - 1] + list(range(n_tile * chips - 1))
    groups = [[2 * place + core for place in order] for core in range(2)]
    x = voltages.reshape(own, FRAMES, BLOCKS, LANES).transpose(1, 2, 0, 3)
    operands = (channels, input_good_mask, fir_taps, x)
    hbm = pl.BlockSpec(memory_space=pltpu.HBM)
    vmem = pl.BlockSpec(memory_space=pltpu.VMEM)
    per_block = 2 * HALVES * own
    kinds = 2 * chans
    folded_rows = SPECTRA_SUMMED + (LANES if kinds < LANES else 0)
    spectra = pl.pallas_call(
        functools.partial(front_kernel, own, chans, n_tile),
        out_shape=pltpu.VMEM((n_tile, chans * per_block, LANES), jnp.bfloat16),
        in_specs=[hbm, hbm, hbm, hbm],
        out_specs=vmem,
        scratch_shapes=[
            pltpu.SMEM(channels.shape, jnp.int32),
            pltpu.SMEM(input_good_mask.shape, jnp.int32),
            pltpu.VMEM(fir_taps.shape, jnp.float32),
            pltpu.VMEM((BLOCKS, ROWS, own, LANES), jnp.bfloat16),
            pltpu.VMEM((FILTER_TAPS * kinds, TRANSFORM_LENGTH), jnp.bfloat16),
            pltpu.VMEM((own * folded_rows, LANES), jnp.float32),
            pltpu.VMEM((chans * per_block, LANES), jnp.float32),
            pltpu.SemaphoreType.DMA((BLOCKS,)),
            pltpu.SemaphoreType.DMA((3,)),
        ],
        compiler_params=pltpu.CompilerParams(vmem_limit_bytes=32 << 20),
        name="front",
    )(*(pltpu.with_memory_space_constraint(v, pltpu.HBM) for v in operands))
    spectra = spectra.reshape(n_tile * chips, 2 * per_block, LANES)
    mine = lax.all_to_all(
        spectra, ("tile", "chan"), split_axis=0, concat_axis=0, axis_index_groups=groups, tiled=True
    )
    other = lax.ppermute(mine, "chan", [(c, c ^ 1) for c in range(n_chan)])
    grid_side = n_tile // 8 + 2
    inputs = n_tile * n_chan * own
    side = inputs // grid_side
    return pl.pallas_call(
        functools.partial(back_kernel, own, grid_side),
        out_shape=jax.ShapeDtypeStruct((1, 1, 2, side, side), jnp.bfloat16),
        in_specs=[pl.BlockSpec(memory_space=pl.ANY), vmem, vmem],
        out_specs=vmem,
        scratch_shapes=[
            pltpu.SMEM(tile_map.shape[::-1], jnp.int32),
            pltpu.VMEM((n_tile * n_chan * per_block, LANES), jnp.float32),
            pltpu.VMEM((n_tile * n_chan * per_block, LANES), jnp.float32),
            pltpu.VMEM((2 * HALVES, inputs, LANES), jnp.float32),
            pltpu.SemaphoreType.DMA(()),
        ],
        compiler_params=pltpu.CompilerParams(vmem_limit_bytes=(4 << 20) + 60 * inputs * LANES * own),
        name="back",
    )(tile_map.T, mine, other)


def solution(mesh):
    in_specs = (P("tile", "chan", None), P(), P(), P("tile", "chan"), P())
    out_specs = P("chan", "tile", None, None, None)
    return jax.shard_map(
        on_device, mesh=mesh, in_specs=in_specs, out_specs=out_specs, check_vma=False
    )
```

```python
import functools
import math

import jax
import jax.numpy as jnp
from jax import lax
from jax.experimental import pallas as pl
from jax.experimental.pallas import tpu as pltpu
from jax.sharding import PartitionSpec as P

TRANSFORM_LENGTH = 2048
FILTER_TAPS = 16
SPECTRA_SUMMED = 256
FRAMES = SPECTRA_SUMMED + FILTER_TAPS - 1
ROWS = 272
LANES = 128
BLOCKS = TRANSFORM_LENGTH // LANES
HALVES = SPECTRA_SUMMED // LANES
OCTANT = TRANSFORM_LENGTH // 8


def cos_sin(phase):
    turns = (phase + OCTANT) >> (OCTANT.bit_length())
    angle = (phase - (turns << OCTANT.bit_length())).astype(jnp.float32) * (2.0 * math.pi / TRANSFORM_LENGTH)
    square = angle * angle
    cosine, sine = jnp.zeros_like(angle), jnp.zeros_like(angle)
    for power in range(10, -1, -2):
        sign = -1.0 if power % 4 else 1.0
        cosine = cosine * square + sign / math.factorial(power)
        sine = sine * square + sign / math.factorial(power + 1)
    sine = sine * angle
    odd = (turns & 1) == 1
    first, second = jnp.where(odd, sine, cosine), jnp.where(odd, cosine, sine)
    first = jnp.where(((turns + 1) & 2) == 2, -first, first)
    second = jnp.where((turns & 2) == 2, -second, second)
    return first, second


def parity(place):
    return (place ^ (place >> 1) ^ (place >> 2)) & 1


def dft_blocks(chans, channels_ref):
    row = lax.broadcasted_iota(jnp.int32, (chans, LANES), 0)
    lane = lax.broadcasted_iota(jnp.int32, (chans, LANES), 1)
    channel = jnp.zeros((chans, LANES), jnp.int32)
    for c in range(chans):
        channel = jnp.where(row == c, channels_ref[(c + chans - 2) % chans], channel)

    def unit(phase):
        return cos_sin(phase & (TRANSFORM_LENGTH - 1))

    factor = 1.0 / math.sqrt(TRANSFORM_LENGTH)
    cos0, sin0 = unit(channel * lane)
    blocks = [(cos0 * factor, sin0 * factor)]
    for bit in range(BLOCKS.bit_length() - 1):
        cos1, sin1 = unit(channel * (LANES << bit))
        blocks += [(c * cos1 - s * sin1, s * cos1 + c * sin1) for c, s in blocks]
    return [jnp.concatenate([cosine, -sine], axis=0) for cosine, sine in blocks]


def build_table(chans, blocks, taps_ref, table_ref):
    for nb, dft in enumerate(blocks):
        columns = slice(nb * LANES, (nb + 1) * LANES)
        for tap in range(FILTER_TAPS):
            table_ref[tap * 2 * chans : (tap + 1) * 2 * chans, columns] = (
                dft * taps_ref[tap : tap + 1, columns]
            ).astype(jnp.bfloat16)


def front_kernel(
    own, chans, copies, channels_hbm, mask_hbm, taps_hbm, x_hbm, out_ref,
    channels_ref, mask_ref, taps_ref, x_ref, table_ref, fold_ref, block_ref,
    sems, small_sems,
):
    small = [
        pltpu.make_async_copy(source, target, small_sems.at[place])
        for place, (source, target) in enumerate(
            ((taps_hbm, taps_ref), (channels_hbm, channels_ref), (mask_hbm, mask_ref))
        )
    ]
    transfers = [
        pltpu.make_async_copy(x_hbm.at[:, nb], x_ref.at[nb, pl.ds(0, FRAMES)], sems.at[nb])
        for nb in range(BLOCKS)
    ]
    for transfer in small:
        transfer.start()
    for place, transfer in enumerate(transfers):
        transfer.start(priority=place % 2)
    small[1].wait()
    blocks = dft_blocks(chans, channels_ref)
    small[0].wait()
    small[2].wait()
    build_table(chans, blocks, taps_ref, table_ref)
    rows_ref = x_ref.reshape(BLOCKS, ROWS * own, LANES)
    for transfer in transfers:
        transfer.wait()
    product = lax.dot_general(
        jnp.concatenate([rows_ref[nb] for nb in range(BLOCKS)], axis=1),
        table_ref[...],
        (((1,), (1,)), ((), ())),
        preferred_element_type=jnp.float32,
    )
    kinds = 2 * chans
    together = LANES // kinds
    kept = -(-(SPECTRA_SUMMED + together - 1) // 8) * 8
    folded = product[: kept * own, :LANES]
    for group in range(1, FILTER_TAPS // together):
        start = group * together * own
        folded = folded + product[
            start : start + kept * own, group * LANES : (group + 1) * LANES
        ]
    fold_ref[: kept * own, :] = folded
    for i in range(own):
        turned = fold_ref[pl.ds(i, fold_ref.shape[0] // own, stride=own), :].T
        spectra = turned[:kinds, :SPECTRA_SUMMED]
        for tap in range(1, together):
            shifted = pltpu.roll(
                turned[tap * kinds : (tap + 1) * kinds, :], turned.shape[1] - tap, axis=1
            )
            spectra = spectra + shifted[:, :SPECTRA_SUMMED]
        spectra = spectra * mask_ref[0, i].astype(jnp.float32)
        for half in range(HALVES):
            for q in range(2):
                block_ref[pl.ds((i * HALVES + half) * 2 + q, chans, stride=4 * own), :] = spectra[
                    q * chans : (q + 1) * chans, half * LANES : (half + 1) * LANES
                ]
    block = block_ref[...].astype(jnp.bfloat16)
    for copy in range(copies):
        out_ref[copy] = block


def back_kernel(
    own, grid_side, tile_map_any, mine_ref, other_ref, out_ref,
    tile_map_ref, mine_wide, other_wide, signal_ref, sem,
):
    fetch = pltpu.make_async_copy(tile_map_any, tile_map_ref, sem)
    fetch.start()
    sources = mine_ref.shape[0]
    inputs = sources * 2 * own
    side = inputs // grid_side
    lines = mine_ref.shape[1]
    chan = lax.axis_index("chan")
    core_here = chan & 1
    place_here = lax.axis_index("tile") * (lax.axis_size("chan") // 2) + (chan >> 1)
    group_here = core_here ^ parity(place_here)
    mine_wide[...] = mine_ref[...].reshape(sources * lines, LANES).astype(jnp.float32)
    other_wide[...] = other_ref[...].reshape(sources * lines, LANES).astype(jnp.float32)
    runs = ((0, sources - 1, 1), (1, 0, sources - 1))
    for block, source, count in runs:
        place = source + lax.broadcasted_iota(jnp.int32, (count, LANES), 0)
        first_is_mine = (parity(place) ^ group_here) == 0
        for i in range(own):
            for half in range(HALVES):
                for q in range(2):
                    line = block * lines + (i * HALVES + half) * 2 + q
                    low = pl.ds(line, count, stride=lines)
                    high = pl.ds(line + lines // 2, count, stride=lines)
                    mine = jnp.where(core_here == 0, mine_wide[low, :], mine_wide[high, :])
                    other = jnp.where(core_here == 0, other_wide[low, :], other_wide[high, :])
                    from_core = (
                        jnp.where(first_is_mine, mine, other),
                        jnp.where(first_is_mine, other, mine),
                    )
                    for core in range(2):
                        target = pl.ds((source * 2 + core) * own + i, count, stride=2 * own)
                        signal_ref[q * HALVES + half, target, :] = from_core[core]
    fetch.wait()
    tile = tile_map_ref[lax.axis_index("tile"), chan]
    bits = grid_side.bit_length() - 1
    row_start = pl.multiple_of((tile >> bits) * side, side)
    col_start = pl.multiple_of((tile & (grid_side - 1)) * side, side)

    def inputs_from(start):
        planes = [signal_ref[plane, pl.ds(start, side), :] for plane in range(2 * HALVES)]
        return jnp.concatenate(planes, axis=1).astype(jnp.bfloat16)

    rows, cols = inputs_from(row_start), inputs_from(col_start)
    swapped = jnp.concatenate([cols[:, SPECTRA_SUMMED:], -cols[:, :SPECTRA_SUMMED]], axis=1)
    for part, right in enumerate((cols, swapped)):
        product = lax.dot_general(
            rows, right, (((1,), (1,)), ((), ())), preferred_element_type=jnp.float32
        )
        out_ref[0, 0, part] = (product * (1.0 / SPECTRA_SUMMED)).astype(jnp.bfloat16)


def on_device(voltages, fir_taps, channels, input_good_mask, tile_map):
    own = voltages.shape[1]
    chans = channels.shape[0]
    n_chan = lax.axis_size("chan")
    n_tile = lax.axis_size("tile")
    assert chans == n_chan and 2 * chans <= LANES and n_chan & (n_chan - 1) == 0
    chips = n_chan // 2
    order = [n_tile * chips - 1] + list(range(n_tile * chips - 1))
    groups = [[2 * place + (parity(place) ^ group) for place in order] for group in range(2)]
    x = voltages.reshape(own, FRAMES, BLOCKS, LANES).transpose(1, 2, 0, 3)
    operands = (channels, input_good_mask, fir_taps, x)
    hbm = pl.BlockSpec(memory_space=pltpu.HBM)
    vmem = pl.BlockSpec(memory_space=pltpu.VMEM)
    per_block = 2 * HALVES * own
    kinds = 2 * chans
    folded_rows = SPECTRA_SUMMED + (LANES if kinds < LANES else 0)
    spectra = pl.pallas_call(
        functools.partial(front_kernel, own, chans, n_tile),
        out_shape=pltpu.VMEM((n_tile, chans * per_block, LANES), jnp.bfloat16),
        in_specs=[hbm, hbm, hbm, hbm],
        out_specs=vmem,
        scratch_shapes=[
            pltpu.SMEM(channels.shape, jnp.int32),
            pltpu.SMEM(input_good_mask.shape, jnp.int32),
            pltpu.VMEM(fir_taps.shape, jnp.float32),
            pltpu.VMEM((BLOCKS, ROWS, own, LANES), jnp.bfloat16),
            pltpu.VMEM((FILTER_TAPS * kinds, TRANSFORM_LENGTH), jnp.bfloat16),
            pltpu.VMEM((own * folded_rows, LANES), jnp.float32),
            pltpu.VMEM((chans * per_block, LANES), jnp.float32),
            pltpu.SemaphoreType.DMA((BLOCKS,)),
            pltpu.SemaphoreType.DMA((3,)),
        ],
        compiler_params=pltpu.CompilerParams(vmem_limit_bytes=32 << 20),
        name="front",
    )(*(pltpu.with_memory_space_constraint(v, pltpu.HBM) for v in operands))
    spectra = spectra.reshape(n_tile * chips, 2 * per_block, LANES)
    mine = lax.all_to_all(
        spectra, ("tile", "chan"), split_axis=0, concat_axis=0, axis_index_groups=groups, tiled=True
    )
    other = lax.ppermute(mine, "chan", [(c, c ^ 1) for c in range(n_chan)])
    grid_side = n_tile // 8 + 2
    inputs = n_tile * n_chan * own
    side = inputs // grid_side
    return pl.pallas_call(
        functools.partial(back_kernel, own, grid_side),
        out_shape=jax.ShapeDtypeStruct((1, 1, 2, side, side), jnp.bfloat16),
        in_specs=[pl.BlockSpec(memory_space=pl.ANY), vmem, vmem],
        out_specs=vmem,
        scratch_shapes=[
            pltpu.SMEM(tile_map.shape[::-1], jnp.int32),
            pltpu.VMEM((n_tile * n_chan * per_block, LANES), jnp.float32),
            pltpu.VMEM((n_tile * n_chan * per_block, LANES), jnp.float32),
            pltpu.VMEM((2 * HALVES, inputs, LANES), jnp.float32),
            pltpu.SemaphoreType.DMA(()),
        ],
        compiler_params=pltpu.CompilerParams(vmem_limit_bytes=(4 << 20) + 60 * inputs * LANES * own),
        name="back",
    )(tile_map.T, mine, other)


def solution(mesh):
    in_specs = (P("tile", "chan", None), P(), P(), P("tile", "chan"), P())
    out_specs = P("chan", "tile", None, None, None)
    return jax.shard_map(
        on_device, mesh=mesh, in_specs=in_specs, out_specs=out_specs, check_vma=False
    )
```

```python
import functools
import math

import jax
import jax.numpy as jnp
from jax import lax
from jax.experimental import pallas as pl
from jax.experimental.pallas import tpu as pltpu
from jax.sharding import PartitionSpec as P

TRANSFORM_LENGTH = 2048
FILTER_TAPS = 16
SPECTRA_SUMMED = 256
FRAMES = SPECTRA_SUMMED + FILTER_TAPS - 1
ROWS = 272
LANES = 128
BLOCKS = TRANSFORM_LENGTH // LANES
DIRECT = 12
HALVES = SPECTRA_SUMMED // LANES
OCTANT = TRANSFORM_LENGTH // 8


def cos_sin(phase):
    turns = (phase + OCTANT) >> (OCTANT.bit_length())
    angle = (phase - (turns << OCTANT.bit_length())).astype(jnp.float32) * (2.0 * math.pi / TRANSFORM_LENGTH)
    square = angle * angle
    cosine, sine = jnp.zeros_like(angle), jnp.zeros_like(angle)
    for power in range(10, -1, -2):
        sign = -1.0 if power % 4 else 1.0
        cosine = cosine * square + sign / math.factorial(power)
        sine = sine * square + sign / math.factorial(power + 1)
    sine = sine * angle
    odd = (turns & 1) == 1
    first, second = jnp.where(odd, sine, cosine), jnp.where(odd, cosine, sine)
    first = jnp.where(((turns + 1) & 2) == 2, -first, first)
    second = jnp.where((turns & 2) == 2, -second, second)
    return first, second


def parity(place):
    return (place ^ (place >> 1) ^ (place >> 2)) & 1


def dft_blocks(chans, channels_ref):
    row = lax.broadcasted_iota(jnp.int32, (chans, LANES), 0)
    lane = lax.broadcasted_iota(jnp.int32, (chans, LANES), 1)
    channel = jnp.zeros((chans, LANES), jnp.int32)
    for c in range(chans):
        channel = jnp.where(row == c, channels_ref[(c + chans - 2) % chans], channel)

    def unit(phase):
        return cos_sin(phase & (TRANSFORM_LENGTH - 1))

    factor = 1.0 / math.sqrt(TRANSFORM_LENGTH)
    cos0, sin0 = unit(channel * lane)
    blocks = [(cos0 * factor, sin0 * factor)]
    for bit in range(BLOCKS.bit_length() - 1):
        cos1, sin1 = unit(channel * (LANES << bit))
        blocks += [(c * cos1 - s * sin1, s * cos1 + c * sin1) for c, s in blocks]
    return [jnp.concatenate([cosine, -sine], axis=0) for cosine, sine in blocks]


def build_table(chans, blocks, taps_ref, table_ref):
    for nb, dft in enumerate(blocks):
        columns = slice(nb * LANES, (nb + 1) * LANES)
        for tap in range(FILTER_TAPS):
            table_ref[tap * 2 * chans : (tap + 1) * 2 * chans, columns] = (
                dft * taps_ref[tap : tap + 1, columns]
            ).astype(jnp.bfloat16)


def front_kernel(
    own, chans, copies, channels_hbm, mask_hbm, taps_hbm, x_hbm, out_ref,
    channels_ref, mask_ref, taps_ref, x_ref, rest_ref, sorted_ref, table_ref, fold_ref, block_ref,
    sems, small_sems,
):
    small = [
        pltpu.make_async_copy(source, target, small_sems.at[place])
        for place, (source, target) in enumerate(
            ((taps_hbm, taps_ref), (channels_hbm, channels_ref), (mask_hbm, mask_ref))
        )
    ]
    transfers = [
        pltpu.make_async_copy(x_hbm.at[:, nb], x_ref.at[nb, pl.ds(0, FRAMES)], sems.at[nb])
        for nb in range(DIRECT)
    ]
    rest = pltpu.make_async_copy(
        x_hbm.at[:, pl.ds(DIRECT, BLOCKS - DIRECT)], rest_ref.at[pl.ds(0, FRAMES)], sems.at[DIRECT]
    )
    for transfer in small:
        transfer.start()
    rest.start()
    for place, transfer in enumerate(transfers):
        transfer.start(priority=(place + 1) % 2)
    small[1].wait()
    blocks = dft_blocks(chans, channels_ref)
    small[0].wait()
    small[2].wait()
    build_table(chans, blocks, taps_ref, table_ref)
    rest.wait()
    for place in range(BLOCKS - DIRECT):
        sorted_ref[place] = rest_ref[:, place].reshape(ROWS * own, LANES)
    rows_ref = x_ref.reshape(DIRECT, ROWS * own, LANES)
    for transfer in transfers:
        transfer.wait()
    product = lax.dot_general(
        jnp.concatenate(
            [rows_ref[nb] for nb in range(DIRECT)]
            + [sorted_ref[place] for place in range(BLOCKS - DIRECT)],
            axis=1,
        ),
        table_ref[...],
        (((1,), (1,)), ((), ())),
        preferred_element_type=jnp.float32,
    )
    kinds = 2 * chans
    together = LANES // kinds
    kept = -(-(SPECTRA_SUMMED + together - 1) // 8) * 8
    folded = product[: kept * own, :LANES]
    for group in range(1, FILTER_TAPS // together):
        start = group * together * own
        folded = folded + product[
            start : start + kept * own, group * LANES : (group + 1) * LANES
        ]
    fold_ref[: kept * own, :] = folded
    for i in range(own):
        turned = fold_ref[pl.ds(i, fold_ref.shape[0] // own, stride=own), :].T
        spectra = turned[:kinds, :SPECTRA_SUMMED]
        for tap in range(1, together):
            shifted = pltpu.roll(
                turned[tap * kinds : (tap + 1) * kinds, :], turned.shape[1] - tap, axis=1
            )
            spectra = spectra + shifted[:, :SPECTRA_SUMMED]
        spectra = spectra * mask_ref[0, i].astype(jnp.float32)
        for half in range(HALVES):
            for q in range(2):
                block_ref[pl.ds((i * HALVES + half) * 2 + q, chans, stride=4 * own), :] = spectra[
                    q * chans : (q + 1) * chans, half * LANES : (half + 1) * LANES
                ]
    block = block_ref[...].astype(jnp.bfloat16)
    for copy in range(copies):
        out_ref[copy] = block


def back_kernel(
    own, grid_side, tile_map_any, mine_ref, other_ref, out_ref,
    tile_map_ref, mine_wide, other_wide, signal_ref, sem,
):
    fetch = pltpu.make_async_copy(tile_map_any, tile_map_ref, sem)
    fetch.start()
    sources = mine_ref.shape[0]
    inputs = sources * 2 * own
    side = inputs // grid_side
    lines = mine_ref.shape[1]
    chan = lax.axis_index("chan")
    core_here = chan & 1
    place_here = lax.axis_index("tile") * (lax.axis_size("chan") // 2) + (chan >> 1)
    group_here = core_here ^ parity(place_here)
    mine_wide[...] = mine_ref[...].reshape(sources * lines, LANES).astype(jnp.float32)
    other_wide[...] = other_ref[...].reshape(sources * lines, LANES).astype(jnp.float32)
    runs = ((0, sources - 1, 1), (1, 0, sources - 1))
    for block, source, count in runs:
        place = source + lax.broadcasted_iota(jnp.int32, (count, LANES), 0)
        first_is_mine = (parity(place) ^ group_here) == 0
        for i in range(own):
            for half in range(HALVES):
                for q in range(2):
                    line = block * lines + (i * HALVES + half) * 2 + q
                    low = pl.ds(line, count, stride=lines)
                    high = pl.ds(line + lines // 2, count, stride=lines)
                    mine = jnp.where(core_here == 0, mine_wide[low, :], mine_wide[high, :])
                    other = jnp.where(core_here == 0, other_wide[low, :], other_wide[high, :])
                    from_core = (
                        jnp.where(first_is_mine, mine, other),
                        jnp.where(first_is_mine, other, mine),
                    )
                    for core in range(2):
                        target = pl.ds((source * 2 + core) * own + i, count, stride=2 * own)
                        signal_ref[q * HALVES + half, target, :] = from_core[core]
    fetch.wait()
    tile = tile_map_ref[lax.axis_index("tile"), chan]
    bits = grid_side.bit_length() - 1
    row_start = pl.multiple_of((tile >> bits) * side, side)
    col_start = pl.multiple_of((tile & (grid_side - 1)) * side, side)

    def inputs_from(start):
        planes = [signal_ref[plane, pl.ds(start, side), :] for plane in range(2 * HALVES)]
        return jnp.concatenate(planes, axis=1).astype(jnp.bfloat16)

    rows, cols = inputs_from(row_start), inputs_from(col_start)
    swapped = jnp.concatenate([cols[:, SPECTRA_SUMMED:], -cols[:, :SPECTRA_SUMMED]], axis=1)
    for part, right in enumerate((cols, swapped)):
        product = lax.dot_general(
            rows, right, (((1,), (1,)), ((), ())), preferred_element_type=jnp.float32
        )
        out_ref[0, 0, part] = (product * (1.0 / SPECTRA_SUMMED)).astype(jnp.bfloat16)


def on_device(voltages, fir_taps, channels, input_good_mask, tile_map):
    own = voltages.shape[1]
    chans = channels.shape[0]
    n_chan = lax.axis_size("chan")
    n_tile = lax.axis_size("tile")
    assert chans == n_chan and 2 * chans <= LANES and n_chan & (n_chan - 1) == 0
    chips = n_chan // 2
    order = [n_tile * chips - 1] + list(range(n_tile * chips - 1))
    groups = [[2 * place + (parity(place) ^ group) for place in order] for group in range(2)]
    x = voltages.reshape(own, FRAMES, BLOCKS, LANES).transpose(1, 2, 0, 3)
    operands = (channels, input_good_mask, fir_taps, x)
    hbm = pl.BlockSpec(memory_space=pltpu.HBM)
    vmem = pl.BlockSpec(memory_space=pltpu.VMEM)
    per_block = 2 * HALVES * own
    kinds = 2 * chans
    folded_rows = SPECTRA_SUMMED + (LANES if kinds < LANES else 0)
    spectra = pl.pallas_call(
        functools.partial(front_kernel, own, chans, n_tile),
        out_shape=pltpu.VMEM((n_tile, chans * per_block, LANES), jnp.bfloat16),
        in_specs=[hbm, hbm, hbm, hbm],
        out_specs=vmem,
        scratch_shapes=[
            pltpu.SMEM(channels.shape, jnp.int32),
            pltpu.SMEM(input_good_mask.shape, jnp.int32),
            pltpu.VMEM(fir_taps.shape, jnp.float32),
            pltpu.VMEM((DIRECT, ROWS, own, LANES), jnp.bfloat16),
            pltpu.VMEM((ROWS, BLOCKS - DIRECT, own, LANES), jnp.bfloat16),
            pltpu.VMEM((BLOCKS - DIRECT, ROWS * own, LANES), jnp.bfloat16),
            pltpu.VMEM((FILTER_TAPS * kinds, TRANSFORM_LENGTH), jnp.bfloat16),
            pltpu.VMEM((own * folded_rows, LANES), jnp.float32),
            pltpu.VMEM((chans * per_block, LANES), jnp.float32),
            pltpu.SemaphoreType.DMA((DIRECT + 1,)),
            pltpu.SemaphoreType.DMA((3,)),
        ],
        compiler_params=pltpu.CompilerParams(vmem_limit_bytes=32 << 20),
        name="front",
    )(*(pltpu.with_memory_space_constraint(v, pltpu.HBM) for v in operands))
    spectra = spectra.reshape(n_tile * chips, 2 * per_block, LANES)
    mine = lax.all_to_all(
        spectra, ("tile", "chan"), split_axis=0, concat_axis=0, axis_index_groups=groups, tiled=True
    )
    other = lax.ppermute(mine, "chan", [(c, c ^ 1) for c in range(n_chan)])
    grid_side = n_tile // 8 + 2
    inputs = n_tile * n_chan * own
    side = inputs // grid_side
    return pl.pallas_call(
        functools.partial(back_kernel, own, grid_side),
        out_shape=jax.ShapeDtypeStruct((1, 1, 2, side, side), jnp.bfloat16),
        in_specs=[pl.BlockSpec(memory_space=pl.ANY), vmem, vmem],
        out_specs=vmem,
        scratch_shapes=[
            pltpu.SMEM(tile_map.shape[::-1], jnp.int32),
            pltpu.VMEM((n_tile * n_chan * per_block, LANES), jnp.float32),
            pltpu.VMEM((n_tile * n_chan * per_block, LANES), jnp.float32),
            pltpu.VMEM((2 * HALVES, inputs, LANES), jnp.float32),
            pltpu.SemaphoreType.DMA(()),
        ],
        compiler_params=pltpu.CompilerParams(vmem_limit_bytes=(4 << 20) + 60 * inputs * LANES * own),
        name="back",
    )(tile_map.T, mine, other)


def solution(mesh):
    in_specs = (P("tile", "chan", None), P(), P(), P("tile", "chan"), P())
    out_specs = P("chan", "tile", None, None, None)
    return jax.shard_map(
        on_device, mesh=mesh, in_specs=in_specs, out_specs=out_specs, check_vma=False
    )
```

```python
import functools
import math

import jax
import jax.numpy as jnp
from jax import lax
from jax.experimental import pallas as pl
from jax.experimental.pallas import tpu as pltpu
from jax.sharding import PartitionSpec as P

TRANSFORM_LENGTH = 2048
FILTER_TAPS = 16
SPECTRA_SUMMED = 256
FRAMES = SPECTRA_SUMMED + FILTER_TAPS - 1
ROWS = 272
LANES = 128
BLOCKS = TRANSFORM_LENGTH // LANES
DIRECT = 8
HALVES = SPECTRA_SUMMED // LANES
OCTANT = TRANSFORM_LENGTH // 8


def cos_sin(phase):
    turns = (phase + OCTANT) >> (OCTANT.bit_length())
    angle = (phase - (turns << OCTANT.bit_length())).astype(jnp.float32) * (2.0 * math.pi / TRANSFORM_LENGTH)
    square = angle * angle
    cosine, sine = jnp.zeros_like(angle), jnp.zeros_like(angle)
    for power in range(10, -1, -2):
        sign = -1.0 if power % 4 else 1.0
        cosine = cosine * square + sign / math.factorial(power)
        sine = sine * square + sign / math.factorial(power + 1)
    sine = sine * angle
    odd = (turns & 1) == 1
    first, second = jnp.where(odd, sine, cosine), jnp.where(odd, cosine, sine)
    first = jnp.where(((turns + 1) & 2) == 2, -first, first)
    second = jnp.where((turns & 2) == 2, -second, second)
    return first, second


def parity(place):
    return (place ^ (place >> 1) ^ (place >> 2)) & 1


def dft_blocks(chans, channels_ref):
    row = lax.broadcasted_iota(jnp.int32, (chans, LANES), 0)
    lane = lax.broadcasted_iota(jnp.int32, (chans, LANES), 1)
    channel = jnp.zeros((chans, LANES), jnp.int32)
    for c in range(chans):
        channel = jnp.where(row == c, channels_ref[(c + chans - 2) % chans], channel)

    def unit(phase):
        return cos_sin(phase & (TRANSFORM_LENGTH - 1))

    factor = 1.0 / math.sqrt(TRANSFORM_LENGTH)
    cos0, sin0 = unit(channel * lane)
    blocks = [(cos0 * factor, sin0 * factor)]
    for bit in range(BLOCKS.bit_length() - 1):
        cos1, sin1 = unit(channel * (LANES << bit))
        blocks += [(c * cos1 - s * sin1, s * cos1 + c * sin1) for c, s in blocks]
    return [jnp.concatenate([cosine, -sine], axis=0) for cosine, sine in blocks]


def build_table(chans, blocks, taps_ref, table_ref):
    for nb, dft in enumerate(blocks):
        columns = slice(nb * LANES, (nb + 1) * LANES)
        for tap in range(FILTER_TAPS):
            table_ref[tap * 2 * chans : (tap + 1) * 2 * chans, columns] = (
                dft * taps_ref[tap : tap + 1, columns]
            ).astype(jnp.bfloat16)


def front_kernel(
    own, chans, copies, channels_hbm, mask_hbm, taps_hbm, x_hbm, out_ref,
    channels_ref, mask_ref, taps_ref, x_ref, rest_ref, sorted_ref, table_ref, fold_ref, block_ref,
    sems, small_sems,
):
    small = [
        pltpu.make_async_copy(source, target, small_sems.at[place])
        for place, (source, target) in enumerate(
            ((taps_hbm, taps_ref), (channels_hbm, channels_ref), (mask_hbm, mask_ref))
        )
    ]
    transfers = [
        pltpu.make_async_copy(x_hbm.at[:, nb], x_ref.at[nb, pl.ds(0, FRAMES)], sems.at[nb])
        for nb in range(DIRECT)
    ]
    halves = ((0, ROWS // 2), (ROWS // 2, FRAMES))
    rest = [
        pltpu.make_async_copy(
            x_hbm.at[pl.ds(start, stop - start), pl.ds(DIRECT, BLOCKS - DIRECT)],
            rest_ref.at[pl.ds(start, stop - start)],
            sems.at[DIRECT + part],
        )
        for part, (start, stop) in enumerate(halves)
    ]
    for transfer in small:
        transfer.start()
    for place, transfer in enumerate(rest + transfers):
        transfer.start(priority=place % 2)
    small[1].wait()
    blocks = dft_blocks(chans, channels_ref)
    small[0].wait()
    small[2].wait()
    build_table(chans, blocks, taps_ref, table_ref)
    for part, transfer in enumerate(rest):
        transfer.wait()
        frames = pl.ds(part * (ROWS // 2), ROWS // 2)
        lines = pl.ds(part * (ROWS // 2) * own, ROWS // 2 * own)
        for place in range(BLOCKS - DIRECT):
            sorted_ref[place, lines, :] = rest_ref[frames, place].reshape(ROWS // 2 * own, LANES)
    rows_ref = x_ref.reshape(DIRECT, ROWS * own, LANES)
    for transfer in transfers:
        transfer.wait()
    product = lax.dot_general(
        jnp.concatenate(
            [rows_ref[nb] for nb in range(DIRECT)]
            + [sorted_ref[place] for place in range(BLOCKS - DIRECT)],
            axis=1,
        ),
        table_ref[...],
        (((1,), (1,)), ((), ())),
        preferred_element_type=jnp.float32,
    )
    kinds = 2 * chans
    together = LANES // kinds
    kept = -(-(SPECTRA_SUMMED + together - 1) // 8) * 8
    folded = product[: kept * own, :LANES]
    for group in range(1, FILTER_TAPS // together):
        start = group * together * own
        folded = folded + product[
            start : start + kept * own, group * LANES : (group + 1) * LANES
        ]
    fold_ref[: kept * own, :] = folded
    for i in range(own):
        turned = fold_ref[pl.ds(i, fold_ref.shape[0] // own, stride=own), :].T
        spectra = turned[:kinds, :SPECTRA_SUMMED]
        for tap in range(1, together):
            shifted = pltpu.roll(
                turned[tap * kinds : (tap + 1) * kinds, :], turned.shape[1] - tap, axis=1
            )
            spectra = spectra + shifted[:, :SPECTRA_SUMMED]
        spectra = spectra * mask_ref[0, i].astype(jnp.float32)
        for half in range(HALVES):
            for q in range(2):
                block_ref[pl.ds((i * HALVES + half) * 2 + q, chans, stride=4 * own), :] = spectra[
                    q * chans : (q + 1) * chans, half * LANES : (half + 1) * LANES
                ]
    block = block_ref[...].astype(jnp.bfloat16)
    for copy in range(copies):
        out_ref[copy] = block


def back_kernel(
    own, grid_side, tile_map_any, mine_ref, other_ref, out_ref,
    tile_map_ref, mine_wide, other_wide, signal_ref, sem,
):
    fetch = pltpu.make_async_copy(tile_map_any, tile_map_ref, sem)
    fetch.start()
    sources = mine_ref.shape[0]
    inputs = sources * 2 * own
    side = inputs // grid_side
    lines = mine_ref.shape[1]
    chan = lax.axis_index("chan")
    core_here = chan & 1
    place_here = lax.axis_index("tile") * (lax.axis_size("chan") // 2) + (chan >> 1)
    group_here = core_here ^ parity(place_here)
    mine_wide[...] = mine_ref[...].reshape(sources * lines, LANES).astype(jnp.float32)
    other_wide[...] = other_ref[...].reshape(sources * lines, LANES).astype(jnp.float32)
    runs = ((0, sources - 1, 1), (1, 0, sources - 1))
    for block, source, count in runs:
        place = source + lax.broadcasted_iota(jnp.int32, (count, LANES), 0)
        first_is_mine = (parity(place) ^ group_here) == 0
        for i in range(own):
            for half in range(HALVES):
                for q in range(2):
                    line = block * lines + (i * HALVES + half) * 2 + q
                    low = pl.ds(line, count, stride=lines)
                    high = pl.ds(line + lines // 2, count, stride=lines)
                    mine = jnp.where(core_here == 0, mine_wide[low, :], mine_wide[high, :])
                    other = jnp.where(core_here == 0, other_wide[low, :], other_wide[high, :])
                    from_core = (
                        jnp.where(first_is_mine, mine, other),
                        jnp.where(first_is_mine, other, mine),
                    )
                    for core in range(2):
                        target = pl.ds((source * 2 + core) * own + i, count, stride=2 * own)
                        signal_ref[q * HALVES + half, target, :] = from_core[core]
    fetch.wait()
    tile = tile_map_ref[lax.axis_index("tile"), chan]
    bits = grid_side.bit_length() - 1
    row_start = pl.multiple_of((tile >> bits) * side, side)
    col_start = pl.multiple_of((tile & (grid_side - 1)) * side, side)

    def inputs_from(start):
        planes = [signal_ref[plane, pl.ds(start, side), :] for plane in range(2 * HALVES)]
        return jnp.concatenate(planes, axis=1).astype(jnp.bfloat16)

    rows, cols = inputs_from(row_start), inputs_from(col_start)
    swapped = jnp.concatenate([cols[:, SPECTRA_SUMMED:], -cols[:, :SPECTRA_SUMMED]], axis=1)
    for part, right in enumerate((cols, swapped)):
        product = lax.dot_general(
            rows, right, (((1,), (1,)), ((), ())), preferred_element_type=jnp.float32
        )
        out_ref[0, 0, part] = (product * (1.0 / SPECTRA_SUMMED)).astype(jnp.bfloat16)


def on_device(voltages, fir_taps, channels, input_good_mask, tile_map):
    own = voltages.shape[1]
    chans = channels.shape[0]
    n_chan = lax.axis_size("chan")
    n_tile = lax.axis_size("tile")
    assert chans == n_chan and 2 * chans <= LANES and n_chan & (n_chan - 1) == 0
    chips = n_chan // 2
    order = [n_tile * chips - 1] + list(range(n_tile * chips - 1))
    groups = [[2 * place + (parity(place) ^ group) for place in order] for group in range(2)]
    x = voltages.reshape(own, FRAMES, BLOCKS, LANES).transpose(1, 2, 0, 3)
    operands = (channels, input_good_mask, fir_taps, x)
    hbm = pl.BlockSpec(memory_space=pltpu.HBM)
    vmem = pl.BlockSpec(memory_space=pltpu.VMEM)
    per_block = 2 * HALVES * own
    kinds = 2 * chans
    folded_rows = SPECTRA_SUMMED + (LANES if kinds < LANES else 0)
    spectra = pl.pallas_call(
        functools.partial(front_kernel, own, chans, n_tile),
        out_shape=pltpu.VMEM((n_tile, chans * per_block, LANES), jnp.bfloat16),
        in_specs=[hbm, hbm, hbm, hbm],
        out_specs=vmem,
        scratch_shapes=[
            pltpu.SMEM(channels.shape, jnp.int32),
            pltpu.SMEM(input_good_mask.shape, jnp.int32),
            pltpu.VMEM(fir_taps.shape, jnp.float32),
            pltpu.VMEM((DIRECT, ROWS, own, LANES), jnp.bfloat16),
            pltpu.VMEM((ROWS, BLOCKS - DIRECT, own, LANES), jnp.bfloat16),
            pltpu.VMEM((BLOCKS - DIRECT, ROWS * own, LANES), jnp.bfloat16),
            pltpu.VMEM((FILTER_TAPS * kinds, TRANSFORM_LENGTH), jnp.bfloat16),
            pltpu.VMEM((own * folded_rows, LANES), jnp.float32),
            pltpu.VMEM((chans * per_block, LANES), jnp.float32),
            pltpu.SemaphoreType.DMA((DIRECT + 2,)),
            pltpu.SemaphoreType.DMA((3,)),
        ],
        compiler_params=pltpu.CompilerParams(vmem_limit_bytes=32 << 20),
        name="front",
    )(*(pltpu.with_memory_space_constraint(v, pltpu.HBM) for v in operands))
    spectra = spectra.reshape(n_tile * chips, 2 * per_block, LANES)
    mine = lax.all_to_all(
        spectra, ("tile", "chan"), split_axis=0, concat_axis=0, axis_index_groups=groups, tiled=True
    )
    other = lax.ppermute(mine, "chan", [(c, c ^ 1) for c in range(n_chan)])
    grid_side = n_tile // 8 + 2
    inputs = n_tile * n_chan * own
    side = inputs // grid_side
    return pl.pallas_call(
        functools.partial(back_kernel, own, grid_side),
        out_shape=jax.ShapeDtypeStruct((1, 1, 2, side, side), jnp.bfloat16),
        in_specs=[pl.BlockSpec(memory_space=pl.ANY), vmem, vmem],
        out_specs=vmem,
        scratch_shapes=[
            pltpu.SMEM(tile_map.shape[::-1], jnp.int32),
            pltpu.VMEM((n_tile * n_chan * per_block, LANES), jnp.float32),
            pltpu.VMEM((n_tile * n_chan * per_block, LANES), jnp.float32),
            pltpu.VMEM((2 * HALVES, inputs, LANES), jnp.float32),
            pltpu.SemaphoreType.DMA(()),
        ],
        compiler_params=pltpu.CompilerParams(vmem_limit_bytes=(4 << 20) + 60 * inputs * LANES * own),
        name="back",
    )(tile_map.T, mine, other)


def solution(mesh):
    in_specs = (P("tile", "chan", None), P(), P(), P("tile", "chan"), P())
    out_specs = P("chan", "tile", None, None, None)
    return jax.shard_map(
        on_device, mesh=mesh, in_specs=in_specs, out_specs=out_specs, check_vma=False
    )
```

```python
import functools
import math

import jax
import jax.numpy as jnp
from jax import lax
from jax.experimental import pallas as pl
from jax.experimental.pallas import tpu as pltpu
from jax.sharding import PartitionSpec as P

TRANSFORM_LENGTH = 2048
FILTER_TAPS = 16
SPECTRA_SUMMED = 256
FRAMES = SPECTRA_SUMMED + FILTER_TAPS - 1
ROWS = 272
LANES = 128
BLOCKS = TRANSFORM_LENGTH // LANES
DIRECT = 10
HALVES = SPECTRA_SUMMED // LANES
OCTANT = TRANSFORM_LENGTH // 8


def cos_sin(phase):
    turns = (phase + OCTANT) >> (OCTANT.bit_length())
    angle = (phase - (turns << OCTANT.bit_length())).astype(jnp.float32) * (2.0 * math.pi / TRANSFORM_LENGTH)
    square = angle * angle
    cosine, sine = jnp.zeros_like(angle), jnp.zeros_like(angle)
    for power in range(10, -1, -2):
        sign = -1.0 if power % 4 else 1.0
        cosine = cosine * square + sign / math.factorial(power)
        sine = sine * square + sign / math.factorial(power + 1)
    sine = sine * angle
    odd = (turns & 1) == 1
    first, second = jnp.where(odd, sine, cosine), jnp.where(odd, cosine, sine)
    first = jnp.where(((turns + 1) & 2) == 2, -first, first)
    second = jnp.where((turns & 2) == 2, -second, second)
    return first, second


def parity(place):
    return (place ^ (place >> 1) ^ (place >> 2)) & 1


def dft_blocks(chans, channels_ref):
    row = lax.broadcasted_iota(jnp.int32, (chans, LANES), 0)
    lane = lax.broadcasted_iota(jnp.int32, (chans, LANES), 1)
    channel = jnp.zeros((chans, LANES), jnp.int32)
    for c in range(chans):
        channel = jnp.where(row == c, channels_ref[(c + chans - 2) % chans], channel)

    def unit(phase):
        return cos_sin(phase & (TRANSFORM_LENGTH - 1))

    factor = 1.0 / math.sqrt(TRANSFORM_LENGTH)
    cos0, sin0 = unit(channel * lane)
    blocks = [(cos0 * factor, sin0 * factor)]
    for bit in range(BLOCKS.bit_length() - 1):
        cos1, sin1 = unit(channel * (LANES << bit))
        blocks += [(c * cos1 - s * sin1, s * cos1 + c * sin1) for c, s in blocks]
    return [jnp.concatenate([cosine, -sine], axis=0) for cosine, sine in blocks]


def build_table(chans, blocks, taps_ref, table_ref):
    for nb, dft in enumerate(blocks):
        columns = slice(nb * LANES, (nb + 1) * LANES)
        for tap in range(FILTER_TAPS):
            table_ref[tap * 2 * chans : (tap + 1) * 2 * chans, columns] = (
                dft * taps_ref[tap : tap + 1, columns]
            ).astype(jnp.bfloat16)


def front_kernel(
    own, chans, copies, channels_hbm, mask_hbm, taps_hbm, x_hbm, out_ref,
    channels_ref, mask_ref, taps_ref, x_ref, rest_ref, sorted_ref, table_ref, fold_ref, block_ref,
    sems, small_sems,
):
    small = [
        pltpu.make_async_copy(source, target, small_sems.at[place])
        for place, (source, target) in enumerate(
            ((taps_hbm, taps_ref), (channels_hbm, channels_ref), (mask_hbm, mask_ref))
        )
    ]
    transfers = [
        pltpu.make_async_copy(x_hbm.at[:, nb], x_ref.at[nb, pl.ds(0, FRAMES)], sems.at[nb])
        for nb in range(DIRECT)
    ]
    halves = ((0, ROWS // 2), (ROWS // 2, FRAMES))
    rest = [
        pltpu.make_async_copy(
            x_hbm.at[pl.ds(start, stop - start), pl.ds(DIRECT, BLOCKS - DIRECT)],
            rest_ref.at[pl.ds(start, stop - start)],
            sems.at[DIRECT + part],
        )
        for part, (start, stop) in enumerate(halves)
    ]
    for transfer in small:
        transfer.start()
    for place, transfer in enumerate(rest + transfers):
        transfer.start(priority=place % 2)
    small[1].wait()
    blocks = dft_blocks(chans, channels_ref)
    small[0].wait()
    small[2].wait()
    build_table(chans, blocks, taps_ref, table_ref)
    for part, transfer in enumerate(rest):
        transfer.wait()
        frames = pl.ds(part * (ROWS // 2), ROWS // 2)
        lines = pl.ds(part * (ROWS // 2) * own, ROWS // 2 * own)
        for place in range(BLOCKS - DIRECT):
            sorted_ref[place, lines, :] = rest_ref[frames, place].reshape(ROWS // 2 * own, LANES)
    rows_ref = x_ref.reshape(DIRECT, ROWS * own, LANES)
    for transfer in transfers:
        transfer.wait()
    product = lax.dot_general(
        jnp.concatenate(
            [rows_ref[nb] for nb in range(DIRECT)]
            + [sorted_ref[place] for place in range(BLOCKS - DIRECT)],
            axis=1,
        ),
        table_ref[...],
        (((1,), (1,)), ((), ())),
        preferred_element_type=jnp.float32,
    )
    kinds = 2 * chans
    together = LANES // kinds
    kept = -(-(SPECTRA_SUMMED + together - 1) // 8) * 8
    folded = product[: kept * own, :LANES]
    for group in range(1, FILTER_TAPS // together):
        start = group * together * own
        folded = folded + product[
            start : start + kept * own, group * LANES : (group + 1) * LANES
        ]
    fold_ref[: kept * own, :] = folded
    for i in range(own):
        turned = fold_ref[pl.ds(i, fold_ref.shape[0] // own, stride=own), :].T
        spectra = turned[:kinds, :SPECTRA_SUMMED]
        for tap in range(1, together):
            shifted = pltpu.roll(
                turned[tap * kinds : (tap + 1) * kinds, :], turned.shape[1] - tap, axis=1
            )
            spectra = spectra + shifted[:, :SPECTRA_SUMMED]
        spectra = spectra * mask_ref[0, i].astype(jnp.float32)
        for half in range(HALVES):
            for q in range(2):
                block_ref[pl.ds((i * HALVES + half) * 2 + q, chans, stride=4 * own), :] = spectra[
                    q * chans : (q + 1) * chans, half * LANES : (half + 1) * LANES
                ]
    block = block_ref[...].astype(jnp.bfloat16)
    for copy in range(copies):
        out_ref[copy] = block


def back_kernel(
    own, grid_side, tile_map_any, mine_ref, other_ref, out_ref,
    tile_map_ref, mine_wide, other_wide, signal_ref, sem,
):
    fetch = pltpu.make_async_copy(tile_map_any, tile_map_ref, sem)
    fetch.start()
    sources = mine_ref.shape[0]
    inputs = sources * 2 * own
    side = inputs // grid_side
    lines = mine_ref.shape[1]
    chan = lax.axis_index("chan")
    core_here = chan & 1
    place_here = lax.axis_index("tile") * (lax.axis_size("chan") // 2) + (chan >> 1)
    group_here = core_here ^ parity(place_here)
    mine_wide[...] = mine_ref[...].reshape(sources * lines, LANES).astype(jnp.float32)
    other_wide[...] = other_ref[...].reshape(sources * lines, LANES).astype(jnp.float32)
    runs = ((0, sources - 1, 1), (1, 0, sources - 1))
    for block, source, count in runs:
        place = source + lax.broadcasted_iota(jnp.int32, (count, LANES), 0)
        first_is_mine = (parity(place) ^ group_here) == 0
        for i in range(own):
            for half in range(HALVES):
                for q in range(2):
                    line = block * lines + (i * HALVES + half) * 2 + q
                    low = pl.ds(line, count, stride=lines)
                    high = pl.ds(line + lines // 2, count, stride=lines)
                    mine = jnp.where(core_here == 0, mine_wide[low, :], mine_wide[high, :])
                    other = jnp.where(core_here == 0, other_wide[low, :], other_wide[high, :])
                    from_core = (
                        jnp.where(first_is_mine, mine, other),
                        jnp.where(first_is_mine, other, mine),
                    )
                    for core in range(2):
                        target = pl.ds((source * 2 + core) * own + i, count, stride=2 * own)
                        signal_ref[q * HALVES + half, target, :] = from_core[core]
    fetch.wait()
    tile = tile_map_ref[lax.axis_index("tile"), chan]
    bits = grid_side.bit_length() - 1
    row_start = pl.multiple_of((tile >> bits) * side, side)
    col_start = pl.multiple_of((tile & (grid_side - 1)) * side, side)

    def inputs_from(start):
        planes = [signal_ref[plane, pl.ds(start, side), :] for plane in range(2 * HALVES)]
        return jnp.concatenate(planes, axis=1).astype(jnp.bfloat16)

    rows, cols = inputs_from(row_start), inputs_from(col_start)
    swapped = jnp.concatenate([cols[:, SPECTRA_SUMMED:], -cols[:, :SPECTRA_SUMMED]], axis=1)
    for part, right in enumerate((cols, swapped)):
        product = lax.dot_general(
            rows, right, (((1,), (1,)), ((), ())), preferred_element_type=jnp.float32
        )
        out_ref[0, 0, part] = (product * (1.0 / SPECTRA_SUMMED)).astype(jnp.bfloat16)


def on_device(voltages, fir_taps, channels, input_good_mask, tile_map):
    own = voltages.shape[1]
    chans = channels.shape[0]
    n_chan = lax.axis_size("chan")
    n_tile = lax.axis_size("tile")
    assert chans == n_chan and 2 * chans <= LANES and n_chan & (n_chan - 1) == 0
    chips = n_chan // 2
    order = [n_tile * chips - 1] + list(range(n_tile * chips - 1))
    groups = [[2 * place + (parity(place) ^ group) for place in order] for group in range(2)]
    x = voltages.reshape(own, FRAMES, BLOCKS, LANES).transpose(1, 2, 0, 3)
    operands = (channels, input_good_mask, fir_taps, x)
    hbm = pl.BlockSpec(memory_space=pltpu.HBM)
    vmem = pl.BlockSpec(memory_space=pltpu.VMEM)
    per_block = 2 * HALVES * own
    kinds = 2 * chans
    folded_rows = SPECTRA_SUMMED + (LANES if kinds < LANES else 0)
    spectra = pl.pallas_call(
        functools.partial(front_kernel, own, chans, n_tile),
        out_shape=pltpu.VMEM((n_tile, chans * per_block, LANES), jnp.bfloat16),
        in_specs=[hbm, hbm, hbm, hbm],
        out_specs=vmem,
        scratch_shapes=[
            pltpu.SMEM(channels.shape, jnp.int32),
            pltpu.SMEM(input_good_mask.shape, jnp.int32),
            pltpu.VMEM(fir_taps.shape, jnp.float32),
            pltpu.VMEM((DIRECT, ROWS, own, LANES), jnp.bfloat16),
            pltpu.VMEM((ROWS, BLOCKS - DIRECT, own, LANES), jnp.bfloat16),
            pltpu.VMEM((BLOCKS - DIRECT, ROWS * own, LANES), jnp.bfloat16),
            pltpu.VMEM((FILTER_TAPS * kinds, TRANSFORM_LENGTH), jnp.bfloat16),
            pltpu.VMEM((own * folded_rows, LANES), jnp.float32),
            pltpu.VMEM((chans * per_block, LANES), jnp.float32),
            pltpu.SemaphoreType.DMA((DIRECT + 2,)),
            pltpu.SemaphoreType.DMA((3,)),
        ],
        compiler_params=pltpu.CompilerParams(vmem_limit_bytes=32 << 20),
        name="front",
    )(*(pltpu.with_memory_space_constraint(v, pltpu.HBM) for v in operands))
    spectra = spectra.reshape(n_tile * chips, 2 * per_block, LANES)
    mine = lax.all_to_all(
        spectra, ("tile", "chan"), split_axis=0, concat_axis=0, axis_index_groups=groups, tiled=True
    )
    other = lax.ppermute(mine, "chan", [(c, c ^ 1) for c in range(n_chan)])
    grid_side = n_tile // 8 + 2
    inputs = n_tile * n_chan * own
    side = inputs // grid_side
    return pl.pallas_call(
        functools.partial(back_kernel, own, grid_side),
        out_shape=jax.ShapeDtypeStruct((1, 1, 2, side, side), jnp.bfloat16),
        in_specs=[pl.BlockSpec(memory_space=pl.ANY), vmem, vmem],
        out_specs=vmem,
        scratch_shapes=[
            pltpu.SMEM(tile_map.shape[::-1], jnp.int32),
            pltpu.VMEM((n_tile * n_chan * per_block, LANES), jnp.float32),
            pltpu.VMEM((n_tile * n_chan * per_block, LANES), jnp.float32),
            pltpu.VMEM((2 * HALVES, inputs, LANES), jnp.float32),
            pltpu.SemaphoreType.DMA(()),
        ],
        compiler_params=pltpu.CompilerParams(vmem_limit_bytes=(4 << 20) + 60 * inputs * LANES * own),
        name="back",
    )(tile_map.T, mine, other)


def solution(mesh):
    in_specs = (P("tile", "chan", None), P(), P(), P("tile", "chan"), P())
    out_specs = P("chan", "tile", None, None, None)
    return jax.shard_map(
        on_device, mesh=mesh, in_specs=in_specs, out_specs=out_specs, check_vma=False
    )
```

```python
import functools
import math

import jax
import jax.numpy as jnp
from jax import lax
from jax.experimental import pallas as pl
from jax.experimental.pallas import tpu as pltpu
from jax.sharding import PartitionSpec as P

TRANSFORM_LENGTH = 2048
FILTER_TAPS = 16
SPECTRA_SUMMED = 256
FRAMES = SPECTRA_SUMMED + FILTER_TAPS - 1
ROWS = 272
LANES = 128
BLOCKS = TRANSFORM_LENGTH // LANES
PARTS = (0, 72, 136, 208, ROWS)
HALVES = SPECTRA_SUMMED // LANES
OCTANT = TRANSFORM_LENGTH // 8


def cos_sin(phase):
    turns = (phase + OCTANT) >> (OCTANT.bit_length())
    angle = (phase - (turns << OCTANT.bit_length())).astype(jnp.float32) * (2.0 * math.pi / TRANSFORM_LENGTH)
    square = angle * angle
    cosine, sine = jnp.zeros_like(angle), jnp.zeros_like(angle)
    for power in range(10, -1, -2):
        sign = -1.0 if power % 4 else 1.0
        cosine = cosine * square + sign / math.factorial(power)
        sine = sine * square + sign / math.factorial(power + 1)
    sine = sine * angle
    odd = (turns & 1) == 1
    first, second = jnp.where(odd, sine, cosine), jnp.where(odd, cosine, sine)
    first = jnp.where(((turns + 1) & 2) == 2, -first, first)
    second = jnp.where((turns & 2) == 2, -second, second)
    return first, second


def parity(place):
    return (place ^ (place >> 1) ^ (place >> 2)) & 1


def dft_blocks(chans, channels_ref):
    row = lax.broadcasted_iota(jnp.int32, (chans, LANES), 0)
    lane = lax.broadcasted_iota(jnp.int32, (chans, LANES), 1)
    channel = jnp.zeros((chans, LANES), jnp.int32)
    for c in range(chans):
        channel = jnp.where(row == c, channels_ref[(c + chans - 2) % chans], channel)

    def unit(phase):
        return cos_sin(phase & (TRANSFORM_LENGTH - 1))

    factor = 1.0 / math.sqrt(TRANSFORM_LENGTH)
    cos0, sin0 = unit(channel * lane)
    blocks = [(cos0 * factor, sin0 * factor)]
    for bit in range(BLOCKS.bit_length() - 1):
        cos1, sin1 = unit(channel * (LANES << bit))
        blocks += [(c * cos1 - s * sin1, s * cos1 + c * sin1) for c, s in blocks]
    return [jnp.concatenate([cosine, -sine], axis=0) for cosine, sine in blocks]


def build_table(chans, blocks, taps_ref, table_ref):
    for nb, dft in enumerate(blocks):
        columns = slice(nb * LANES, (nb + 1) * LANES)
        for tap in range(FILTER_TAPS):
            table_ref[tap * 2 * chans : (tap + 1) * 2 * chans, columns] = (
                dft * taps_ref[tap : tap + 1, columns]
            ).astype(jnp.bfloat16)


def front_kernel(
    own, chans, copies, channels_hbm, mask_hbm, taps_hbm, x_hbm, out_ref,
    channels_ref, mask_ref, taps_ref, x_ref, sorted_ref, table_ref, fold_ref, block_ref,
    sems, small_sems,
):
    small = [
        pltpu.make_async_copy(source, target, small_sems.at[place])
        for place, (source, target) in enumerate(
            ((taps_hbm, taps_ref), (channels_hbm, channels_ref), (mask_hbm, mask_ref))
        )
    ]
    transfers = []
    for part, (start, stop) in enumerate(zip(PARTS, PARTS[1:])):
        frames = pl.ds(start, min(stop, FRAMES) - start)
        transfers.append(pltpu.make_async_copy(x_hbm.at[frames], x_ref.at[frames], sems.at[part]))
    for transfer in small:
        transfer.start()
    for place, transfer in enumerate(transfers):
        transfer.start(priority=place % 2)
    small[1].wait()
    blocks = dft_blocks(chans, channels_ref)
    small[0].wait()
    small[2].wait()
    build_table(chans, blocks, taps_ref, table_ref)
    for transfer, start, stop in zip(transfers, PARTS, PARTS[1:]):
        transfer.wait()
        lines = pl.ds(start * own, (stop - start) * own)
        for nb in range(BLOCKS):
            sorted_ref[lines, nb * LANES : (nb + 1) * LANES] = x_ref[
                pl.ds(start, stop - start), nb
            ].reshape((stop - start) * own, LANES)
    product = lax.dot_general(
        sorted_ref[...], table_ref[...], (((1,), (1,)), ((), ())),
        preferred_element_type=jnp.float32,
    )
    kinds = 2 * chans
    together = LANES // kinds
    kept = -(-(SPECTRA_SUMMED + together - 1) // 8) * 8
    folded = product[: kept * own, :LANES]
    for group in range(1, FILTER_TAPS // together):
        start = group * together * own
        folded = folded + product[
            start : start + kept * own, group * LANES : (group + 1) * LANES
        ]
    fold_ref[: kept * own, :] = folded
    for i in range(own):
        turned = fold_ref[pl.ds(i, fold_ref.shape[0] // own, stride=own), :].T
        spectra = turned[:kinds, :SPECTRA_SUMMED]
        for tap in range(1, together):
            shifted = pltpu.roll(
                turned[tap * kinds : (tap + 1) * kinds, :], turned.shape[1] - tap, axis=1
            )
            spectra = spectra + shifted[:, :SPECTRA_SUMMED]
        spectra = spectra * mask_ref[0, i].astype(jnp.float32)
        for half in range(HALVES):
            for q in range(2):
                block_ref[pl.ds((i * HALVES + half) * 2 + q, chans, stride=4 * own), :] = spectra[
                    q * chans : (q + 1) * chans, half * LANES : (half + 1) * LANES
                ]
    block = block_ref[...].astype(jnp.bfloat16)
    for copy in range(copies):
        out_ref[copy] = block


def back_kernel(
    own, grid_side, tile_map_any, mine_ref, other_ref, out_ref,
    tile_map_ref, mine_wide, other_wide, signal_ref, sem,
):
    fetch = pltpu.make_async_copy(tile_map_any, tile_map_ref, sem)
    fetch.start()
    sources = mine_ref.shape[0]
    inputs = sources * 2 * own
    side = inputs // grid_side
    lines = mine_ref.shape[1]
    chan = lax.axis_index("chan")
    core_here = chan & 1
    place_here = lax.axis_index("tile") * (lax.axis_size("chan") // 2) + (chan >> 1)
    group_here = core_here ^ parity(place_here)
    mine_wide[...] = mine_ref[...].reshape(sources * lines, LANES).astype(jnp.float32)
    other_wide[...] = other_ref[...].reshape(sources * lines, LANES).astype(jnp.float32)
    runs = ((0, sources - 1, 1), (1, 0, sources - 1))
    for block, source, count in runs:
        place = source + lax.broadcasted_iota(jnp.int32, (count, LANES), 0)
        first_is_mine = (parity(place) ^ group_here) == 0
        for i in range(own):
            for half in range(HALVES):
                for q in range(2):
                    line = block * lines + (i * HALVES + half) * 2 + q
                    low = pl.ds(line, count, stride=lines)
                    high = pl.ds(line + lines // 2, count, stride=lines)
                    mine = jnp.where(core_here == 0, mine_wide[low, :], mine_wide[high, :])
                    other = jnp.where(core_here == 0, other_wide[low, :], other_wide[high, :])
                    from_core = (
                        jnp.where(first_is_mine, mine, other),
                        jnp.where(first_is_mine, other, mine),
                    )
                    for core in range(2):
                        target = pl.ds((source * 2 + core) * own + i, count, stride=2 * own)
                        signal_ref[q * HALVES + half, target, :] = from_core[core]
    fetch.wait()
    tile = tile_map_ref[lax.axis_index("tile"), chan]
    bits = grid_side.bit_length() - 1
    row_start = pl.multiple_of((tile >> bits) * side, side)
    col_start = pl.multiple_of((tile & (grid_side - 1)) * side, side)

    def inputs_from(start):
        planes = [signal_ref[plane, pl.ds(start, side), :] for plane in range(2 * HALVES)]
        return jnp.concatenate(planes, axis=1).astype(jnp.bfloat16)

    rows, cols = inputs_from(row_start), inputs_from(col_start)
    swapped = jnp.concatenate([cols[:, SPECTRA_SUMMED:], -cols[:, :SPECTRA_SUMMED]], axis=1)
    for part, right in enumerate((cols, swapped)):
        product = lax.dot_general(
            rows, right, (((1,), (1,)), ((), ())), preferred_element_type=jnp.float32
        )
        out_ref[0, 0, part] = (product * (1.0 / SPECTRA_SUMMED)).astype(jnp.bfloat16)


def on_device(voltages, fir_taps, channels, input_good_mask, tile_map):
    own = voltages.shape[1]
    chans = channels.shape[0]
    n_chan = lax.axis_size("chan")
    n_tile = lax.axis_size("tile")
    assert chans == n_chan and 2 * chans <= LANES and n_chan & (n_chan - 1) == 0
    chips = n_chan // 2
    order = [n_tile * chips - 1] + list(range(n_tile * chips - 1))
    groups = [[2 * place + (parity(place) ^ group) for place in order] for group in range(2)]
    x = voltages.reshape(own, FRAMES, BLOCKS, LANES).transpose(1, 2, 0, 3)
    operands = (channels, input_good_mask, fir_taps, x)
    hbm = pl.BlockSpec(memory_space=pltpu.HBM)
    vmem = pl.BlockSpec(memory_space=pltpu.VMEM)
    per_block = 2 * HALVES * own
    kinds = 2 * chans
    folded_rows = SPECTRA_SUMMED + (LANES if kinds < LANES else 0)
    spectra = pl.pallas_call(
        functools.partial(front_kernel, own, chans, n_tile),
        out_shape=pltpu.VMEM((n_tile, chans * per_block, LANES), jnp.bfloat16),
        in_specs=[hbm, hbm, hbm, hbm],
        out_specs=vmem,
        scratch_shapes=[
            pltpu.SMEM(channels.shape, jnp.int32),
            pltpu.SMEM(input_good_mask.shape, jnp.int32),
            pltpu.VMEM(fir_taps.shape, jnp.float32),
            pltpu.VMEM((ROWS, BLOCKS, own, LANES), jnp.bfloat16),
            pltpu.VMEM((ROWS * own, TRANSFORM_LENGTH), jnp.bfloat16),
            pltpu.VMEM((FILTER_TAPS * kinds, TRANSFORM_LENGTH), jnp.bfloat16),
            pltpu.VMEM((own * folded_rows, LANES), jnp.float32),
            pltpu.VMEM((chans * per_block, LANES), jnp.float32),
            pltpu.SemaphoreType.DMA((len(PARTS) - 1,)),
            pltpu.SemaphoreType.DMA((3,)),
        ],
        compiler_params=pltpu.CompilerParams(vmem_limit_bytes=32 << 20),
        name="front",
    )(*(pltpu.with_memory_space_constraint(v, pltpu.HBM) for v in operands))
    spectra = spectra.reshape(n_tile * chips, 2 * per_block, LANES)
    mine = lax.all_to_all(
        spectra, ("tile", "chan"), split_axis=0, concat_axis=0, axis_index_groups=groups, tiled=True
    )
    other = lax.ppermute(mine, "chan", [(c, c ^ 1) for c in range(n_chan)])
    grid_side = n_tile // 8 + 2
    inputs = n_tile * n_chan * own
    side = inputs // grid_side
    return pl.pallas_call(
        functools.partial(back_kernel, own, grid_side),
        out_shape=jax.ShapeDtypeStruct((1, 1, 2, side, side), jnp.bfloat16),
        in_specs=[pl.BlockSpec(memory_space=pl.ANY), vmem, vmem],
        out_specs=vmem,
        scratch_shapes=[
            pltpu.SMEM(tile_map.shape[::-1], jnp.int32),
            pltpu.VMEM((n_tile * n_chan * per_block, LANES), jnp.float32),
            pltpu.VMEM((n_tile * n_chan * per_block, LANES), jnp.float32),
            pltpu.VMEM((2 * HALVES, inputs, LANES), jnp.float32),
            pltpu.SemaphoreType.DMA(()),
        ],
        compiler_params=pltpu.CompilerParams(vmem_limit_bytes=(4 << 20) + 60 * inputs * LANES * own),
        name="back",
    )(tile_map.T, mine, other)


def solution(mesh):
    in_specs = (P("tile", "chan", None), P(), P(), P("tile", "chan"), P())
    out_specs = P("chan", "tile", None, None, None)
    return jax.shard_map(
        on_device, mesh=mesh, in_specs=in_specs, out_specs=out_specs, check_vma=False
    )
```

```python
import functools
import math

import jax
import jax.numpy as jnp
from jax import lax
from jax.experimental import pallas as pl
from jax.experimental.pallas import tpu as pltpu
from jax.sharding import PartitionSpec as P

TRANSFORM_LENGTH = 2048
FILTER_TAPS = 16
SPECTRA_SUMMED = 256
FRAMES = SPECTRA_SUMMED + FILTER_TAPS - 1
ROWS = 272
LANES = 128
BLOCKS = TRANSFORM_LENGTH // LANES
DIRECT = 8
HALVES = SPECTRA_SUMMED // LANES
OCTANT = TRANSFORM_LENGTH // 8


def cos_sin(phase):
    turns = (phase + OCTANT) >> (OCTANT.bit_length())
    angle = (phase - (turns << OCTANT.bit_length())).astype(jnp.float32) * (2.0 * math.pi / TRANSFORM_LENGTH)
    square = angle * angle
    cosine, sine = jnp.zeros_like(angle), jnp.zeros_like(angle)
    for power in range(10, -1, -2):
        sign = -1.0 if power % 4 else 1.0
        cosine = cosine * square + sign / math.factorial(power)
        sine = sine * square + sign / math.factorial(power + 1)
    sine = sine * angle
    odd = (turns & 1) == 1
    first, second = jnp.where(odd, sine, cosine), jnp.where(odd, cosine, sine)
    first = jnp.where(((turns + 1) & 2) == 2, -first, first)
    second = jnp.where((turns & 2) == 2, -second, second)
    return first, second


def parity(place):
    return (place ^ (place >> 1) ^ (place >> 2)) & 1


def dft_blocks(chans, channels_ref):
    row = lax.broadcasted_iota(jnp.int32, (chans, LANES), 0)
    lane = lax.broadcasted_iota(jnp.int32, (chans, LANES), 1)
    channel = jnp.zeros((chans, LANES), jnp.int32)
    for c in range(chans):
        channel = jnp.where(row == c, channels_ref[(c + chans - 2) % chans], channel)

    def unit(phase):
        return cos_sin(phase & (TRANSFORM_LENGTH - 1))

    factor = 1.0 / math.sqrt(TRANSFORM_LENGTH)
    cos0, sin0 = unit(channel * lane)
    blocks = [(cos0 * factor, sin0 * factor)]
    for bit in range(BLOCKS.bit_length() - 1):
        cos1, sin1 = unit(channel * (LANES << bit))
        blocks += [(c * cos1 - s * sin1, s * cos1 + c * sin1) for c, s in blocks]
    return [jnp.concatenate([cosine, -sine], axis=0) for cosine, sine in blocks]


def build_table(chans, blocks, taps_ref, table_ref):
    for nb, dft in enumerate(blocks):
        columns = slice(nb * LANES, (nb + 1) * LANES)
        for tap in range(FILTER_TAPS):
            table_ref[tap * 2 * chans : (tap + 1) * 2 * chans, columns] = (
                dft * taps_ref[tap : tap + 1, columns]
            ).astype(jnp.bfloat16)


def front_kernel(
    own, chans, copies, channels_hbm, mask_hbm, taps_hbm, x_hbm, out_ref,
    channels_ref, mask_ref, taps_ref, x_ref, rest_ref, sorted_ref, table_ref, fold_ref, block_ref,
    sems, small_sems,
):
    small = [
        pltpu.make_async_copy(source, target, small_sems.at[place])
        for place, (source, target) in enumerate(
            ((taps_hbm, taps_ref), (channels_hbm, channels_ref), (mask_hbm, mask_ref))
        )
    ]
    transfers = [
        pltpu.make_async_copy(x_hbm.at[:, nb], x_ref.at[nb, pl.ds(0, FRAMES)], sems.at[nb])
        for nb in range(DIRECT)
    ]
    halves = ((0, ROWS // 2), (ROWS // 2, FRAMES))
    rest = [
        pltpu.make_async_copy(
            x_hbm.at[pl.ds(start, stop - start), pl.ds(DIRECT, BLOCKS - DIRECT)],
            rest_ref.at[pl.ds(start, stop - start)],
            sems.at[DIRECT + part],
        )
        for part, (start, stop) in enumerate(halves)
    ]
    for transfer in small:
        transfer.start()
    for place, transfer in enumerate(rest + transfers):
        transfer.start(priority=place % 2)
    small[1].wait()
    blocks = dft_blocks(chans, channels_ref)
    small[0].wait()
    small[2].wait()
    build_table(chans, blocks, taps_ref, table_ref)
    for part, transfer in enumerate(rest):
        transfer.wait()
        frames = pl.ds(part * (ROWS // 2), ROWS // 2)
        lines = pl.ds(part * (ROWS // 2) * own, ROWS // 2 * own)
        for place in range(BLOCKS - DIRECT):
            sorted_ref[place, lines, :] = rest_ref[frames, place].reshape(ROWS // 2 * own, LANES)
    rows_ref = x_ref.reshape(DIRECT, ROWS * own, LANES)
    product = lax.dot_general(
        jnp.concatenate([sorted_ref[place] for place in range(BLOCKS - DIRECT)], axis=1),
        table_ref[:, DIRECT * LANES :],
        (((1,), (1,)), ((), ())),
        preferred_element_type=jnp.float32,
    )
    for transfer in transfers:
        transfer.wait()
    product = product + lax.dot_general(
        jnp.concatenate([rows_ref[nb] for nb in range(DIRECT)], axis=1),
        table_ref[:, : DIRECT * LANES],
        (((1,), (1,)), ((), ())),
        preferred_element_type=jnp.float32,
    )
    kinds = 2 * chans
    together = LANES // kinds
    kept = -(-(SPECTRA_SUMMED + together - 1) // 8) * 8
    folded = product[: kept * own, :LANES]
    for group in range(1, FILTER_TAPS // together):
        start = group * together * own
        folded = folded + product[
            start : start + kept * own, group * LANES : (group + 1) * LANES
        ]
    fold_ref[: kept * own, :] = folded
    for i in range(own):
        turned = fold_ref[pl.ds(i, fold_ref.shape[0] // own, stride=own), :].T
        spectra = turned[:kinds, :SPECTRA_SUMMED]
        for tap in range(1, together):
            shifted = pltpu.roll(
                turned[tap * kinds : (tap + 1) * kinds, :], turned.shape[1] - tap, axis=1
            )
            spectra = spectra + shifted[:, :SPECTRA_SUMMED]
        spectra = spectra * mask_ref[0, i].astype(jnp.float32)
        for half in range(HALVES):
            for q in range(2):
                block_ref[pl.ds((i * HALVES + half) * 2 + q, chans, stride=4 * own), :] = spectra[
                    q * chans : (q + 1) * chans, half * LANES : (half + 1) * LANES
                ]
    block = block_ref[...].astype(jnp.bfloat16)
    for copy in range(copies):
        out_ref[copy] = block


def back_kernel(
    own, grid_side, tile_map_any, mine_ref, other_ref, out_ref,
    tile_map_ref, mine_wide, other_wide, signal_ref, sem,
):
    fetch = pltpu.make_async_copy(tile_map_any, tile_map_ref, sem)
    fetch.start()
    sources = mine_ref.shape[0]
    inputs = sources * 2 * own
    side = inputs // grid_side
    lines = mine_ref.shape[1]
    chan = lax.axis_index("chan")
    core_here = chan & 1
    place_here = lax.axis_index("tile") * (lax.axis_size("chan") // 2) + (chan >> 1)
    group_here = core_here ^ parity(place_here)
    mine_wide[...] = mine_ref[...].reshape(sources * lines, LANES).astype(jnp.float32)
    other_wide[...] = other_ref[...].reshape(sources * lines, LANES).astype(jnp.float32)
    runs = ((0, sources - 1, 1), (1, 0, sources - 1))
    for block, source, count in runs:
        place = source + lax.broadcasted_iota(jnp.int32, (count, LANES), 0)
        first_is_mine = (parity(place) ^ group_here) == 0
        for i in range(own):
            for half in range(HALVES):
                for q in range(2):
                    line = block * lines + (i * HALVES + half) * 2 + q
                    low = pl.ds(line, count, stride=lines)
                    high = pl.ds(line + lines // 2, count, stride=lines)
                    mine = jnp.where(core_here == 0, mine_wide[low, :], mine_wide[high, :])
                    other = jnp.where(core_here == 0, other_wide[low, :], other_wide[high, :])
                    from_core = (
                        jnp.where(first_is_mine, mine, other),
                        jnp.where(first_is_mine, other, mine),
                    )
                    for core in range(2):
                        target = pl.ds((source * 2 + core) * own + i, count, stride=2 * own)
                        signal_ref[q * HALVES + half, target, :] = from_core[core]
    fetch.wait()
    tile = tile_map_ref[lax.axis_index("tile"), chan]
    bits = grid_side.bit_length() - 1
    row_start = pl.multiple_of((tile >> bits) * side, side)
    col_start = pl.multiple_of((tile & (grid_side - 1)) * side, side)

    def inputs_from(start):
        planes = [signal_ref[plane, pl.ds(start, side), :] for plane in range(2 * HALVES)]
        return jnp.concatenate(planes, axis=1).astype(jnp.bfloat16)

    rows, cols = inputs_from(row_start), inputs_from(col_start)
    swapped = jnp.concatenate([cols[:, SPECTRA_SUMMED:], -cols[:, :SPECTRA_SUMMED]], axis=1)
    for part, right in enumerate((cols, swapped)):
        product = lax.dot_general(
            rows, right, (((1,), (1,)), ((), ())), preferred_element_type=jnp.float32
        )
        out_ref[0, 0, part] = (product * (1.0 / SPECTRA_SUMMED)).astype(jnp.bfloat16)


def on_device(voltages, fir_taps, channels, input_good_mask, tile_map):
    own = voltages.shape[1]
    chans = channels.shape[0]
    n_chan = lax.axis_size("chan")
    n_tile = lax.axis_size("tile")
    assert chans == n_chan and 2 * chans <= LANES and n_chan & (n_chan - 1) == 0
    chips = n_chan // 2
    order = [n_tile * chips - 1] + list(range(n_tile * chips - 1))
    groups = [[2 * place + (parity(place) ^ group) for place in order] for group in range(2)]
    x = voltages.reshape(own, FRAMES, BLOCKS, LANES).transpose(1, 2, 0, 3)
    operands = (channels, input_good_mask, fir_taps, x)
    hbm = pl.BlockSpec(memory_space=pltpu.HBM)
    vmem = pl.BlockSpec(memory_space=pltpu.VMEM)
    per_block = 2 * HALVES * own
    kinds = 2 * chans
    folded_rows = SPECTRA_SUMMED + (LANES if kinds < LANES else 0)
    spectra = pl.pallas_call(
        functools.partial(front_kernel, own, chans, n_tile),
        out_shape=pltpu.VMEM((n_tile, chans * per_block, LANES), jnp.bfloat16),
        in_specs=[hbm, hbm, hbm, hbm],
        out_specs=vmem,
        scratch_shapes=[
            pltpu.SMEM(channels.shape, jnp.int32),
            pltpu.SMEM(input_good_mask.shape, jnp.int32),
            pltpu.VMEM(fir_taps.shape, jnp.float32),
            pltpu.VMEM((DIRECT, ROWS, own, LANES), jnp.bfloat16),
            pltpu.VMEM((ROWS, BLOCKS - DIRECT, own, LANES), jnp.bfloat16),
            pltpu.VMEM((BLOCKS - DIRECT, ROWS * own, LANES), jnp.bfloat16),
            pltpu.VMEM((FILTER_TAPS * kinds, TRANSFORM_LENGTH), jnp.bfloat16),
            pltpu.VMEM((own * folded_rows, LANES), jnp.float32),
            pltpu.VMEM((chans * per_block, LANES), jnp.float32),
            pltpu.SemaphoreType.DMA((DIRECT + 2,)),
            pltpu.SemaphoreType.DMA((3,)),
        ],
        compiler_params=pltpu.CompilerParams(vmem_limit_bytes=32 << 20),
        name="front",
    )(*(pltpu.with_memory_space_constraint(v, pltpu.HBM) for v in operands))
    spectra = spectra.reshape(n_tile * chips, 2 * per_block, LANES)
    mine = lax.all_to_all(
        spectra, ("tile", "chan"), split_axis=0, concat_axis=0, axis_index_groups=groups, tiled=True
    )
    other = lax.ppermute(mine, "chan", [(c, c ^ 1) for c in range(n_chan)])
    grid_side = n_tile // 8 + 2
    inputs = n_tile * n_chan * own
    side = inputs // grid_side
    return pl.pallas_call(
        functools.partial(back_kernel, own, grid_side),
        out_shape=jax.ShapeDtypeStruct((1, 1, 2, side, side), jnp.bfloat16),
        in_specs=[pl.BlockSpec(memory_space=pl.ANY), vmem, vmem],
        out_specs=vmem,
        scratch_shapes=[
            pltpu.SMEM(tile_map.shape[::-1], jnp.int32),
            pltpu.VMEM((n_tile * n_chan * per_block, LANES), jnp.float32),
            pltpu.VMEM((n_tile * n_chan * per_block, LANES), jnp.float32),
            pltpu.VMEM((2 * HALVES, inputs, LANES), jnp.float32),
            pltpu.SemaphoreType.DMA(()),
        ],
        compiler_params=pltpu.CompilerParams(vmem_limit_bytes=(4 << 20) + 60 * inputs * LANES * own),
        name="back",
    )(tile_map.T, mine, other)


def solution(mesh):
    in_specs = (P("tile", "chan", None), P(), P(), P("tile", "chan"), P())
    out_specs = P("chan", "tile", None, None, None)
    return jax.shard_map(
        on_device, mesh=mesh, in_specs=in_specs, out_specs=out_specs, check_vma=False
    )
```

```python
import functools
import math

import jax
import jax.numpy as jnp
from jax import lax
from jax.experimental import pallas as pl
from jax.experimental.pallas import tpu as pltpu
from jax.sharding import PartitionSpec as P

TRANSFORM_LENGTH = 2048
FILTER_TAPS = 16
SPECTRA_SUMMED = 256
FRAMES = SPECTRA_SUMMED + FILTER_TAPS - 1
ROWS = 272
LANES = 128
BLOCKS = TRANSFORM_LENGTH // LANES
DIRECT = 10
HALVES = SPECTRA_SUMMED // LANES
OCTANT = TRANSFORM_LENGTH // 8


def cos_sin(phase):
    turns = (phase + OCTANT) >> (OCTANT.bit_length())
    angle = (phase - (turns << OCTANT.bit_length())).astype(jnp.float32) * (2.0 * math.pi / TRANSFORM_LENGTH)
    square = angle * angle
    cosine, sine = jnp.zeros_like(angle), jnp.zeros_like(angle)
    for power in range(10, -1, -2):
        sign = -1.0 if power % 4 else 1.0
        cosine = cosine * square + sign / math.factorial(power)
        sine = sine * square + sign / math.factorial(power + 1)
    sine = sine * angle
    odd = (turns & 1) == 1
    first, second = jnp.where(odd, sine, cosine), jnp.where(odd, cosine, sine)
    first = jnp.where(((turns + 1) & 2) == 2, -first, first)
    second = jnp.where((turns & 2) == 2, -second, second)
    return first, second


def parity(place):
    return (place ^ (place >> 1) ^ (place >> 2)) & 1


def dft_blocks(chans, channels_ref):
    row = lax.broadcasted_iota(jnp.int32, (chans, LANES), 0)
    lane = lax.broadcasted_iota(jnp.int32, (chans, LANES), 1)
    channel = jnp.zeros((chans, LANES), jnp.int32)
    for c in range(chans):
        channel = jnp.where(row == c, channels_ref[(c + chans - 2) % chans], channel)

    def unit(phase):
        return cos_sin(phase & (TRANSFORM_LENGTH - 1))

    factor = 1.0 / math.sqrt(TRANSFORM_LENGTH)
    cos0, sin0 = unit(channel * lane)
    blocks = [(cos0 * factor, sin0 * factor)]
    for bit in range(BLOCKS.bit_length() - 1):
        cos1, sin1 = unit(channel * (LANES << bit))
        blocks += [(c * cos1 - s * sin1, s * cos1 + c * sin1) for c, s in blocks]
    return [jnp.concatenate([cosine, -sine], axis=0) for cosine, sine in blocks]


def build_table(chans, blocks, taps_ref, table_ref):
    for nb, dft in enumerate(blocks):
        columns = slice(nb * LANES, (nb + 1) * LANES)
        for tap in range(FILTER_TAPS):
            table_ref[tap * 2 * chans : (tap + 1) * 2 * chans, columns] = (
                dft * taps_ref[tap : tap + 1, columns]
            ).astype(jnp.bfloat16)


def front_kernel(
    own, chans, copies, channels_hbm, mask_hbm, taps_hbm, x_hbm, out_ref,
    channels_ref, mask_ref, taps_ref, x_ref, rest_ref, sorted_ref, table_ref, fold_ref, block_ref,
    sems, small_sems,
):
    small = [
        pltpu.make_async_copy(source, target, small_sems.at[place])
        for place, (source, target) in enumerate(
            ((taps_hbm, taps_ref), (channels_hbm, channels_ref), (mask_hbm, mask_ref))
        )
    ]
    transfers = [
        pltpu.make_async_copy(x_hbm.at[:, nb], x_ref.at[nb, pl.ds(0, FRAMES)], sems.at[nb])
        for nb in range(DIRECT)
    ]
    halves = ((0, ROWS // 2), (ROWS // 2, FRAMES))
    rest = [
        pltpu.make_async_copy(
            x_hbm.at[pl.ds(start, stop - start), pl.ds(DIRECT, BLOCKS - DIRECT)],
            rest_ref.at[pl.ds(start, stop - start)],
            sems.at[DIRECT + part],
        )
        for part, (start, stop) in enumerate(halves)
    ]
    for transfer in small:
        transfer.start()
    for place, transfer in enumerate(rest + transfers):
        transfer.start(priority=place % 2)
    small[1].wait()
    blocks = dft_blocks(chans, channels_ref)
    small[0].wait()
    small[2].wait()
    build_table(chans, blocks, taps_ref, table_ref)
    for part, transfer in enumerate(rest):
        transfer.wait()
        frames = pl.ds(part * (ROWS // 2), ROWS // 2)
        lines = pl.ds(part * (ROWS // 2) * own, ROWS // 2 * own)
        for place in range(BLOCKS - DIRECT):
            sorted_ref[place, lines, :] = rest_ref[frames, place].reshape(ROWS // 2 * own, LANES)
    rows_ref = x_ref.reshape(DIRECT, ROWS * own, LANES)
    for transfer in transfers:
        transfer.wait()
    product = lax.dot_general(
        jnp.concatenate(
            [rows_ref[nb] for nb in range(DIRECT)]
            + [sorted_ref[place] for place in range(BLOCKS - DIRECT)],
            axis=1,
        ),
        table_ref[...],
        (((1,), (1,)), ((), ())),
        preferred_element_type=jnp.float32,
    )
    kinds = 2 * chans
    together = LANES // kinds
    kept = -(-(SPECTRA_SUMMED + together - 1) // 8) * 8
    folded = product[: kept * own, :LANES]
    for group in range(1, FILTER_TAPS // together):
        start = group * together * own
        folded = folded + product[
            start : start + kept * own, group * LANES : (group + 1) * LANES
        ]
    fold_ref[: kept * own, :] = folded
    for i in range(own):
        turned = fold_ref[pl.ds(i, fold_ref.shape[0] // own, stride=own), :].T
        spectra = turned[:kinds, :SPECTRA_SUMMED]
        for tap in range(1, together):
            shifted = pltpu.roll(
                turned[tap * kinds : (tap + 1) * kinds, :], turned.shape[1] - tap, axis=1
            )
            spectra = spectra + shifted[:, :SPECTRA_SUMMED]
        spectra = spectra * mask_ref[0, i].astype(jnp.float32)
        for half in range(HALVES):
            for q in range(2):
                block_ref[pl.ds((i * HALVES + half) * 2 + q, chans, stride=4 * own), :] = spectra[
                    q * chans : (q + 1) * chans, half * LANES : (half + 1) * LANES
                ]
    block = block_ref[...].astype(jnp.bfloat16)
    for copy in range(copies):
        out_ref[copy] = block


def back_kernel(
    own, grid_side, tile_map_any, mine_ref, other_ref, out_ref,
    tile_map_ref, wide_ref, signal_ref, sem,
):
    fetch = pltpu.make_async_copy(tile_map_any, tile_map_ref, sem)
    fetch.start()
    sources = mine_ref.shape[0]
    inputs = sources * 2 * own
    side = inputs // grid_side
    lines = mine_ref.shape[1] // 2
    pitch = lines + 1
    chan = lax.axis_index("chan")
    core_here = chan & 1
    place_here = lax.axis_index("tile") * (lax.axis_size("chan") // 2) + (chan >> 1)
    group_here = core_here ^ parity(place_here)

    def my_channel(blocks_ref, block):
        both = blocks_ref[block].astype(jnp.float32)
        return jnp.where(core_here == 0, both[:lines], both[lines:])

    for block in range(sources):
        place = (block - 1) % sources
        first_is_mine = group_here == parity(place)
        mine, other = my_channel(mine_ref, block), my_channel(other_ref, block)
        target = pl.ds(place * pitch, lines)
        wide_ref[0, target, :] = jnp.where(first_is_mine, mine, other)
        wide_ref[1, target, :] = jnp.where(first_is_mine, other, mine)
    for core in range(2):
        for i in range(own):
            for half in range(HALVES):
                for q in range(2):
                    line = (i * HALVES + half) * 2 + q
                    target = pl.ds(core * own + i, sources, stride=2 * own)
                    signal_ref[q * HALVES + half, target, :] = wide_ref[
                        core, pl.ds(line, sources, stride=pitch), :
                    ]
    fetch.wait()
    tile = tile_map_ref[lax.axis_index("tile"), chan]
    bits = grid_side.bit_length() - 1
    row_start = pl.multiple_of((tile >> bits) * side, side)
    col_start = pl.multiple_of((tile & (grid_side - 1)) * side, side)

    def inputs_from(start):
        planes = [signal_ref[plane, pl.ds(start, side), :] for plane in range(2 * HALVES)]
        return jnp.concatenate(planes, axis=1).astype(jnp.bfloat16)

    rows, cols = inputs_from(row_start), inputs_from(col_start)
    turned = jnp.concatenate([-rows[:, SPECTRA_SUMMED:], rows[:, :SPECTRA_SUMMED]], axis=1)
    product = lax.dot_general(
        jnp.concatenate([rows, turned], axis=0), cols, (((1,), (1,)), ((), ())),
        preferred_element_type=jnp.float32,
    )
    visible = (product * (1.0 / SPECTRA_SUMMED)).astype(jnp.bfloat16)
    for part in range(2):
        out_ref[0, 0, part] = visible[part * side : (part + 1) * side]


def on_device(voltages, fir_taps, channels, input_good_mask, tile_map):
    own = voltages.shape[1]
    chans = channels.shape[0]
    n_chan = lax.axis_size("chan")
    n_tile = lax.axis_size("tile")
    assert chans == n_chan and 2 * chans <= LANES and n_chan & (n_chan - 1) == 0
    chips = n_chan // 2
    order = [n_tile * chips - 1] + list(range(n_tile * chips - 1))
    groups = [[2 * place + (parity(place) ^ group) for place in order] for group in range(2)]
    x = voltages.reshape(own, FRAMES, BLOCKS, LANES).transpose(1, 2, 0, 3)
    operands = (channels, input_good_mask, fir_taps, x)
    hbm = pl.BlockSpec(memory_space=pltpu.HBM)
    vmem = pl.BlockSpec(memory_space=pltpu.VMEM)
    per_block = 2 * HALVES * own
    kinds = 2 * chans
    folded_rows = SPECTRA_SUMMED + (LANES if kinds < LANES else 0)
    spectra = pl.pallas_call(
        functools.partial(front_kernel, own, chans, n_tile),
        out_shape=pltpu.VMEM((n_tile, chans * per_block, LANES), jnp.bfloat16),
        in_specs=[hbm, hbm, hbm, hbm],
        out_specs=vmem,
        scratch_shapes=[
            pltpu.SMEM(channels.shape, jnp.int32),
            pltpu.SMEM(input_good_mask.shape, jnp.int32),
            pltpu.VMEM(fir_taps.shape, jnp.float32),
            pltpu.VMEM((DIRECT, ROWS, own, LANES), jnp.bfloat16),
            pltpu.VMEM((ROWS, BLOCKS - DIRECT, own, LANES), jnp.bfloat16),
            pltpu.VMEM((BLOCKS - DIRECT, ROWS * own, LANES), jnp.bfloat16),
            pltpu.VMEM((FILTER_TAPS * kinds, TRANSFORM_LENGTH), jnp.bfloat16),
            pltpu.VMEM((own * folded_rows, LANES), jnp.float32),
            pltpu.VMEM((chans * per_block, LANES), jnp.float32),
            pltpu.SemaphoreType.DMA((DIRECT + 2,)),
            pltpu.SemaphoreType.DMA((3,)),
        ],
        compiler_params=pltpu.CompilerParams(vmem_limit_bytes=32 << 20),
        name="front",
    )(*(pltpu.with_memory_space_constraint(v, pltpu.HBM) for v in operands))
    spectra = spectra.reshape(n_tile * chips, 2 * per_block, LANES)
    mine = lax.all_to_all(
        spectra, ("tile", "chan"), split_axis=0, concat_axis=0, axis_index_groups=groups, tiled=True
    )
    other = lax.ppermute(mine, "chan", [(c, c ^ 1) for c in range(n_chan)])
    grid_side = n_tile // 8 + 2
    inputs = n_tile * n_chan * own
    side = inputs // grid_side
    return pl.pallas_call(
        functools.partial(back_kernel, own, grid_side),
        out_shape=jax.ShapeDtypeStruct((1, 1, 2, side, side), jnp.bfloat16),
        in_specs=[pl.BlockSpec(memory_space=pl.ANY), vmem, vmem],
        out_specs=vmem,
        scratch_shapes=[
            pltpu.SMEM(tile_map.shape[::-1], jnp.int32),
            pltpu.VMEM((2, n_tile * chips * (per_block + 1), LANES), jnp.float32),
            pltpu.VMEM((2 * HALVES, inputs, LANES), jnp.float32),
            pltpu.SemaphoreType.DMA(()),
        ],
        compiler_params=pltpu.CompilerParams(vmem_limit_bytes=(4 << 20) + 60 * inputs * LANES * own),
        name="back",
    )(tile_map.T, mine, other)


def solution(mesh):
    in_specs = (P("tile", "chan", None), P(), P(), P("tile", "chan"), P())
    out_specs = P("chan", "tile", None, None, None)
    return jax.shard_map(
        on_device, mesh=mesh, in_specs=in_specs, out_specs=out_specs, check_vma=False
    )
```

```python
import functools
import math

import jax
import jax.numpy as jnp
from jax import lax
from jax.experimental import pallas as pl
from jax.experimental.pallas import tpu as pltpu
from jax.sharding import PartitionSpec as P

TRANSFORM_LENGTH = 2048
FILTER_TAPS = 16
SPECTRA_SUMMED = 256
FRAMES = SPECTRA_SUMMED + FILTER_TAPS - 1
ROWS = 272
LANES = 128
BLOCKS = TRANSFORM_LENGTH // LANES
DIRECT = 10
HALVES = SPECTRA_SUMMED // LANES
OCTANT = TRANSFORM_LENGTH // 8


def cos_sin(phase):
    turns = (phase + OCTANT) >> (OCTANT.bit_length())
    angle = (phase - (turns << OCTANT.bit_length())).astype(jnp.float32) * (2.0 * math.pi / TRANSFORM_LENGTH)
    square = angle * angle
    cosine, sine = jnp.zeros_like(angle), jnp.zeros_like(angle)
    for power in range(10, -1, -2):
        sign = -1.0 if power % 4 else 1.0
        cosine = cosine * square + sign / math.factorial(power)
        sine = sine * square + sign / math.factorial(power + 1)
    sine = sine * angle
    odd = (turns & 1) == 1
    first, second = jnp.where(odd, sine, cosine), jnp.where(odd, cosine, sine)
    first = jnp.where(((turns + 1) & 2) == 2, -first, first)
    second = jnp.where((turns & 2) == 2, -second, second)
    return first, second


def parity(place):
    return (place ^ (place >> 1) ^ (place >> 2)) & 1


def dft_blocks(chans, channels_ref):
    lane = lax.broadcasted_iota(jnp.int32, (chans, LANES), 1)
    place = lax.broadcasted_iota(jnp.int32, (chans, chans), 0)
    source = lax.broadcasted_iota(jnp.int32, (chans, chans), 1)
    turned = jnp.where(source == ((place + chans - 2) & (chans - 1)), channels_ref[...], 0)
    channel = jnp.sum(turned.astype(jnp.float32), axis=1, keepdims=True).astype(jnp.int32)
    channel = jnp.broadcast_to(channel, (chans, LANES))

    def unit(phase):
        return cos_sin(phase & (TRANSFORM_LENGTH - 1))

    factor = 1.0 / math.sqrt(TRANSFORM_LENGTH)
    cos0, sin0 = unit(channel * lane)
    blocks = [(cos0 * factor, sin0 * factor)]
    for bit in range(BLOCKS.bit_length() - 1):
        cos1, sin1 = unit(channel * (LANES << bit))
        blocks += [(c * cos1 - s * sin1, s * cos1 + c * sin1) for c, s in blocks]
    return [jnp.concatenate([cosine, -sine], axis=0) for cosine, sine in blocks]


def build_table(chans, blocks, taps_ref, table_ref):
    for nb, dft in enumerate(blocks):
        columns = slice(nb * LANES, (nb + 1) * LANES)
        for tap in range(FILTER_TAPS):
            table_ref[tap * 2 * chans : (tap + 1) * 2 * chans, columns] = (
                dft * taps_ref[tap : tap + 1, columns]
            ).astype(jnp.bfloat16)


def front_kernel(
    own, chans, copies, channels_hbm, mask_hbm, taps_hbm, x_hbm, out_ref,
    channels_ref, mask_ref, taps_ref, x_ref, rest_ref, sorted_ref, table_ref, fold_ref, block_ref,
    sems, small_sems,
):
    small = [
        pltpu.make_async_copy(source, target, small_sems.at[place])
        for place, (source, target) in enumerate(
            ((taps_hbm, taps_ref), (channels_hbm, channels_ref), (mask_hbm, mask_ref))
        )
    ]
    transfers = [
        pltpu.make_async_copy(x_hbm.at[:, nb], x_ref.at[nb, pl.ds(0, FRAMES)], sems.at[nb])
        for nb in range(DIRECT)
    ]
    halves = ((0, ROWS // 2), (ROWS // 2, FRAMES))
    rest = [
        pltpu.make_async_copy(
            x_hbm.at[pl.ds(start, stop - start), pl.ds(DIRECT, BLOCKS - DIRECT)],
            rest_ref.at[pl.ds(start, stop - start)],
            sems.at[DIRECT + part],
        )
        for part, (start, stop) in enumerate(halves)
    ]
    for transfer in small:
        transfer.start()
    for place, transfer in enumerate(rest + transfers):
        transfer.start(priority=place % 2)
    small[1].wait()
    blocks = dft_blocks(chans, channels_ref)
    small[0].wait()
    small[2].wait()
    build_table(chans, blocks, taps_ref, table_ref)
    for part, transfer in enumerate(rest):
        transfer.wait()
        frames = pl.ds(part * (ROWS // 2), ROWS // 2)
        lines = pl.ds(part * (ROWS // 2) * own, ROWS // 2 * own)
        for place in range(BLOCKS - DIRECT):
            sorted_ref[place, lines, :] = rest_ref[frames, place].reshape(ROWS // 2 * own, LANES)
    rows_ref = x_ref.reshape(DIRECT, ROWS * own, LANES)
    for transfer in transfers:
        transfer.wait()
    product = lax.dot_general(
        jnp.concatenate(
            [rows_ref[nb] for nb in range(DIRECT)]
            + [sorted_ref[place] for place in range(BLOCKS - DIRECT)],
            axis=1,
        ),
        table_ref[...],
        (((1,), (1,)), ((), ())),
        preferred_element_type=jnp.float32,
    )
    kinds = 2 * chans
    together = LANES // kinds
    kept = -(-(SPECTRA_SUMMED + together - 1) // 8) * 8
    folded = product[: kept * own, :LANES]
    for group in range(1, FILTER_TAPS // together):
        start = group * together * own
        folded = folded + product[
            start : start + kept * own, group * LANES : (group + 1) * LANES
        ]
    fold_ref[: kept * own, :] = folded
    for i in range(own):
        turned = fold_ref[pl.ds(i, fold_ref.shape[0] // own, stride=own), :].T
        spectra = turned[:kinds, :SPECTRA_SUMMED]
        for tap in range(1, together):
            shifted = pltpu.roll(
                turned[tap * kinds : (tap + 1) * kinds, :], turned.shape[1] - tap, axis=1
            )
            spectra = spectra + shifted[:, :SPECTRA_SUMMED]
        spectra = spectra * mask_ref[0, i].astype(jnp.float32)
        for half in range(HALVES):
            for q in range(2):
                block_ref[pl.ds((i * HALVES + half) * 2 + q, chans, stride=4 * own), :] = spectra[
                    q * chans : (q + 1) * chans, half * LANES : (half + 1) * LANES
                ]
    block = block_ref[...].astype(jnp.bfloat16)
    for copy in range(copies):
        out_ref[copy] = block


def back_kernel(
    own, grid_side, tile_map_ref, mine_ref, other_ref, out_ref, wide_ref, signal_ref
):
    slot = lax.broadcasted_iota(jnp.int32, tile_map_ref.shape, 0)
    owner = lax.broadcasted_iota(jnp.int32, tile_map_ref.shape, 1)
    wanted = (slot == lax.axis_index("tile")) & (owner == lax.axis_index("chan"))
    tile = jnp.sum(jnp.where(wanted, tile_map_ref[...].astype(jnp.float32), 0.0)).astype(jnp.int32)
    sources = mine_ref.shape[0]
    inputs = sources * 2 * own
    side = inputs // grid_side
    lines = mine_ref.shape[1] // 2
    pitch = lines + 1
    chan = lax.axis_index("chan")
    core_here = chan & 1
    place_here = lax.axis_index("tile") * (lax.axis_size("chan") // 2) + (chan >> 1)
    group_here = core_here ^ parity(place_here)

    def my_channel(blocks_ref, block):
        both = blocks_ref[block].astype(jnp.float32)
        return jnp.where(core_here == 0, both[:lines], both[lines:])

    for block in range(sources):
        place = (block - 1) % sources
        first_is_mine = group_here == parity(place)
        mine, other = my_channel(mine_ref, block), my_channel(other_ref, block)
        target = pl.ds(place * pitch, lines)
        wide_ref[0, target, :] = jnp.where(first_is_mine, mine, other)
        wide_ref[1, target, :] = jnp.where(first_is_mine, other, mine)
    for core in range(2):
        for i in range(own):
            for half in range(HALVES):
                for q in range(2):
                    line = (i * HALVES + half) * 2 + q
                    target = pl.ds(core * own + i, sources, stride=2 * own)
                    signal_ref[q * HALVES + half, target, :] = wide_ref[
                        core, pl.ds(line, sources, stride=pitch), :
                    ]
    bits = grid_side.bit_length() - 1
    row_start = pl.multiple_of((tile >> bits) * side, side)
    col_start = pl.multiple_of((tile & (grid_side - 1)) * side, side)

    def inputs_from(start):
        planes = [signal_ref[plane, pl.ds(start, side), :] for plane in range(2 * HALVES)]
        return jnp.concatenate(planes, axis=1).astype(jnp.bfloat16)

    rows, cols = inputs_from(row_start), inputs_from(col_start)
    turned = jnp.concatenate([-rows[:, SPECTRA_SUMMED:], rows[:, :SPECTRA_SUMMED]], axis=1)
    product = lax.dot_general(
        jnp.concatenate([rows, turned], axis=0), cols, (((1,), (1,)), ((), ())),
        preferred_element_type=jnp.float32,
    )
    visible = (product * (1.0 / SPECTRA_SUMMED)).astype(jnp.bfloat16)
    for part in range(2):
        out_ref[0, 0, part] = visible[part * side : (part + 1) * side]


def on_device(voltages, fir_taps, channels, input_good_mask, tile_map):
    own = voltages.shape[1]
    chans = channels.shape[0]
    n_chan = lax.axis_size("chan")
    n_tile = lax.axis_size("tile")
    assert chans == n_chan and 2 * chans <= LANES and n_chan & (n_chan - 1) == 0
    chips = n_chan // 2
    order = [n_tile * chips - 1] + list(range(n_tile * chips - 1))
    groups = [[2 * place + (parity(place) ^ group) for place in order] for group in range(2)]
    x = voltages.reshape(own, FRAMES, BLOCKS, LANES).transpose(1, 2, 0, 3)
    operands = (channels.reshape(1, chans), input_good_mask, fir_taps, x)
    hbm = pl.BlockSpec(memory_space=pltpu.HBM)
    vmem = pl.BlockSpec(memory_space=pltpu.VMEM)
    per_block = 2 * HALVES * own
    kinds = 2 * chans
    folded_rows = SPECTRA_SUMMED + (LANES if kinds < LANES else 0)
    spectra = pl.pallas_call(
        functools.partial(front_kernel, own, chans, n_tile),
        out_shape=pltpu.VMEM((n_tile, chans * per_block, LANES), jnp.bfloat16),
        in_specs=[hbm, hbm, hbm, hbm],
        out_specs=vmem,
        scratch_shapes=[
            pltpu.VMEM((1, chans), jnp.int32),
            pltpu.SMEM(input_good_mask.shape, jnp.int32),
            pltpu.VMEM(fir_taps.shape, jnp.float32),
            pltpu.VMEM((DIRECT, ROWS, own, LANES), jnp.bfloat16),
            pltpu.VMEM((ROWS, BLOCKS - DIRECT, own, LANES), jnp.bfloat16),
            pltpu.VMEM((BLOCKS - DIRECT, ROWS * own, LANES), jnp.bfloat16),
            pltpu.VMEM((FILTER_TAPS * kinds, TRANSFORM_LENGTH), jnp.bfloat16),
            pltpu.VMEM((own * folded_rows, LANES), jnp.float32),
            pltpu.VMEM((chans * per_block, LANES), jnp.float32),
            pltpu.SemaphoreType.DMA((DIRECT + 2,)),
            pltpu.SemaphoreType.DMA((3,)),
        ],
        compiler_params=pltpu.CompilerParams(vmem_limit_bytes=32 << 20),
        name="front",
    )(*(pltpu.with_memory_space_constraint(v, pltpu.HBM) for v in operands))
    spectra = spectra.reshape(n_tile * chips, 2 * per_block, LANES)
    mine = lax.all_to_all(
        spectra, ("tile", "chan"), split_axis=0, concat_axis=0, axis_index_groups=groups, tiled=True
    )
    other = lax.ppermute(mine, "chan", [(c, c ^ 1) for c in range(n_chan)])
    grid_side = n_tile // 8 + 2
    inputs = n_tile * n_chan * own
    side = inputs // grid_side
    return pl.pallas_call(
        functools.partial(back_kernel, own, grid_side),
        out_shape=jax.ShapeDtypeStruct((1, 1, 2, side, side), jnp.bfloat16),
        in_specs=[vmem, vmem, vmem],
        out_specs=vmem,
        scratch_shapes=[
            pltpu.VMEM((2, n_tile * chips * (per_block + 1), LANES), jnp.float32),
            pltpu.VMEM((2 * HALVES, inputs, LANES), jnp.float32),
        ],
        compiler_params=pltpu.CompilerParams(vmem_limit_bytes=(4 << 20) + 60 * inputs * LANES * own),
        name="back",
    )(tile_map.T, mine, other)


def solution(mesh):
    in_specs = (P("tile", "chan", None), P(), P(), P("tile", "chan"), P())
    out_specs = P("chan", "tile", None, None, None)
    return jax.shard_map(
        on_device, mesh=mesh, in_specs=in_specs, out_specs=out_specs, check_vma=False
    )
```

```python
import functools
import math

import jax
import jax.numpy as jnp
from jax import lax
from jax.experimental import pallas as pl
from jax.experimental.pallas import tpu as pltpu
from jax.sharding import PartitionSpec as P

TRANSFORM_LENGTH = 2048
FILTER_TAPS = 16
SPECTRA_SUMMED = 256
FRAMES = SPECTRA_SUMMED + FILTER_TAPS - 1
ROWS = 272
LANES = 128
BLOCKS = TRANSFORM_LENGTH // LANES
DIRECT = 10
HALVES = SPECTRA_SUMMED // LANES
OCTANT = TRANSFORM_LENGTH // 8


def cos_sin(phase):
    turns = (phase + OCTANT) >> (OCTANT.bit_length())
    angle = (phase - (turns << OCTANT.bit_length())).astype(jnp.float32) * (2.0 * math.pi / TRANSFORM_LENGTH)
    square = angle * angle
    cosine, sine = jnp.zeros_like(angle), jnp.zeros_like(angle)
    for power in range(10, -1, -2):
        sign = -1.0 if power % 4 else 1.0
        cosine = cosine * square + sign / math.factorial(power)
        sine = sine * square + sign / math.factorial(power + 1)
    sine = sine * angle
    odd = (turns & 1) == 1
    first, second = jnp.where(odd, sine, cosine), jnp.where(odd, cosine, sine)
    first = jnp.where(((turns + 1) & 2) == 2, -first, first)
    second = jnp.where((turns & 2) == 2, -second, second)
    return first, second


def parity(place):
    return (place ^ (place >> 1) ^ (place >> 2)) & 1


def dft_blocks(chans, channels_ref):
    lane = lax.broadcasted_iota(jnp.int32, (chans, LANES), 1)
    place = lax.broadcasted_iota(jnp.int32, (chans, chans), 0)
    source = lax.broadcasted_iota(jnp.int32, (chans, chans), 1)
    turned = jnp.where(source == ((place + chans - 2) & (chans - 1)), channels_ref[...], 0)
    channel = jnp.sum(turned.astype(jnp.float32), axis=1, keepdims=True).astype(jnp.int32)
    channel = jnp.broadcast_to(channel, (chans, LANES))

    def unit(phase):
        return cos_sin(phase & (TRANSFORM_LENGTH - 1))

    factor = 1.0 / math.sqrt(TRANSFORM_LENGTH)
    cos0, sin0 = unit(channel * lane)
    blocks = [(cos0 * factor, sin0 * factor)]
    for bit in range(BLOCKS.bit_length() - 1):
        cos1, sin1 = unit(channel * (LANES << bit))
        blocks += [(c * cos1 - s * sin1, s * cos1 + c * sin1) for c, s in blocks]
    return [jnp.concatenate([cosine, -sine], axis=0) for cosine, sine in blocks]


def build_table(chans, blocks, taps_ref, table_ref):
    for nb, dft in enumerate(blocks):
        columns = slice(nb * LANES, (nb + 1) * LANES)
        for tap in range(FILTER_TAPS):
            table_ref[tap * 2 * chans : (tap + 1) * 2 * chans, columns] = (
                dft * taps_ref[tap : tap + 1, columns]
            ).astype(jnp.bfloat16)


def front_kernel(
    own, chans, copies, channels_hbm, mask_hbm, taps_hbm, x_hbm, out_ref,
    channels_ref, mask_ref, taps_ref, x_ref, rest_ref, sorted_ref, table_ref, fold_ref, block_ref,
    sems, small_sems,
):
    small = [
        pltpu.make_async_copy(source, target, small_sems.at[place])
        for place, (source, target) in enumerate(
            ((taps_hbm, taps_ref), (channels_hbm, channels_ref), (mask_hbm, mask_ref))
        )
    ]
    transfers = [
        pltpu.make_async_copy(x_hbm.at[:, nb], x_ref.at[nb, pl.ds(0, FRAMES)], sems.at[nb])
        for nb in range(DIRECT)
    ]
    halves = ((0, ROWS // 2), (ROWS // 2, FRAMES))
    rest = [
        pltpu.make_async_copy(
            x_hbm.at[pl.ds(start, stop - start), pl.ds(DIRECT, BLOCKS - DIRECT)],
            rest_ref.at[pl.ds(start, stop - start)],
            sems.at[DIRECT + part],
        )
        for part, (start, stop) in enumerate(halves)
    ]
    for transfer in small:
        transfer.start()
    for place, transfer in enumerate(rest + transfers):
        transfer.start(priority=place % 2)
    small[1].wait()
    blocks = dft_blocks(chans, channels_ref)
    small[0].wait()
    small[2].wait()
    build_table(chans, blocks, taps_ref, table_ref)
    for part, transfer in enumerate(rest):
        transfer.wait()
        frames = pl.ds(part * (ROWS // 2), ROWS // 2)
        lines = pl.ds(part * (ROWS // 2) * own, ROWS // 2 * own)
        for place in range(BLOCKS - DIRECT):
            sorted_ref[place, lines, :] = rest_ref[frames, place].reshape(ROWS // 2 * own, LANES)
    rows_ref = x_ref.reshape(DIRECT, ROWS * own, LANES)
    for transfer in transfers:
        transfer.wait()
    product = lax.dot_general(
        jnp.concatenate(
            [rows_ref[nb] for nb in range(DIRECT)]
            + [sorted_ref[place] for place in range(BLOCKS - DIRECT)],
            axis=1,
        ),
        table_ref[...],
        (((1,), (1,)), ((), ())),
        preferred_element_type=jnp.float32,
    )
    kinds = 2 * chans
    together = LANES // kinds
    kept = -(-(SPECTRA_SUMMED + together - 1) // 8) * 8
    folded = product[: kept * own, :LANES]
    for group in range(1, FILTER_TAPS // together):
        start = group * together * own
        folded = folded + product[
            start : start + kept * own, group * LANES : (group + 1) * LANES
        ]
    fold_ref[: kept * own, :] = folded
    for i in range(own):
        turned = fold_ref[pl.ds(i, fold_ref.shape[0] // own, stride=own), :].T
        spectra = turned[:kinds, :SPECTRA_SUMMED]
        for tap in range(1, together):
            shifted = pltpu.roll(
                turned[tap * kinds : (tap + 1) * kinds, :], turned.shape[1] - tap, axis=1
            )
            spectra = spectra + shifted[:, :SPECTRA_SUMMED]
        spectra = spectra * mask_ref[:, i : i + 1].astype(jnp.float32)
        for half in range(HALVES):
            for q in range(2):
                block_ref[pl.ds((i * HALVES + half) * 2 + q, chans, stride=4 * own), :] = spectra[
                    q * chans : (q + 1) * chans, half * LANES : (half + 1) * LANES
                ]
    block = block_ref[...].astype(jnp.bfloat16)
    for copy in range(copies):
        out_ref[copy] = block


def back_kernel(
    own, grid_side, tile_map_ref, mine_ref, other_ref, out_ref, wide_ref, signal_ref
):
    slot = lax.broadcasted_iota(jnp.int32, tile_map_ref.shape, 0)
    owner = lax.broadcasted_iota(jnp.int32, tile_map_ref.shape, 1)
    wanted = (slot == lax.axis_index("tile")) & (owner == lax.axis_index("chan"))
    tile = jnp.sum(jnp.where(wanted, tile_map_ref[...].astype(jnp.float32), 0.0)).astype(jnp.int32)
    sources = mine_ref.shape[0]
    inputs = sources * 2 * own
    side = inputs // grid_side
    lines = mine_ref.shape[1] // 2
    pitch = lines + 1
    chan = lax.axis_index("chan")
    core_here = chan & 1
    place_here = lax.axis_index("tile") * (lax.axis_size("chan") // 2) + (chan >> 1)
    group_here = core_here ^ parity(place_here)

    def my_channel(blocks_ref, block):
        both = blocks_ref[block].astype(jnp.float32)
        return jnp.where(core_here == 0, both[:lines], both[lines:])

    for block in range(sources):
        place = (block - 1) % sources
        first_is_mine = group_here == parity(place)
        mine, other = my_channel(mine_ref, block), my_channel(other_ref, block)
        target = pl.ds(place * pitch, lines)
        wide_ref[0, target, :] = jnp.where(first_is_mine, mine, other)
        wide_ref[1, target, :] = jnp.where(first_is_mine, other, mine)
    for core in range(2):
        for i in range(own):
            for half in range(HALVES):
                for q in range(2):
                    line = (i * HALVES + half) * 2 + q
                    target = pl.ds(core * own + i, sources, stride=2 * own)
                    signal_ref[q * HALVES + half, target, :] = wide_ref[
                        core, pl.ds(line, sources, stride=pitch), :
                    ]
    bits = grid_side.bit_length() - 1
    row_start = pl.multiple_of((tile >> bits) * side, side)
    col_start = pl.multiple_of((tile & (grid_side - 1)) * side, side)

    def inputs_from(start):
        planes = [signal_ref[plane, pl.ds(start, side), :] for plane in range(2 * HALVES)]
        return jnp.concatenate(planes, axis=1).astype(jnp.bfloat16)

    rows, cols = inputs_from(row_start), inputs_from(col_start)
    turned = jnp.concatenate([-rows[:, SPECTRA_SUMMED:], rows[:, :SPECTRA_SUMMED]], axis=1)
    product = lax.dot_general(
        jnp.concatenate([rows, turned], axis=0), cols, (((1,), (1,)), ((), ())),
        preferred_element_type=jnp.float32,
    )
    visible = (product * (1.0 / SPECTRA_SUMMED)).astype(jnp.bfloat16)
    for part in range(2):
        out_ref[0, 0, part] = visible[part * side : (part + 1) * side]


def on_device(voltages, fir_taps, channels, input_good_mask, tile_map):
    own = voltages.shape[1]
    chans = channels.shape[0]
    n_chan = lax.axis_size("chan")
    n_tile = lax.axis_size("tile")
    assert chans == n_chan and 2 * chans <= LANES and n_chan & (n_chan - 1) == 0
    chips = n_chan // 2
    order = [n_tile * chips - 1] + list(range(n_tile * chips - 1))
    groups = [[2 * place + (parity(place) ^ group) for place in order] for group in range(2)]
    x = voltages.reshape(own, FRAMES, BLOCKS, LANES).transpose(1, 2, 0, 3)
    operands = (channels.reshape(1, chans), input_good_mask, fir_taps, x)
    hbm = pl.BlockSpec(memory_space=pltpu.HBM)
    vmem = pl.BlockSpec(memory_space=pltpu.VMEM)
    per_block = 2 * HALVES * own
    kinds = 2 * chans
    folded_rows = SPECTRA_SUMMED + (LANES if kinds < LANES else 0)
    spectra = pl.pallas_call(
        functools.partial(front_kernel, own, chans, n_tile),
        out_shape=pltpu.VMEM((n_tile, chans * per_block, LANES), jnp.bfloat16),
        in_specs=[hbm, hbm, hbm, hbm],
        out_specs=vmem,
        scratch_shapes=[
            pltpu.VMEM((1, chans), jnp.int32),
            pltpu.VMEM(input_good_mask.shape, jnp.int32),
            pltpu.VMEM(fir_taps.shape, jnp.float32),
            pltpu.VMEM((DIRECT, ROWS, own, LANES), jnp.bfloat16),
            pltpu.VMEM((ROWS, BLOCKS - DIRECT, own, LANES), jnp.bfloat16),
            pltpu.VMEM((BLOCKS - DIRECT, ROWS * own, LANES), jnp.bfloat16),
            pltpu.VMEM((FILTER_TAPS * kinds, TRANSFORM_LENGTH), jnp.bfloat16),
            pltpu.VMEM((own * folded_rows, LANES), jnp.float32),
            pltpu.VMEM((chans * per_block, LANES), jnp.float32),
            pltpu.SemaphoreType.DMA((DIRECT + 2,)),
            pltpu.SemaphoreType.DMA((3,)),
        ],
        compiler_params=pltpu.CompilerParams(vmem_limit_bytes=32 << 20),
        name="front",
    )(*(pltpu.with_memory_space_constraint(v, pltpu.HBM) for v in operands))
    spectra = spectra.reshape(n_tile * chips, 2 * per_block, LANES)
    mine = lax.all_to_all(
        spectra, ("tile", "chan"), split_axis=0, concat_axis=0, axis_index_groups=groups, tiled=True
    )
    other = lax.ppermute(mine, "chan", [(c, c ^ 1) for c in range(n_chan)])
    grid_side = n_tile // 8 + 2
    inputs = n_tile * n_chan * own
    side = inputs // grid_side
    return pl.pallas_call(
        functools.partial(back_kernel, own, grid_side),
        out_shape=jax.ShapeDtypeStruct((1, 1, 2, side, side), jnp.bfloat16),
        in_specs=[vmem, vmem, vmem],
        out_specs=vmem,
        scratch_shapes=[
            pltpu.VMEM((2, n_tile * chips * (per_block + 1), LANES), jnp.float32),
            pltpu.VMEM((2 * HALVES, inputs, LANES), jnp.float32),
        ],
        compiler_params=pltpu.CompilerParams(vmem_limit_bytes=(4 << 20) + 60 * inputs * LANES * own),
        name="back",
    )(tile_map.T, mine, other)


def solution(mesh):
    in_specs = (P("tile", "chan", None), P(), P(), P("tile", "chan"), P())
    out_specs = P("chan", "tile", None, None, None)
    return jax.shard_map(
        on_device, mesh=mesh, in_specs=in_specs, out_specs=out_specs, check_vma=False
    )
```

```python
import functools
import math

import jax
import jax.numpy as jnp
from jax import lax
from jax.experimental import pallas as pl
from jax.experimental.pallas import tpu as pltpu
from jax.sharding import PartitionSpec as P

TRANSFORM_LENGTH = 2048
FILTER_TAPS = 16
SPECTRA_SUMMED = 256
FRAMES = SPECTRA_SUMMED + FILTER_TAPS - 1
ROWS = 272
LANES = 128
BLOCKS = TRANSFORM_LENGTH // LANES
DIRECT = 10
HALVES = SPECTRA_SUMMED // LANES
OCTANT = TRANSFORM_LENGTH // 8


def cos_sin(phase):
    turns = (phase + OCTANT) >> (OCTANT.bit_length())
    angle = (phase - (turns << OCTANT.bit_length())).astype(jnp.float32) * (2.0 * math.pi / TRANSFORM_LENGTH)
    square = angle * angle
    cosine, sine = jnp.zeros_like(angle), jnp.zeros_like(angle)
    for power in range(10, -1, -2):
        sign = -1.0 if power % 4 else 1.0
        cosine = cosine * square + sign / math.factorial(power)
        sine = sine * square + sign / math.factorial(power + 1)
    sine = sine * angle
    odd = (turns & 1) == 1
    first, second = jnp.where(odd, sine, cosine), jnp.where(odd, cosine, sine)
    first = jnp.where(((turns + 1) & 2) == 2, -first, first)
    second = jnp.where((turns & 2) == 2, -second, second)
    return first, second


def parity(place):
    return (place ^ (place >> 1) ^ (place >> 2)) & 1


def dft_blocks(chans, channels_ref):
    lane = lax.broadcasted_iota(jnp.int32, (chans, LANES), 1)
    place = lax.broadcasted_iota(jnp.int32, (chans, chans), 0)
    source = lax.broadcasted_iota(jnp.int32, (chans, chans), 1)
    turned = jnp.where(source == ((place + chans - 2) & (chans - 1)), channels_ref[...], 0)
    channel = jnp.sum(turned.astype(jnp.float32), axis=1, keepdims=True).astype(jnp.int32)
    channel = jnp.broadcast_to(channel, (chans, LANES))

    def unit(phase):
        return cos_sin(phase & (TRANSFORM_LENGTH - 1))

    factor = 1.0 / math.sqrt(TRANSFORM_LENGTH)
    cos0, sin0 = unit(channel * lane)
    blocks = [(cos0 * factor, sin0 * factor)]
    for bit in range(BLOCKS.bit_length() - 1):
        cos1, sin1 = unit(channel * (LANES << bit))
        blocks += [(c * cos1 - s * sin1, s * cos1 + c * sin1) for c, s in blocks]
    return [jnp.concatenate([cosine, -sine], axis=0) for cosine, sine in blocks]


def build_table(blocks, taps_ref, table_ref):
    for nb, dft in enumerate(blocks):
        columns = slice(nb * LANES, (nb + 1) * LANES)
        scaled = [dft * taps_ref[tap : tap + 1, columns] for tap in range(FILTER_TAPS)]
        table_ref[columns, :] = jnp.concatenate(scaled, axis=0).astype(jnp.bfloat16).T


def front_kernel(
    own, chans, copies, channels_hbm, mask_hbm, taps_hbm, x_hbm, out_ref,
    channels_ref, mask_ref, taps_ref, x_ref, rest_ref, sorted_ref, table_ref, fold_ref, block_ref,
    sems, small_sems,
):
    small = [
        pltpu.make_async_copy(source, target, small_sems.at[place])
        for place, (source, target) in enumerate(
            ((taps_hbm, taps_ref), (channels_hbm, channels_ref), (mask_hbm, mask_ref))
        )
    ]
    transfers = [
        pltpu.make_async_copy(x_hbm.at[:, nb], x_ref.at[nb, pl.ds(0, FRAMES)], sems.at[nb])
        for nb in range(DIRECT)
    ]
    halves = ((0, ROWS // 2), (ROWS // 2, FRAMES))
    rest = [
        pltpu.make_async_copy(
            x_hbm.at[pl.ds(start, stop - start), pl.ds(DIRECT, BLOCKS - DIRECT)],
            rest_ref.at[pl.ds(start, stop - start)],
            sems.at[DIRECT + part],
        )
        for part, (start, stop) in enumerate(halves)
    ]
    for transfer in small:
        transfer.start()
    for place, transfer in enumerate(rest + transfers):
        transfer.start(priority=place % 2)
    small[1].wait()
    blocks = dft_blocks(chans, channels_ref)
    small[0].wait()
    small[2].wait()
    build_table(blocks, taps_ref, table_ref)
    for part, transfer in enumerate(rest):
        transfer.wait()
        frames = pl.ds(part * (ROWS // 2), ROWS // 2)
        lines = pl.ds(part * (ROWS // 2) * own, ROWS // 2 * own)
        for place in range(BLOCKS - DIRECT):
            sorted_ref[place, lines, :] = rest_ref[frames, place].reshape(ROWS // 2 * own, LANES)
    rows_ref = x_ref.reshape(DIRECT, ROWS * own, LANES)
    for transfer in transfers:
        transfer.wait()
    product = lax.dot_general(
        jnp.concatenate(
            [rows_ref[nb] for nb in range(DIRECT)]
            + [sorted_ref[place] for place in range(BLOCKS - DIRECT)],
            axis=1,
        ),
        table_ref[...],
        (((1,), (0,)), ((), ())),
        preferred_element_type=jnp.float32,
    )
    kinds = 2 * chans
    together = LANES // kinds
    kept = -(-(SPECTRA_SUMMED + together - 1) // 8) * 8
    folded = product[: kept * own, :LANES]
    for group in range(1, FILTER_TAPS // together):
        start = group * together * own
        folded = folded + product[
            start : start + kept * own, group * LANES : (group + 1) * LANES
        ]
    fold_ref[: kept * own, :] = folded
    for i in range(own):
        turned = fold_ref[pl.ds(i, fold_ref.shape[0] // own, stride=own), :].T
        spectra = turned[:kinds, :SPECTRA_SUMMED]
        for tap in range(1, together):
            shifted = pltpu.roll(
                turned[tap * kinds : (tap + 1) * kinds, :], turned.shape[1] - tap, axis=1
            )
            spectra = spectra + shifted[:, :SPECTRA_SUMMED]
        spectra = spectra * mask_ref[:, i : i + 1].astype(jnp.float32)
        for half in range(HALVES):
            for q in range(2):
                block_ref[pl.ds((i * HALVES + half) * 2 + q, chans, stride=4 * own), :] = spectra[
                    q * chans : (q + 1) * chans, half * LANES : (half + 1) * LANES
                ]
    block = block_ref[...].astype(jnp.bfloat16)
    for copy in range(copies):
        out_ref[copy] = block


def back_kernel(
    own, grid_side, tile_map_ref, mine_ref, other_ref, out_ref, wide_ref, signal_ref
):
    slot = lax.broadcasted_iota(jnp.int32, tile_map_ref.shape, 0)
    owner = lax.broadcasted_iota(jnp.int32, tile_map_ref.shape, 1)
    wanted = (slot == lax.axis_index("tile")) & (owner == lax.axis_index("chan"))
    tile = jnp.sum(jnp.where(wanted, tile_map_ref[...].astype(jnp.float32), 0.0)).astype(jnp.int32)
    sources = mine_ref.shape[0]
    inputs = sources * 2 * own
    side = inputs // grid_side
    lines = mine_ref.shape[1] // 2
    pitch = lines + 1
    chan = lax.axis_index("chan")
    core_here = chan & 1
    place_here = lax.axis_index("tile") * (lax.axis_size("chan") // 2) + (chan >> 1)
    group_here = core_here ^ parity(place_here)

    def my_channel(blocks_ref, block):
        both = blocks_ref[block].astype(jnp.float32)
        return jnp.where(core_here == 0, both[:lines], both[lines:])

    for block in range(sources):
        place = (block - 1) % sources
        first_is_mine = group_here == parity(place)
        mine, other = my_channel(mine_ref, block), my_channel(other_ref, block)
        target = pl.ds(place * pitch, lines)
        wide_ref[0, target, :] = jnp.where(first_is_mine, mine, other)
        wide_ref[1, target, :] = jnp.where(first_is_mine, other, mine)
    for core in range(2):
        for i in range(own):
            for half in range(HALVES):
                for q in range(2):
                    line = (i * HALVES + half) * 2 + q
                    target = pl.ds(core * own + i, sources, stride=2 * own)
                    signal_ref[q * HALVES + half, target, :] = wide_ref[
                        core, pl.ds(line, sources, stride=pitch), :
                    ]
    bits = grid_side.bit_length() - 1
    row_start = pl.multiple_of((tile >> bits) * side, side)
    col_start = pl.multiple_of((tile & (grid_side - 1)) * side, side)

    def inputs_from(start):
        planes = [signal_ref[plane, pl.ds(start, side), :] for plane in range(2 * HALVES)]
        return jnp.concatenate(planes, axis=1).astype(jnp.bfloat16)

    rows, cols = inputs_from(row_start), inputs_from(col_start)
    turned = jnp.concatenate([-rows[:, SPECTRA_SUMMED:], rows[:, :SPECTRA_SUMMED]], axis=1)
    product = lax.dot_general(
        jnp.concatenate([rows, turned], axis=0), cols, (((1,), (1,)), ((), ())),
        preferred_element_type=jnp.float32,
    )
    visible = (product * (1.0 / SPECTRA_SUMMED)).astype(jnp.bfloat16)
    for part in range(2):
        out_ref[0, 0, part] = visible[part * side : (part + 1) * side]


def on_device(voltages, fir_taps, channels, input_good_mask, tile_map):
    own = voltages.shape[1]
    chans = channels.shape[0]
    n_chan = lax.axis_size("chan")
    n_tile = lax.axis_size("tile")
    assert chans == n_chan and 2 * chans <= LANES and n_chan & (n_chan - 1) == 0
    chips = n_chan // 2
    order = [n_tile * chips - 1] + list(range(n_tile * chips - 1))
    groups = [[2 * place + (parity(place) ^ group) for place in order] for group in range(2)]
    x = voltages.reshape(own, FRAMES, BLOCKS, LANES).transpose(1, 2, 0, 3)
    operands = (channels.reshape(1, chans), input_good_mask, fir_taps, x)
    hbm = pl.BlockSpec(memory_space=pltpu.HBM)
    vmem = pl.BlockSpec(memory_space=pltpu.VMEM)
    per_block = 2 * HALVES * own
    kinds = 2 * chans
    folded_rows = SPECTRA_SUMMED + (LANES if kinds < LANES else 0)
    spectra = pl.pallas_call(
        functools.partial(front_kernel, own, chans, n_tile),
        out_shape=pltpu.VMEM((n_tile, chans * per_block, LANES), jnp.bfloat16),
        in_specs=[hbm, hbm, hbm, hbm],
        out_specs=vmem,
        scratch_shapes=[
            pltpu.VMEM((1, chans), jnp.int32),
            pltpu.VMEM(input_good_mask.shape, jnp.int32),
            pltpu.VMEM(fir_taps.shape, jnp.float32),
            pltpu.VMEM((DIRECT, ROWS, own, LANES), jnp.bfloat16),
            pltpu.VMEM((ROWS, BLOCKS - DIRECT, own, LANES), jnp.bfloat16),
            pltpu.VMEM((BLOCKS - DIRECT, ROWS * own, LANES), jnp.bfloat16),
            pltpu.VMEM((TRANSFORM_LENGTH, FILTER_TAPS * kinds), jnp.bfloat16),
            pltpu.VMEM((own * folded_rows, LANES), jnp.float32),
            pltpu.VMEM((chans * per_block, LANES), jnp.float32),
            pltpu.SemaphoreType.DMA((DIRECT + 2,)),
            pltpu.SemaphoreType.DMA((3,)),
        ],
        compiler_params=pltpu.CompilerParams(vmem_limit_bytes=32 << 20),
        name="front",
    )(*(pltpu.with_memory_space_constraint(v, pltpu.HBM) for v in operands))
    spectra = spectra.reshape(n_tile * chips, 2 * per_block, LANES)
    mine = lax.all_to_all(
        spectra, ("tile", "chan"), split_axis=0, concat_axis=0, axis_index_groups=groups, tiled=True
    )
    other = lax.ppermute(mine, "chan", [(c, c ^ 1) for c in range(n_chan)])
    grid_side = n_tile // 8 + 2
    inputs = n_tile * n_chan * own
    side = inputs // grid_side
    return pl.pallas_call(
        functools.partial(back_kernel, own, grid_side),
        out_shape=jax.ShapeDtypeStruct((1, 1, 2, side, side), jnp.bfloat16),
        in_specs=[vmem, vmem, vmem],
        out_specs=vmem,
        scratch_shapes=[
            pltpu.VMEM((2, n_tile * chips * (per_block + 1), LANES), jnp.float32),
            pltpu.VMEM((2 * HALVES, inputs, LANES), jnp.float32),
        ],
        compiler_params=pltpu.CompilerParams(vmem_limit_bytes=(4 << 20) + 60 * inputs * LANES * own),
        name="back",
    )(tile_map.T, mine, other)


def solution(mesh):
    in_specs = (P("tile", "chan", None), P(), P(), P("tile", "chan"), P())
    out_specs = P("chan", "tile", None, None, None)
    return jax.shard_map(
        on_device, mesh=mesh, in_specs=in_specs, out_specs=out_specs, check_vma=False
    )
```

```python
import functools
import math

import jax
import jax.numpy as jnp
from jax import lax
from jax.experimental import pallas as pl
from jax.experimental.pallas import tpu as pltpu
from jax.sharding import PartitionSpec as P

TRANSFORM_LENGTH = 2048
FILTER_TAPS = 16
SPECTRA_SUMMED = 256
FRAMES = SPECTRA_SUMMED + FILTER_TAPS - 1
ROWS = 272
LANES = 128
BLOCKS = TRANSFORM_LENGTH // LANES
DIRECT = 10
HALVES = SPECTRA_SUMMED // LANES
OCTANT = TRANSFORM_LENGTH // 8


def cos_sin(phase):
    turns = (phase + OCTANT) >> (OCTANT.bit_length())
    angle = (phase - (turns << OCTANT.bit_length())).astype(jnp.float32) * (2.0 * math.pi / TRANSFORM_LENGTH)
    square = angle * angle
    cosine, sine = jnp.zeros_like(angle), jnp.zeros_like(angle)
    for power in range(10, -1, -2):
        sign = -1.0 if power % 4 else 1.0
        cosine = cosine * square + sign / math.factorial(power)
        sine = sine * square + sign / math.factorial(power + 1)
    sine = sine * angle
    odd = (turns & 1) == 1
    first, second = jnp.where(odd, sine, cosine), jnp.where(odd, cosine, sine)
    first = jnp.where(((turns + 1) & 2) == 2, -first, first)
    second = jnp.where((turns & 2) == 2, -second, second)
    return first, second


def parity(place):
    return (place ^ (place >> 1) ^ (place >> 2)) & 1


def dft_blocks(chans, channels_ref):
    lane = lax.broadcasted_iota(jnp.int32, (chans, LANES), 1)
    place = lax.broadcasted_iota(jnp.int32, (chans, chans), 0)
    source = lax.broadcasted_iota(jnp.int32, (chans, chans), 1)
    turned = jnp.where(source == ((place + chans - 2) & (chans - 1)), channels_ref[...], 0)
    channel = jnp.sum(turned.astype(jnp.float32), axis=1, keepdims=True).astype(jnp.int32)
    channel = jnp.broadcast_to(channel, (chans, LANES))

    def unit(phase):
        return cos_sin(phase & (TRANSFORM_LENGTH - 1))

    factor = 1.0 / math.sqrt(TRANSFORM_LENGTH)
    cos0, sin0 = unit(channel * lane)
    blocks = [(cos0 * factor, sin0 * factor)]
    for bit in range(BLOCKS.bit_length() - 1):
        cos1, sin1 = unit(channel * (LANES << bit))
        blocks += [(c * cos1 - s * sin1, s * cos1 + c * sin1) for c, s in blocks]
    return [jnp.concatenate([cosine, -sine], axis=0) for cosine, sine in blocks]


def build_table(chans, blocks, taps_ref, table_ref):
    for nb, dft in enumerate(blocks):
        columns = slice(nb * LANES, (nb + 1) * LANES)
        for tap in range(FILTER_TAPS):
            table_ref[tap * 2 * chans : (tap + 1) * 2 * chans, columns] = (
                dft * taps_ref[tap : tap + 1, columns]
            ).astype(jnp.bfloat16)


def front_kernel(
    own, chans, copies, channels_hbm, mask_hbm, taps_hbm, x_hbm, out_ref,
    channels_ref, mask_ref, taps_ref, x_ref, rest_ref, sorted_ref, table_ref, fold_ref, block_ref,
    sems, small_sems,
):
    small = [
        pltpu.make_async_copy(source, target, small_sems.at[place])
        for place, (source, target) in enumerate(
            ((taps_hbm, taps_ref), (channels_hbm, channels_ref), (mask_hbm, mask_ref))
        )
    ]
    transfers = [
        pltpu.make_async_copy(x_hbm.at[:, nb], x_ref.at[nb, pl.ds(0, FRAMES)], sems.at[nb])
        for nb in range(DIRECT)
    ]
    halves = ((0, ROWS // 2), (ROWS // 2, FRAMES))
    rest = [
        pltpu.make_async_copy(
            x_hbm.at[pl.ds(start, stop - start), pl.ds(DIRECT, BLOCKS - DIRECT)],
            rest_ref.at[pl.ds(start, stop - start)],
            sems.at[DIRECT + part],
        )
        for part, (start, stop) in enumerate(halves)
    ]
    for transfer in small:
        transfer.start()
    for place, transfer in enumerate(rest + transfers):
        transfer.start(priority=place % 2)
    small[1].wait()
    blocks = dft_blocks(chans, channels_ref)
    small[0].wait()
    small[2].wait()
    build_table(chans, blocks, taps_ref, table_ref)
    for transfer in rest + transfers:
        transfer.wait()
    for place in range(BLOCKS - DIRECT):
        sorted_ref[place] = rest_ref[:, place].reshape(ROWS * own, LANES)
    rows_ref = x_ref.reshape(DIRECT, ROWS * own, LANES)
    product = lax.dot_general(
        jnp.concatenate(
            [rows_ref[nb] for nb in range(DIRECT)]
            + [sorted_ref[place] for place in range(BLOCKS - DIRECT)],
            axis=1,
        ),
        table_ref[...],
        (((1,), (1,)), ((), ())),
        preferred_element_type=jnp.float32,
    )
    kinds = 2 * chans
    together = LANES // kinds
    kept = -(-(SPECTRA_SUMMED + together - 1) // 8) * 8
    folded = product[: kept * own, :LANES]
    for group in range(1, FILTER_TAPS // together):
        start = group * together * own
        folded = folded + product[
            start : start + kept * own, group * LANES : (group + 1) * LANES
        ]
    fold_ref[: kept * own, :] = folded
    for i in range(own):
        turned = fold_ref[pl.ds(i, fold_ref.shape[0] // own, stride=own), :].T
        spectra = turned[:kinds, :SPECTRA_SUMMED]
        for tap in range(1, together):
            shifted = pltpu.roll(
                turned[tap * kinds : (tap + 1) * kinds, :], turned.shape[1] - tap, axis=1
            )
            spectra = spectra + shifted[:, :SPECTRA_SUMMED]
        spectra = spectra * mask_ref[:, i : i + 1].astype(jnp.float32)
        for half in range(HALVES):
            for q in range(2):
                block_ref[pl.ds((i * HALVES + half) * 2 + q, chans, stride=4 * own), :] = spectra[
                    q * chans : (q + 1) * chans, half * LANES : (half + 1) * LANES
                ]
    block = block_ref[...].astype(jnp.bfloat16)
    for copy in range(copies):
        out_ref[copy] = block


def back_kernel(
    own, grid_side, tile_map_ref, mine_ref, other_ref, out_ref, wide_ref, signal_ref
):
    slot = lax.broadcasted_iota(jnp.int32, tile_map_ref.shape, 0)
    owner = lax.broadcasted_iota(jnp.int32, tile_map_ref.shape, 1)
    wanted = (slot == lax.axis_index("tile")) & (owner == lax.axis_index("chan"))
    tile = jnp.sum(jnp.where(wanted, tile_map_ref[...].astype(jnp.float32), 0.0)).astype(jnp.int32)
    sources = mine_ref.shape[0]
    inputs = sources * 2 * own
    side = inputs // grid_side
    lines = mine_ref.shape[1] // 2
    pitch = lines + 1
    chan = lax.axis_index("chan")
    core_here = chan & 1
    place_here = lax.axis_index("tile") * (lax.axis_size("chan") // 2) + (chan >> 1)
    group_here = core_here ^ parity(place_here)

    def my_channel(blocks_ref, block):
        both = blocks_ref[block].astype(jnp.float32)
        return jnp.where(core_here == 0, both[:lines], both[lines:])

    for block in range(sources):
        place = (block - 1) % sources
        first_is_mine = group_here == parity(place)
        mine, other = my_channel(mine_ref, block), my_channel(other_ref, block)
        target = pl.ds(place * pitch, lines)
        wide_ref[0, target, :] = jnp.where(first_is_mine, mine, other)
        wide_ref[1, target, :] = jnp.where(first_is_mine, other, mine)
    for core in range(2):
        for i in range(own):
            for half in range(HALVES):
                for q in range(2):
                    line = (i * HALVES + half) * 2 + q
                    target = pl.ds(core * own + i, sources, stride=2 * own)
                    signal_ref[q * HALVES + half, target, :] = wide_ref[
                        core, pl.ds(line, sources, stride=pitch), :
                    ]
    bits = grid_side.bit_length() - 1
    row_start = pl.multiple_of((tile >> bits) * side, side)
    col_start = pl.multiple_of((tile & (grid_side - 1)) * side, side)

    def inputs_from(start):
        planes = [signal_ref[plane, pl.ds(start, side), :] for plane in range(2 * HALVES)]
        return jnp.concatenate(planes, axis=1).astype(jnp.bfloat16)

    rows, cols = inputs_from(row_start), inputs_from(col_start)
    turned = jnp.concatenate([-rows[:, SPECTRA_SUMMED:], rows[:, :SPECTRA_SUMMED]], axis=1)
    product = lax.dot_general(
        jnp.concatenate([rows, turned], axis=0), cols, (((1,), (1,)), ((), ())),
        preferred_element_type=jnp.float32,
    )
    visible = (product * (1.0 / SPECTRA_SUMMED)).astype(jnp.bfloat16)
    for part in range(2):
        out_ref[0, 0, part] = visible[part * side : (part + 1) * side]


def on_device(voltages, fir_taps, channels, input_good_mask, tile_map):
    own = voltages.shape[1]
    chans = channels.shape[0]
    n_chan = lax.axis_size("chan")
    n_tile = lax.axis_size("tile")
    assert chans == n_chan and 2 * chans <= LANES and n_chan & (n_chan - 1) == 0
    chips = n_chan // 2
    order = [n_tile * chips - 1] + list(range(n_tile * chips - 1))
    groups = [[2 * place + (parity(place) ^ group) for place in order] for group in range(2)]
    x = voltages.reshape(own, FRAMES, BLOCKS, LANES).transpose(1, 2, 0, 3)
    operands = (channels.reshape(1, chans), input_good_mask, fir_taps, x)
    hbm = pl.BlockSpec(memory_space=pltpu.HBM)
    vmem = pl.BlockSpec(memory_space=pltpu.VMEM)
    per_block = 2 * HALVES * own
    kinds = 2 * chans
    folded_rows = SPECTRA_SUMMED + (LANES if kinds < LANES else 0)
    spectra = pl.pallas_call(
        functools.partial(front_kernel, own, chans, n_tile),
        out_shape=pltpu.VMEM((n_tile, chans * per_block, LANES), jnp.bfloat16),
        in_specs=[hbm, hbm, hbm, hbm],
        out_specs=vmem,
        scratch_shapes=[
            pltpu.VMEM((1, chans), jnp.int32),
            pltpu.VMEM(input_good_mask.shape, jnp.int32),
            pltpu.VMEM(fir_taps.shape, jnp.float32),
            pltpu.VMEM((DIRECT, ROWS, own, LANES), jnp.bfloat16),
            pltpu.VMEM((ROWS, BLOCKS - DIRECT, own, LANES), jnp.bfloat16),
            pltpu.VMEM((BLOCKS - DIRECT, ROWS * own, LANES), jnp.bfloat16),
            pltpu.VMEM((FILTER_TAPS * kinds, TRANSFORM_LENGTH), jnp.bfloat16),
            pltpu.VMEM((own * folded_rows, LANES), jnp.float32),
            pltpu.VMEM((chans * per_block, LANES), jnp.float32),
            pltpu.SemaphoreType.DMA((DIRECT + 2,)),
            pltpu.SemaphoreType.DMA((3,)),
        ],
        compiler_params=pltpu.CompilerParams(vmem_limit_bytes=32 << 20),
        name="front",
    )(*(pltpu.with_memory_space_constraint(v, pltpu.HBM) for v in operands))
    spectra = spectra.reshape(n_tile * chips, 2 * per_block, LANES)
    mine = lax.all_to_all(
        spectra, ("tile", "chan"), split_axis=0, concat_axis=0, axis_index_groups=groups, tiled=True
    )
    other = lax.ppermute(mine, "chan", [(c, c ^ 1) for c in range(n_chan)])
    grid_side = n_tile // 8 + 2
    inputs = n_tile * n_chan * own
    side = inputs // grid_side
    return pl.pallas_call(
        functools.partial(back_kernel, own, grid_side),
        out_shape=jax.ShapeDtypeStruct((1, 1, 2, side, side), jnp.bfloat16),
        in_specs=[vmem, vmem, vmem],
        out_specs=vmem,
        scratch_shapes=[
            pltpu.VMEM((2, n_tile * chips * (per_block + 1), LANES), jnp.float32),
            pltpu.VMEM((2 * HALVES, inputs, LANES), jnp.float32),
        ],
        compiler_params=pltpu.CompilerParams(vmem_limit_bytes=(4 << 20) + 60 * inputs * LANES * own),
        name="back",
    )(tile_map.T, mine, other)


def solution(mesh):
    in_specs = (P("tile", "chan", None), P(), P(), P("tile", "chan"), P())
    out_specs = P("chan", "tile", None, None, None)
    return jax.shard_map(
        on_device, mesh=mesh, in_specs=in_specs, out_specs=out_specs, check_vma=False
    )
```

```python
import functools
import math

import jax
import jax.numpy as jnp
from jax import lax
from jax.experimental import pallas as pl
from jax.experimental.pallas import tpu as pltpu
from jax.sharding import PartitionSpec as P

TRANSFORM_LENGTH = 2048
FILTER_TAPS = 16
SPECTRA_SUMMED = 256
FRAMES = SPECTRA_SUMMED + FILTER_TAPS - 1
ROWS = 272
LANES = 128
BLOCKS = TRANSFORM_LENGTH // LANES
DIRECT = 10
HALVES = SPECTRA_SUMMED // LANES
OCTANT = TRANSFORM_LENGTH // 8


def cos_sin(phase):
    turns = (phase + OCTANT) >> (OCTANT.bit_length())
    angle = (phase - (turns << OCTANT.bit_length())).astype(jnp.float32) * (2.0 * math.pi / TRANSFORM_LENGTH)
    square = angle * angle
    cosine, sine = jnp.zeros_like(angle), jnp.zeros_like(angle)
    for power in range(10, -1, -2):
        sign = -1.0 if power % 4 else 1.0
        cosine = cosine * square + sign / math.factorial(power)
        sine = sine * square + sign / math.factorial(power + 1)
    sine = sine * angle
    odd = (turns & 1) == 1
    first, second = jnp.where(odd, sine, cosine), jnp.where(odd, cosine, sine)
    first = jnp.where(((turns + 1) & 2) == 2, -first, first)
    second = jnp.where((turns & 2) == 2, -second, second)
    return first, second


def parity(place):
    return (place ^ (place >> 1) ^ (place >> 2)) & 1


def dft_blocks(chans, channels_ref):
    lane = lax.broadcasted_iota(jnp.int32, (chans, LANES), 1)
    place = lax.broadcasted_iota(jnp.int32, (chans, chans), 0)
    source = lax.broadcasted_iota(jnp.int32, (chans, chans), 1)
    turned = jnp.where(source == ((place + chans - 2) & (chans - 1)), channels_ref[...], 0)
    channel = jnp.sum(turned.astype(jnp.float32), axis=1, keepdims=True).astype(jnp.int32)
    channel = jnp.broadcast_to(channel, (chans, LANES))

    def unit(phase):
        return cos_sin(phase & (TRANSFORM_LENGTH - 1))

    factor = 1.0 / math.sqrt(TRANSFORM_LENGTH)
    cos0, sin0 = unit(channel * lane)
    blocks = [(cos0 * factor, sin0 * factor)]
    for bit in range(BLOCKS.bit_length() - 1):
        cos1, sin1 = unit(channel * (LANES << bit))
        blocks += [(c * cos1 - s * sin1, s * cos1 + c * sin1) for c, s in blocks]
    return [jnp.concatenate([cosine, -sine], axis=0) for cosine, sine in blocks]


def build_table(chans, blocks, taps_ref, table_ref):
    for nb, dft in enumerate(blocks):
        columns = slice(nb * LANES, (nb + 1) * LANES)
        for tap in range(FILTER_TAPS):
            table_ref[tap * 2 * chans : (tap + 1) * 2 * chans, columns] = (
                dft * taps_ref[tap : tap + 1, columns]
            ).astype(jnp.bfloat16)


def front_kernel(
    own, chans, copies, channels_hbm, mask_hbm, taps_hbm, x_hbm, out_ref,
    channels_ref, mask_ref, taps_ref, x_ref, rest_ref, sorted_ref, table_ref, fold_ref, block_ref,
    sems, small_sems,
):
    small = [
        pltpu.make_async_copy(source, target, small_sems.at[place])
        for place, (source, target) in enumerate(
            ((taps_hbm, taps_ref), (channels_hbm, channels_ref), (mask_hbm, mask_ref))
        )
    ]
    transfers = [
        pltpu.make_async_copy(x_hbm.at[:, nb], x_ref.at[nb, pl.ds(0, FRAMES)], sems.at[nb])
        for nb in range(DIRECT)
    ]
    halves = ((0, ROWS // 2), (ROWS // 2, FRAMES))
    rest = [
        pltpu.make_async_copy(
            x_hbm.at[pl.ds(start, stop - start), pl.ds(DIRECT, BLOCKS - DIRECT)],
            rest_ref.at[pl.ds(start, stop - start)],
            sems.at[DIRECT + part],
        )
        for part, (start, stop) in enumerate(halves)
    ]
    for transfer in small:
        transfer.start()
    for place, transfer in enumerate(rest + transfers):
        transfer.start(priority=place % 2)
    small[1].wait()
    blocks = dft_blocks(chans, channels_ref)
    small[0].wait()
    small[2].wait()
    build_table(chans, blocks, taps_ref, table_ref)
    for part, transfer in enumerate(rest):
        transfer.wait()
        frames = pl.ds(part * (ROWS // 2), ROWS // 2)
        lines = pl.ds(part * (ROWS // 2) * own, ROWS // 2 * own)
        for place in range(BLOCKS - DIRECT):
            sorted_ref[place, lines, :] = rest_ref[frames, place].reshape(ROWS // 2 * own, LANES)
    rows_ref = x_ref.reshape(DIRECT, ROWS * own, LANES)
    for transfer in transfers:
        transfer.wait()
    product = lax.dot_general(
        jnp.concatenate(
            [rows_ref[nb] for nb in range(DIRECT)]
            + [sorted_ref[place] for place in range(BLOCKS - DIRECT)],
            axis=1,
        ),
        table_ref[...],
        (((1,), (1,)), ((), ())),
        preferred_element_type=jnp.float32,
    )
    kinds = 2 * chans
    together = LANES // kinds
    kept = -(-(SPECTRA_SUMMED + together - 1) // 8) * 8
    folded = product[: kept * own, :LANES]
    for group in range(1, FILTER_TAPS // together):
        start = group * together * own
        folded = folded + product[
            start : start + kept * own, group * LANES : (group + 1) * LANES
        ]
    fold_ref[...] = folded
    for i in range(own):
        turned = fold_ref[pl.ds(i, kept, stride=own), :].T
        spectra = turned[:kinds, :SPECTRA_SUMMED]
        for tap in range(1, together):
            spectra = spectra + turned[
                tap * kinds : (tap + 1) * kinds, tap : tap + SPECTRA_SUMMED
            ]
        spectra = spectra * mask_ref[:, i : i + 1].astype(jnp.float32)
        for half in range(HALVES):
            for q in range(2):
                block_ref[pl.ds((i * HALVES + half) * 2 + q, chans, stride=4 * own), :] = spectra[
                    q * chans : (q + 1) * chans, half * LANES : (half + 1) * LANES
                ]
    block = block_ref[...].astype(jnp.bfloat16)
    for copy in range(copies):
        out_ref[copy] = block


def back_kernel(
    own, grid_side, tile_map_ref, mine_ref, other_ref, out_ref, wide_ref, signal_ref
):
    slot = lax.broadcasted_iota(jnp.int32, tile_map_ref.shape, 0)
    owner = lax.broadcasted_iota(jnp.int32, tile_map_ref.shape, 1)
    wanted = (slot == lax.axis_index("tile")) & (owner == lax.axis_index("chan"))
    tile = jnp.sum(jnp.where(wanted, tile_map_ref[...].astype(jnp.float32), 0.0)).astype(jnp.int32)
    sources = mine_ref.shape[0]
    inputs = sources * 2 * own
    side = inputs // grid_side
    lines = mine_ref.shape[1] // 2
    pitch = lines + 1
    chan = lax.axis_index("chan")
    core_here = chan & 1
    place_here = lax.axis_index("tile") * (lax.axis_size("chan") // 2) + (chan >> 1)
    group_here = core_here ^ parity(place_here)

    def my_channel(blocks_ref, block):
        both = blocks_ref[block].astype(jnp.float32)
        return jnp.where(core_here == 0, both[:lines], both[lines:])

    for block in range(sources):
        place = (block - 1) % sources
        first_is_mine = group_here == parity(place)
        mine, other = my_channel(mine_ref, block), my_channel(other_ref, block)
        target = pl.ds(place * pitch, lines)
        wide_ref[0, target, :] = jnp.where(first_is_mine, mine, other)
        wide_ref[1, target, :] = jnp.where(first_is_mine, other, mine)
    for core in range(2):
        for i in range(own):
            for half in range(HALVES):
                for q in range(2):
                    line = (i * HALVES + half) * 2 + q
                    target = pl.ds(core * own + i, sources, stride=2 * own)
                    signal_ref[q * HALVES + half, target, :] = wide_ref[
                        core, pl.ds(line, sources, stride=pitch), :
                    ]
    bits = grid_side.bit_length() - 1
    row_start = pl.multiple_of((tile >> bits) * side, side)
    col_start = pl.multiple_of((tile & (grid_side - 1)) * side, side)

    def inputs_from(start):
        planes = [signal_ref[plane, pl.ds(start, side), :] for plane in range(2 * HALVES)]
        return jnp.concatenate(planes, axis=1).astype(jnp.bfloat16)

    rows, cols = inputs_from(row_start), inputs_from(col_start)
    turned = jnp.concatenate([-rows[:, SPECTRA_SUMMED:], rows[:, :SPECTRA_SUMMED]], axis=1)
    product = lax.dot_general(
        jnp.concatenate([rows, turned], axis=0), cols, (((1,), (1,)), ((), ())),
        preferred_element_type=jnp.float32,
    )
    visible = (product * (1.0 / SPECTRA_SUMMED)).astype(jnp.bfloat16)
    for part in range(2):
        out_ref[0, 0, part] = visible[part * side : (part + 1) * side]


def on_device(voltages, fir_taps, channels, input_good_mask, tile_map):
    own = voltages.shape[1]
    chans = channels.shape[0]
    n_chan = lax.axis_size("chan")
    n_tile = lax.axis_size("tile")
    assert chans == n_chan and 2 * chans <= LANES and n_chan & (n_chan - 1) == 0
    chips = n_chan // 2
    order = [n_tile * chips - 1] + list(range(n_tile * chips - 1))
    groups = [[2 * place + (parity(place) ^ group) for place in order] for group in range(2)]
    x = voltages.reshape(own, FRAMES, BLOCKS, LANES).transpose(1, 2, 0, 3)
    operands = (channels.reshape(1, chans), input_good_mask, fir_taps, x)
    hbm = pl.BlockSpec(memory_space=pltpu.HBM)
    vmem = pl.BlockSpec(memory_space=pltpu.VMEM)
    per_block = 2 * HALVES * own
    kinds = 2 * chans
    folded_rows = -(-(SPECTRA_SUMMED + LANES // kinds - 1) // 8) * 8
    spectra = pl.pallas_call(
        functools.partial(front_kernel, own, chans, n_tile),
        out_shape=pltpu.VMEM((n_tile, chans * per_block, LANES), jnp.bfloat16),
        in_specs=[hbm, hbm, hbm, hbm],
        out_specs=vmem,
        scratch_shapes=[
            pltpu.VMEM((1, chans), jnp.int32),
            pltpu.VMEM(input_good_mask.shape, jnp.int32),
            pltpu.VMEM(fir_taps.shape, jnp.float32),
            pltpu.VMEM((DIRECT, ROWS, own, LANES), jnp.bfloat16),
            pltpu.VMEM((ROWS, BLOCKS - DIRECT, own, LANES), jnp.bfloat16),
            pltpu.VMEM((BLOCKS - DIRECT, ROWS * own, LANES), jnp.bfloat16),
            pltpu.VMEM((FILTER_TAPS * kinds, TRANSFORM_LENGTH), jnp.bfloat16),
            pltpu.VMEM((own * folded_rows, LANES), jnp.float32),
            pltpu.VMEM((chans * per_block, LANES), jnp.float32),
            pltpu.SemaphoreType.DMA((DIRECT + 2,)),
            pltpu.SemaphoreType.DMA((3,)),
        ],
        compiler_params=pltpu.CompilerParams(vmem_limit_bytes=32 << 20),
        name="front",
    )(*(pltpu.with_memory_space_constraint(v, pltpu.HBM) for v in operands))
    spectra = spectra.reshape(n_tile * chips, 2 * per_block, LANES)
    mine = lax.all_to_all(
        spectra, ("tile", "chan"), split_axis=0, concat_axis=0, axis_index_groups=groups, tiled=True
    )
    other = lax.ppermute(mine, "chan", [(c, c ^ 1) for c in range(n_chan)])
    grid_side = n_tile // 8 + 2
    inputs = n_tile * n_chan * own
    side = inputs // grid_side
    return pl.pallas_call(
        functools.partial(back_kernel, own, grid_side),
        out_shape=jax.ShapeDtypeStruct((1, 1, 2, side, side), jnp.bfloat16),
        in_specs=[vmem, vmem, vmem],
        out_specs=vmem,
        scratch_shapes=[
            pltpu.VMEM((2, n_tile * chips * (per_block + 1), LANES), jnp.float32),
            pltpu.VMEM((2 * HALVES, inputs, LANES), jnp.float32),
        ],
        compiler_params=pltpu.CompilerParams(vmem_limit_bytes=(4 << 20) + 60 * inputs * LANES * own),
        name="back",
    )(tile_map.T, mine, other)


def solution(mesh):
    in_specs = (P("tile", "chan", None), P(), P(), P("tile", "chan"), P())
    out_specs = P("chan", "tile", None, None, None)
    return jax.shard_map(
        on_device, mesh=mesh, in_specs=in_specs, out_specs=out_specs, check_vma=False
    )
```

```python
import functools
import math

import jax
import jax.numpy as jnp
from jax import lax
from jax.experimental import pallas as pl
from jax.experimental.pallas import tpu as pltpu
from jax.sharding import PartitionSpec as P

TRANSFORM_LENGTH = 2048
FILTER_TAPS = 16
SPECTRA_SUMMED = 256
FRAMES = SPECTRA_SUMMED + FILTER_TAPS - 1
ROWS = 272
LANES = 128
BLOCKS = TRANSFORM_LENGTH // LANES
DIRECT = 10
EARLY = 5
HALVES = SPECTRA_SUMMED // LANES
OCTANT = TRANSFORM_LENGTH // 8


def cos_sin(phase):
    turns = (phase + OCTANT) >> (OCTANT.bit_length())
    angle = (phase - (turns << OCTANT.bit_length())).astype(jnp.float32) * (2.0 * math.pi / TRANSFORM_LENGTH)
    square = angle * angle
    cosine, sine = jnp.zeros_like(angle), jnp.zeros_like(angle)
    for power in range(10, -1, -2):
        sign = -1.0 if power % 4 else 1.0
        cosine = cosine * square + sign / math.factorial(power)
        sine = sine * square + sign / math.factorial(power + 1)
    sine = sine * angle
    odd = (turns & 1) == 1
    first, second = jnp.where(odd, sine, cosine), jnp.where(odd, cosine, sine)
    first = jnp.where(((turns + 1) & 2) == 2, -first, first)
    second = jnp.where((turns & 2) == 2, -second, second)
    return first, second


def parity(place):
    return (place ^ (place >> 1) ^ (place >> 2)) & 1


def dft_blocks(chans, channels_ref):
    lane = lax.broadcasted_iota(jnp.int32, (chans, LANES), 1)
    place = lax.broadcasted_iota(jnp.int32, (chans, chans), 0)
    source = lax.broadcasted_iota(jnp.int32, (chans, chans), 1)
    turned = jnp.where(source == ((place + chans - 2) & (chans - 1)), channels_ref[...], 0)
    channel = jnp.sum(turned.astype(jnp.float32), axis=1, keepdims=True).astype(jnp.int32)
    channel = jnp.broadcast_to(channel, (chans, LANES))

    def unit(phase):
        return cos_sin(phase & (TRANSFORM_LENGTH - 1))

    factor = 1.0 / math.sqrt(TRANSFORM_LENGTH)
    cos0, sin0 = unit(channel * lane)
    blocks = [(cos0 * factor, sin0 * factor)]
    for bit in range(BLOCKS.bit_length() - 1):
        cos1, sin1 = unit(channel * (LANES << bit))
        blocks += [(c * cos1 - s * sin1, s * cos1 + c * sin1) for c, s in blocks]
    return [jnp.concatenate([cosine, -sine], axis=0) for cosine, sine in blocks]


def build_table(chans, blocks, taps_ref, table_ref):
    for nb, dft in enumerate(blocks):
        columns = slice(nb * LANES, (nb + 1) * LANES)
        for tap in range(FILTER_TAPS):
            table_ref[tap * 2 * chans : (tap + 1) * 2 * chans, columns] = (
                dft * taps_ref[tap : tap + 1, columns]
            ).astype(jnp.bfloat16)


def front_kernel(
    own, chans, copies, channels_hbm, mask_hbm, taps_hbm, x_hbm, out_ref,
    channels_ref, mask_ref, taps_ref, x_ref, rest_ref, sorted_ref, table_ref, fold_ref, block_ref,
    sems, small_sems,
):
    small = [
        pltpu.make_async_copy(source, target, small_sems.at[place])
        for place, (source, target) in enumerate(
            ((taps_hbm, taps_ref), (channels_hbm, channels_ref), (mask_hbm, mask_ref))
        )
    ]
    transfers = [
        pltpu.make_async_copy(x_hbm.at[:, nb], x_ref.at[nb, pl.ds(0, FRAMES)], sems.at[nb])
        for nb in range(DIRECT)
    ]
    halves = ((0, ROWS // 2), (ROWS // 2, FRAMES))
    rest = [
        pltpu.make_async_copy(
            x_hbm.at[pl.ds(start, stop - start), pl.ds(DIRECT, BLOCKS - DIRECT)],
            rest_ref.at[pl.ds(start, stop - start)],
            sems.at[DIRECT + part],
        )
        for part, (start, stop) in enumerate(halves)
    ]
    for transfer in small:
        transfer.start()
    for place, transfer in enumerate(rest + transfers[:EARLY]):
        transfer.start(priority=place % 2)
    small[1].wait()
    blocks = dft_blocks(chans, channels_ref)
    small[0].wait()
    small[2].wait()
    for place, transfer in enumerate(transfers[EARLY:]):
        transfer.start(priority=place % 2)
    build_table(chans, blocks, taps_ref, table_ref)
    for part, transfer in enumerate(rest):
        transfer.wait()
        frames = pl.ds(part * (ROWS // 2), ROWS // 2)
        lines = pl.ds(part * (ROWS // 2) * own, ROWS // 2 * own)
        for place in range(BLOCKS - DIRECT):
            sorted_ref[place, lines, :] = rest_ref[frames, place].reshape(ROWS // 2 * own, LANES)
    rows_ref = x_ref.reshape(DIRECT, ROWS * own, LANES)

    def product_of(parts, *columns):
        table = jnp.concatenate([table_ref[:, part] for part in columns], axis=1)
        return lax.dot_general(
            jnp.concatenate(parts, axis=1), table, (((1,), (1,)), ((), ())),
            preferred_element_type=jnp.float32,
        )

    for transfer in transfers[:EARLY]:
        transfer.wait()
    product = product_of(
        [rows_ref[nb] for nb in range(EARLY)]
        + [sorted_ref[place] for place in range(BLOCKS - DIRECT)],
        slice(0, EARLY * LANES),
        slice(DIRECT * LANES, BLOCKS * LANES),
    )
    for transfer in transfers[EARLY:]:
        transfer.wait()
    product = product + product_of(
        [rows_ref[nb] for nb in range(EARLY, DIRECT)], slice(EARLY * LANES, DIRECT * LANES)
    )
    kinds = 2 * chans
    together = LANES // kinds
    kept = -(-(SPECTRA_SUMMED + together - 1) // 8) * 8
    folded = product[: kept * own, :LANES]
    for group in range(1, FILTER_TAPS // together):
        start = group * together * own
        folded = folded + product[
            start : start + kept * own, group * LANES : (group + 1) * LANES
        ]
    fold_ref[: kept * own, :] = folded
    for i in range(own):
        turned = fold_ref[pl.ds(i, fold_ref.shape[0] // own, stride=own), :].T
        spectra = turned[:kinds, :SPECTRA_SUMMED]
        for tap in range(1, together):
            shifted = pltpu.roll(
                turned[tap * kinds : (tap + 1) * kinds, :], turned.shape[1] - tap, axis=1
            )
            spectra = spectra + shifted[:, :SPECTRA_SUMMED]
        spectra = spectra * mask_ref[:, i : i + 1].astype(jnp.float32)
        for half in range(HALVES):
            for q in range(2):
                block_ref[pl.ds((i * HALVES + half) * 2 + q, chans, stride=4 * own), :] = spectra[
                    q * chans : (q + 1) * chans, half * LANES : (half + 1) * LANES
                ]
    block = block_ref[...].astype(jnp.bfloat16)
    for copy in range(copies):
        out_ref[copy] = block


def back_kernel(
    own, grid_side, tile_map_ref, mine_ref, other_ref, out_ref, wide_ref, signal_ref
):
    slot = lax.broadcasted_iota(jnp.int32, tile_map_ref.shape, 0)
    owner = lax.broadcasted_iota(jnp.int32, tile_map_ref.shape, 1)
    wanted = (slot == lax.axis_index("tile")) & (owner == lax.axis_index("chan"))
    tile = jnp.sum(jnp.where(wanted, tile_map_ref[...].astype(jnp.float32), 0.0)).astype(jnp.int32)
    sources = mine_ref.shape[0]
    inputs = sources * 2 * own
    side = inputs // grid_side
    lines = mine_ref.shape[1] // 2
    pitch = lines + 1
    chan = lax.axis_index("chan")
    core_here = chan & 1
    place_here = lax.axis_index("tile") * (lax.axis_size("chan") // 2) + (chan >> 1)
    group_here = core_here ^ parity(place_here)

    def my_channel(blocks_ref, block):
        both = blocks_ref[block].astype(jnp.float32)
        return jnp.where(core_here == 0, both[:lines], both[lines:])

    for block in range(sources):
        place = (block - 1) % sources
        first_is_mine = group_here == parity(place)
        mine, other = my_channel(mine_ref, block), my_channel(other_ref, block)
        target = pl.ds(place * pitch, lines)
        wide_ref[0, target, :] = jnp.where(first_is_mine, mine, other)
        wide_ref[1, target, :] = jnp.where(first_is_mine, other, mine)
    for core in range(2):
        for i in range(own):
            for half in range(HALVES):
                for q in range(2):
                    line = (i * HALVES + half) * 2 + q
                    target = pl.ds(core * own + i, sources, stride=2 * own)
                    signal_ref[q * HALVES + half, target, :] = wide_ref[
                        core, pl.ds(line, sources, stride=pitch), :
                    ]
    bits = grid_side.bit_length() - 1
    row_start = pl.multiple_of((tile >> bits) * side, side)
    col_start = pl.multiple_of((tile & (grid_side - 1)) * side, side)

    def inputs_from(start):
        planes = [signal_ref[plane, pl.ds(start, side), :] for plane in range(2 * HALVES)]
        return jnp.concatenate(planes, axis=1).astype(jnp.bfloat16)

    rows, cols = inputs_from(row_start), inputs_from(col_start)
    turned = jnp.concatenate([-rows[:, SPECTRA_SUMMED:], rows[:, :SPECTRA_SUMMED]], axis=1)
    product = lax.dot_general(
        jnp.concatenate([rows, turned], axis=0), cols, (((1,), (1,)), ((), ())),
        preferred_element_type=jnp.float32,
    )
    visible = (product * (1.0 / SPECTRA_SUMMED)).astype(jnp.bfloat16)
    for part in range(2):
        out_ref[0, 0, part] = visible[part * side : (part + 1) * side]


def on_device(voltages, fir_taps, channels, input_good_mask, tile_map):
    own = voltages.shape[1]
    chans = channels.shape[0]
    n_chan = lax.axis_size("chan")
    n_tile = lax.axis_size("tile")
    assert chans == n_chan and 2 * chans <= LANES and n_chan & (n_chan - 1) == 0
    chips = n_chan // 2
    order = [n_tile * chips - 1] + list(range(n_tile * chips - 1))
    groups = [[2 * place + (parity(place) ^ group) for place in order] for group in range(2)]
    x = voltages.reshape(own, FRAMES, BLOCKS, LANES).transpose(1, 2, 0, 3)
    operands = (channels.reshape(1, chans), input_good_mask, fir_taps, x)
    hbm = pl.BlockSpec(memory_space=pltpu.HBM)
    vmem = pl.BlockSpec(memory_space=pltpu.VMEM)
    per_block = 2 * HALVES * own
    kinds = 2 * chans
    folded_rows = SPECTRA_SUMMED + (LANES if kinds < LANES else 0)
    spectra = pl.pallas_call(
        functools.partial(front_kernel, own, chans, n_tile),
        out_shape=pltpu.VMEM((n_tile, chans * per_block, LANES), jnp.bfloat16),
        in_specs=[hbm, hbm, hbm, hbm],
        out_specs=vmem,
        scratch_shapes=[
            pltpu.VMEM((1, chans), jnp.int32),
            pltpu.VMEM(input_good_mask.shape, jnp.int32),
            pltpu.VMEM(fir_taps.shape, jnp.float32),
            pltpu.VMEM((DIRECT, ROWS, own, LANES), jnp.bfloat16),
            pltpu.VMEM((ROWS, BLOCKS - DIRECT, own, LANES), jnp.bfloat16),
            pltpu.VMEM((BLOCKS - DIRECT, ROWS * own, LANES), jnp.bfloat16),
            pltpu.VMEM((FILTER_TAPS * kinds, TRANSFORM_LENGTH), jnp.bfloat16),
            pltpu.VMEM((own * folded_rows, LANES), jnp.float32),
            pltpu.VMEM((chans * per_block, LANES), jnp.float32),
            pltpu.SemaphoreType.DMA((DIRECT + 2,)),
            pltpu.SemaphoreType.DMA((3,)),
        ],
        compiler_params=pltpu.CompilerParams(vmem_limit_bytes=32 << 20),
        name="front",
    )(*(pltpu.with_memory_space_constraint(v, pltpu.HBM) for v in operands))
    spectra = spectra.reshape(n_tile * chips, 2 * per_block, LANES)
    mine = lax.all_to_all(
        spectra, ("tile", "chan"), split_axis=0, concat_axis=0, axis_index_groups=groups, tiled=True
    )
    other = lax.ppermute(mine, "chan", [(c, c ^ 1) for c in range(n_chan)])
    grid_side = n_tile // 8 + 2
    inputs = n_tile * n_chan * own
    side = inputs // grid_side
    return pl.pallas_call(
        functools.partial(back_kernel, own, grid_side),
        out_shape=jax.ShapeDtypeStruct((1, 1, 2, side, side), jnp.bfloat16),
        in_specs=[vmem, vmem, vmem],
        out_specs=vmem,
        scratch_shapes=[
            pltpu.VMEM((2, n_tile * chips * (per_block + 1), LANES), jnp.float32),
            pltpu.VMEM((2 * HALVES, inputs, LANES), jnp.float32),
        ],
        compiler_params=pltpu.CompilerParams(vmem_limit_bytes=(4 << 20) + 60 * inputs * LANES * own),
        name="back",
    )(tile_map.T, mine, other)


def solution(mesh):
    in_specs = (P("tile", "chan", None), P(), P(), P("tile", "chan"), P())
    out_specs = P("chan", "tile", None, None, None)
    return jax.shard_map(
        on_device, mesh=mesh, in_specs=in_specs, out_specs=out_specs, check_vma=False
    )
```

```python
import functools
import math

import jax
import jax.numpy as jnp
from jax import lax
from jax.experimental import pallas as pl
from jax.experimental.pallas import tpu as pltpu
from jax.sharding import PartitionSpec as P

TRANSFORM_LENGTH = 2048
FILTER_TAPS = 16
SPECTRA_SUMMED = 256
FRAMES = SPECTRA_SUMMED + FILTER_TAPS - 1
ROWS = 272
LANES = 128
BLOCKS = TRANSFORM_LENGTH // LANES
DIRECT = 10
HALVES = SPECTRA_SUMMED // LANES
OCTANT = TRANSFORM_LENGTH // 8


def cos_sin(phase):
    turns = (phase + OCTANT) >> (OCTANT.bit_length())
    angle = (phase - (turns << OCTANT.bit_length())).astype(jnp.float32) * (2.0 * math.pi / TRANSFORM_LENGTH)
    square = angle * angle
    cosine, sine = jnp.zeros_like(angle), jnp.zeros_like(angle)
    for power in range(10, -1, -2):
        sign = -1.0 if power % 4 else 1.0
        cosine = cosine * square + sign / math.factorial(power)
        sine = sine * square + sign / math.factorial(power + 1)
    sine = sine * angle
    odd = (turns & 1) == 1
    first, second = jnp.where(odd, sine, cosine), jnp.where(odd, cosine, sine)
    first = jnp.where(((turns + 1) & 2) == 2, -first, first)
    second = jnp.where((turns & 2) == 2, -second, second)
    return first, second


def parity(place):
    return (place ^ (place >> 1) ^ (place >> 2)) & 1


def dft_blocks(chans, channels_ref):
    lane = lax.broadcasted_iota(jnp.int32, (chans, LANES), 1)
    place = lax.broadcasted_iota(jnp.int32, (chans, chans), 0)
    source = lax.broadcasted_iota(jnp.int32, (chans, chans), 1)
    turned = jnp.where(source == ((place + chans - 2) & (chans - 1)), channels_ref[...], 0)
    channel = jnp.sum(turned.astype(jnp.float32), axis=1, keepdims=True).astype(jnp.int32)
    channel = jnp.broadcast_to(channel, (chans, LANES))

    def unit(phase):
        return cos_sin(phase & (TRANSFORM_LENGTH - 1))

    factor = 1.0 / math.sqrt(TRANSFORM_LENGTH)
    cos0, sin0 = unit(channel * lane)
    blocks = [(cos0 * factor, sin0 * factor)]
    for bit in range(BLOCKS.bit_length() - 1):
        cos1, sin1 = unit(channel * (LANES << bit))
        blocks += [(c * cos1 - s * sin1, s * cos1 + c * sin1) for c, s in blocks]
    return [jnp.concatenate([cosine, -sine], axis=0) for cosine, sine in blocks]


def build_table(chans, blocks, taps_ref, table_ref):
    for nb, dft in enumerate(blocks):
        columns = slice(nb * LANES, (nb + 1) * LANES)
        for tap in range(FILTER_TAPS):
            table_ref[tap * 2 * chans : (tap + 1) * 2 * chans, columns] = (
                dft * taps_ref[tap : tap + 1, columns]
            ).astype(jnp.bfloat16)


def front_kernel(
    own, chans, copies, channels_hbm, mask_hbm, taps_hbm, x_hbm, out_ref,
    channels_ref, mask_ref, taps_ref, x_ref, rest_ref, sorted_ref, table_ref, fold_ref, block_ref,
    sems, small_sems,
):
    small = [
        pltpu.make_async_copy(source, target, small_sems.at[place])
        for place, (source, target) in enumerate(
            ((taps_hbm, taps_ref), (channels_hbm, channels_ref), (mask_hbm, mask_ref))
        )
    ]
    transfers = [
        pltpu.make_async_copy(x_hbm.at[:, nb], x_ref.at[nb, pl.ds(0, FRAMES)], sems.at[nb])
        for nb in range(DIRECT)
    ]
    halves = ((0, ROWS // 2), (ROWS // 2, FRAMES))
    rest = [
        pltpu.make_async_copy(
            x_hbm.at[pl.ds(start, stop - start), pl.ds(DIRECT, BLOCKS - DIRECT)],
            rest_ref.at[pl.ds(start, stop - start)],
            sems.at[DIRECT + part],
        )
        for part, (start, stop) in enumerate(halves)
    ]
    for place, transfer in enumerate(rest + transfers):
        transfer.start(priority=place % 2)
    for transfer in small:
        transfer.start()
    small[1].wait()
    blocks = dft_blocks(chans, channels_ref)
    small[0].wait()
    small[2].wait()
    build_table(chans, blocks, taps_ref, table_ref)
    for part, transfer in enumerate(rest):
        transfer.wait()
        frames = pl.ds(part * (ROWS // 2), ROWS // 2)
        lines = pl.ds(part * (ROWS // 2) * own, ROWS // 2 * own)
        for place in range(BLOCKS - DIRECT):
            sorted_ref[place, lines, :] = rest_ref[frames, place].reshape(ROWS // 2 * own, LANES)
    rows_ref = x_ref.reshape(DIRECT, ROWS * own, LANES)
    for transfer in transfers:
        transfer.wait()
    product = lax.dot_general(
        jnp.concatenate(
            [rows_ref[nb] for nb in range(DIRECT)]
            + [sorted_ref[place] for place in range(BLOCKS - DIRECT)],
            axis=1,
        ),
        table_ref[...],
        (((1,), (1,)), ((), ())),
        preferred_element_type=jnp.float32,
    )
    kinds = 2 * chans
    together = LANES // kinds
    kept = -(-(SPECTRA_SUMMED + together - 1) // 8) * 8
    folded = product[: kept * own, :LANES]
    for group in range(1, FILTER_TAPS // together):
        start = group * together * own
        folded = folded + product[
            start : start + kept * own, group * LANES : (group + 1) * LANES
        ]
    fold_ref[: kept * own, :] = folded
    for i in range(own):
        turned = fold_ref[pl.ds(i, fold_ref.shape[0] // own, stride=own), :].T
        spectra = turned[:kinds, :SPECTRA_SUMMED]
        for tap in range(1, together):
            shifted = pltpu.roll(
                turned[tap * kinds : (tap + 1) * kinds, :], turned.shape[1] - tap, axis=1
            )
            spectra = spectra + shifted[:, :SPECTRA_SUMMED]
        spectra = spectra * mask_ref[:, i : i + 1].astype(jnp.float32)
        for half in range(HALVES):
            for q in range(2):
                block_ref[pl.ds((i * HALVES + half) * 2 + q, chans, stride=4 * own), :] = spectra[
                    q * chans : (q + 1) * chans, half * LANES : (half + 1) * LANES
                ]
    block = block_ref[...].astype(jnp.bfloat16)
    for copy in range(copies):
        out_ref[copy] = block


def back_kernel(
    own, grid_side, tile_map_ref, mine_ref, other_ref, out_ref, wide_ref, signal_ref
):
    slot = lax.broadcasted_iota(jnp.int32, tile_map_ref.shape, 0)
    owner = lax.broadcasted_iota(jnp.int32, tile_map_ref.shape, 1)
    wanted = (slot == lax.axis_index("tile")) & (owner == lax.axis_index("chan"))
    tile = jnp.sum(jnp.where(wanted, tile_map_ref[...].astype(jnp.float32), 0.0)).astype(jnp.int32)
    sources = mine_ref.shape[0]
    inputs = sources * 2 * own
    side = inputs // grid_side
    lines = mine_ref.shape[1] // 2
    pitch = lines + 1
    chan = lax.axis_index("chan")
    core_here = chan & 1
    place_here = lax.axis_index("tile") * (lax.axis_size("chan") // 2) + (chan >> 1)
    group_here = core_here ^ parity(place_here)

    def my_channel(blocks_ref, block):
        both = blocks_ref[block].astype(jnp.float32)
        return jnp.where(core_here == 0, both[:lines], both[lines:])

    for block in range(sources):
        place = (block - 1) % sources
        first_is_mine = group_here == parity(place)
        mine, other = my_channel(mine_ref, block), my_channel(other_ref, block)
        target = pl.ds(place * pitch, lines)
        wide_ref[0, target, :] = jnp.where(first_is_mine, mine, other)
        wide_ref[1, target, :] = jnp.where(first_is_mine, other, mine)
    for core in range(2):
        for i in range(own):
            for half in range(HALVES):
                for q in range(2):
                    line = (i * HALVES + half) * 2 + q
                    target = pl.ds(core * own + i, sources, stride=2 * own)
                    signal_ref[q * HALVES + half, target, :] = wide_ref[
                        core, pl.ds(line, sources, stride=pitch), :
                    ]
    bits = grid_side.bit_length() - 1
    row_start = pl.multiple_of((tile >> bits) * side, side)
    col_start = pl.multiple_of((tile & (grid_side - 1)) * side, side)

    def inputs_from(start):
        planes = [signal_ref[plane, pl.ds(start, side), :] for plane in range(2 * HALVES)]
        return jnp.concatenate(planes, axis=1).astype(jnp.bfloat16)

    rows, cols = inputs_from(row_start), inputs_from(col_start)
    turned = jnp.concatenate([-rows[:, SPECTRA_SUMMED:], rows[:, :SPECTRA_SUMMED]], axis=1)
    product = lax.dot_general(
        jnp.concatenate([rows, turned], axis=0), cols, (((1,), (1,)), ((), ())),
        preferred_element_type=jnp.float32,
    )
    visible = (product * (1.0 / SPECTRA_SUMMED)).astype(jnp.bfloat16)
    for part in range(2):
        out_ref[0, 0, part] = visible[part * side : (part + 1) * side]


def on_device(voltages, fir_taps, channels, input_good_mask, tile_map):
    own = voltages.shape[1]
    chans = channels.shape[0]
    n_chan = lax.axis_size("chan")
    n_tile = lax.axis_size("tile")
    assert chans == n_chan and 2 * chans <= LANES and n_chan & (n_chan - 1) == 0
    chips = n_chan // 2
    order = [n_tile * chips - 1] + list(range(n_tile * chips - 1))
    groups = [[2 * place + (parity(place) ^ group) for place in order] for group in range(2)]
    x = voltages.reshape(own, FRAMES, BLOCKS, LANES).transpose(1, 2, 0, 3)
    operands = (channels.reshape(1, chans), input_good_mask, fir_taps, x)
    hbm = pl.BlockSpec(memory_space=pltpu.HBM)
    vmem = pl.BlockSpec(memory_space=pltpu.VMEM)
    per_block = 2 * HALVES * own
    kinds = 2 * chans
    folded_rows = SPECTRA_SUMMED + (LANES if kinds < LANES else 0)
    spectra = pl.pallas_call(
        functools.partial(front_kernel, own, chans, n_tile),
        out_shape=pltpu.VMEM((n_tile, chans * per_block, LANES), jnp.bfloat16),
        in_specs=[hbm, hbm, hbm, hbm],
        out_specs=vmem,
        scratch_shapes=[
            pltpu.VMEM((1, chans), jnp.int32),
            pltpu.VMEM(input_good_mask.shape, jnp.int32),
            pltpu.VMEM(fir_taps.shape, jnp.float32),
            pltpu.VMEM((DIRECT, ROWS, own, LANES), jnp.bfloat16),
            pltpu.VMEM((ROWS, BLOCKS - DIRECT, own, LANES), jnp.bfloat16),
            pltpu.VMEM((BLOCKS - DIRECT, ROWS * own, LANES), jnp.bfloat16),
            pltpu.VMEM((FILTER_TAPS * kinds, TRANSFORM_LENGTH), jnp.bfloat16),
            pltpu.VMEM((own * folded_rows, LANES), jnp.float32),
            pltpu.VMEM((chans * per_block, LANES), jnp.float32),
            pltpu.SemaphoreType.DMA((DIRECT + 2,)),
            pltpu.SemaphoreType.DMA((3,)),
        ],
        compiler_params=pltpu.CompilerParams(vmem_limit_bytes=32 << 20),
        name="front",
    )(*(pltpu.with_memory_space_constraint(v, pltpu.HBM) for v in operands))
    spectra = spectra.reshape(n_tile * chips, 2 * per_block, LANES)
    mine = lax.all_to_all(
        spectra, ("tile", "chan"), split_axis=0, concat_axis=0, axis_index_groups=groups, tiled=True
    )
    other = lax.ppermute(mine, "chan", [(c, c ^ 1) for c in range(n_chan)])
    grid_side = n_tile // 8 + 2
    inputs = n_tile * n_chan * own
    side = inputs // grid_side
    return pl.pallas_call(
        functools.partial(back_kernel, own, grid_side),
        out_shape=jax.ShapeDtypeStruct((1, 1, 2, side, side), jnp.bfloat16),
        in_specs=[vmem, vmem, vmem],
        out_specs=vmem,
        scratch_shapes=[
            pltpu.VMEM((2, n_tile * chips * (per_block + 1), LANES), jnp.float32),
            pltpu.VMEM((2 * HALVES, inputs, LANES), jnp.float32),
        ],
        compiler_params=pltpu.CompilerParams(vmem_limit_bytes=(4 << 20) + 60 * inputs * LANES * own),
        name="back",
    )(tile_map.T, mine, other)


def solution(mesh):
    in_specs = (P("tile", "chan", None), P(), P(), P("tile", "chan"), P())
    out_specs = P("chan", "tile", None, None, None)
    return jax.shard_map(
        on_device, mesh=mesh, in_specs=in_specs, out_specs=out_specs, check_vma=False
    )
```

```python
import functools
import math

import jax
import jax.numpy as jnp
from jax import lax
from jax.experimental import pallas as pl
from jax.experimental.pallas import tpu as pltpu
from jax.sharding import PartitionSpec as P

TRANSFORM_LENGTH = 2048
FILTER_TAPS = 16
SPECTRA_SUMMED = 256
FRAMES = SPECTRA_SUMMED + FILTER_TAPS - 1
ROWS = 272
LANES = 128
BLOCKS = TRANSFORM_LENGTH // LANES
DIRECT = 8
HALVES = SPECTRA_SUMMED // LANES
OCTANT = TRANSFORM_LENGTH // 8


def cos_sin(phase):
    turns = (phase + OCTANT) >> (OCTANT.bit_length())
    angle = (phase - (turns << OCTANT.bit_length())).astype(jnp.float32) * (2.0 * math.pi / TRANSFORM_LENGTH)
    square = angle * angle
    cosine, sine = jnp.zeros_like(angle), jnp.zeros_like(angle)
    for power in range(10, -1, -2):
        sign = -1.0 if power % 4 else 1.0
        cosine = cosine * square + sign / math.factorial(power)
        sine = sine * square + sign / math.factorial(power + 1)
    sine = sine * angle
    odd = (turns & 1) == 1
    first, second = jnp.where(odd, sine, cosine), jnp.where(odd, cosine, sine)
    first = jnp.where(((turns + 1) & 2) == 2, -first, first)
    second = jnp.where((turns & 2) == 2, -second, second)
    return first, second


def parity(place):
    return (place ^ (place >> 1) ^ (place >> 2)) & 1


def dft_blocks(chans, channels_ref):
    lane = lax.broadcasted_iota(jnp.int32, (chans, LANES), 1)
    place = lax.broadcasted_iota(jnp.int32, (chans, chans), 0)
    source = lax.broadcasted_iota(jnp.int32, (chans, chans), 1)
    turned = jnp.where(source == ((place + chans - 2) & (chans - 1)), channels_ref[...], 0)
    channel = jnp.sum(turned.astype(jnp.float32), axis=1, keepdims=True).astype(jnp.int32)
    channel = jnp.broadcast_to(channel, (chans, LANES))

    def unit(phase):
        return cos_sin(phase & (TRANSFORM_LENGTH - 1))

    factor = 1.0 / math.sqrt(TRANSFORM_LENGTH)
    cos0, sin0 = unit(channel * lane)
    blocks = [(cos0 * factor, sin0 * factor)]
    for bit in range(BLOCKS.bit_length() - 1):
        cos1, sin1 = unit(channel * (LANES << bit))
        blocks += [(c * cos1 - s * sin1, s * cos1 + c * sin1) for c, s in blocks]
    return [jnp.concatenate([cosine, -sine], axis=0) for cosine, sine in blocks]


def build_table(chans, blocks, taps_ref, table_ref):
    for nb, dft in enumerate(blocks):
        columns = slice(nb * LANES, (nb + 1) * LANES)
        for tap in range(FILTER_TAPS):
            table_ref[tap * 2 * chans : (tap + 1) * 2 * chans, columns] = (
                dft * taps_ref[tap : tap + 1, columns]
            ).astype(jnp.bfloat16)


def front_kernel(
    own, chans, copies, channels_hbm, mask_hbm, taps_hbm, x_hbm, out_ref,
    channels_ref, mask_ref, taps_ref, x_ref, rest_ref, sorted_ref, table_ref, fold_ref, block_ref,
    sems, small_sems,
):
    small = [
        pltpu.make_async_copy(source, target, small_sems.at[place])
        for place, (source, target) in enumerate(
            ((taps_hbm, taps_ref), (channels_hbm, channels_ref), (mask_hbm, mask_ref))
        )
    ]
    transfers = [
        pltpu.make_async_copy(x_hbm.at[:, nb], x_ref.at[nb, pl.ds(0, FRAMES)], sems.at[nb])
        for nb in range(DIRECT)
    ]
    halves = ((0, ROWS // 2), (ROWS // 2, FRAMES))
    rest = [
        pltpu.make_async_copy(
            x_hbm.at[pl.ds(start, stop - start), pl.ds(DIRECT, BLOCKS - DIRECT)],
            rest_ref.at[pl.ds(start, stop - start)],
            sems.at[DIRECT + part],
        )
        for part, (start, stop) in enumerate(halves)
    ]
    for place, transfer in enumerate(rest + transfers):
        transfer.start(priority=place % 2)
    for transfer in small:
        transfer.start()
    small[1].wait()
    blocks = dft_blocks(chans, channels_ref)
    small[0].wait()
    small[2].wait()
    build_table(chans, blocks, taps_ref, table_ref)
    for part, transfer in enumerate(rest):
        transfer.wait()
        frames = pl.ds(part * (ROWS // 2), ROWS // 2)
        lines = pl.ds(part * (ROWS // 2) * own, ROWS // 2 * own)
        for place in range(BLOCKS - DIRECT):
            sorted_ref[place, lines, :] = rest_ref[frames, place].reshape(ROWS // 2 * own, LANES)
    rows_ref = x_ref.reshape(DIRECT, ROWS * own, LANES)
    for transfer in transfers:
        transfer.wait()
    product = lax.dot_general(
        jnp.concatenate(
            [rows_ref[nb] for nb in range(DIRECT)]
            + [sorted_ref[place] for place in range(BLOCKS - DIRECT)],
            axis=1,
        ),
        table_ref[...],
        (((1,), (1,)), ((), ())),
        preferred_element_type=jnp.float32,
    )
    kinds = 2 * chans
    together = LANES // kinds
    kept = -(-(SPECTRA_SUMMED + together - 1) // 8) * 8
    folded = product[: kept * own, :LANES]
    for group in range(1, FILTER_TAPS // together):
        start = group * together * own
        folded = folded + product[
            start : start + kept * own, group * LANES : (group + 1) * LANES
        ]
    fold_ref[: kept * own, :] = folded
    for i in range(own):
        turned = fold_ref[pl.ds(i, fold_ref.shape[0] // own, stride=own), :].T
        spectra = turned[:kinds, :SPECTRA_SUMMED]
        for tap in range(1, together):
            shifted = pltpu.roll(
                turned[tap * kinds : (tap + 1) * kinds, :], turned.shape[1] - tap, axis=1
            )
            spectra = spectra + shifted[:, :SPECTRA_SUMMED]
        spectra = spectra * mask_ref[:, i : i + 1].astype(jnp.float32)
        for half in range(HALVES):
            for q in range(2):
                block_ref[pl.ds((i * HALVES + half) * 2 + q, chans, stride=4 * own), :] = spectra[
                    q * chans : (q + 1) * chans, half * LANES : (half + 1) * LANES
                ]
    block = block_ref[...].astype(jnp.bfloat16)
    for copy in range(copies):
        out_ref[copy] = block


def back_kernel(
    own, grid_side, tile_map_ref, mine_ref, other_ref, out_ref, wide_ref, signal_ref
):
    slot = lax.broadcasted_iota(jnp.int32, tile_map_ref.shape, 0)
    owner = lax.broadcasted_iota(jnp.int32, tile_map_ref.shape, 1)
    wanted = (slot == lax.axis_index("tile")) & (owner == lax.axis_index("chan"))
    tile = jnp.sum(jnp.where(wanted, tile_map_ref[...].astype(jnp.float32), 0.0)).astype(jnp.int32)
    sources = mine_ref.shape[0]
    inputs = sources * 2 * own
    side = inputs // grid_side
    lines = mine_ref.shape[1] // 2
    pitch = lines + 1
    chan = lax.axis_index("chan")
    core_here = chan & 1
    place_here = lax.axis_index("tile") * (lax.axis_size("chan") // 2) + (chan >> 1)
    group_here = core_here ^ parity(place_here)

    def my_channel(blocks_ref, block):
        both = blocks_ref[block].astype(jnp.float32)
        return jnp.where(core_here == 0, both[:lines], both[lines:])

    for block in range(sources):
        place = (block - 1) % sources
        first_is_mine = group_here == parity(place)
        mine, other = my_channel(mine_ref, block), my_channel(other_ref, block)
        target = pl.ds(place * pitch, lines)
        wide_ref[0, target, :] = jnp.where(first_is_mine, mine, other)
        wide_ref[1, target, :] = jnp.where(first_is_mine, other, mine)
    for core in range(2):
        for i in range(own):
            for half in range(HALVES):
                for q in range(2):
                    line = (i * HALVES + half) * 2 + q
                    target = pl.ds(core * own + i, sources, stride=2 * own)
                    signal_ref[q * HALVES + half, target, :] = wide_ref[
                        core, pl.ds(line, sources, stride=pitch), :
                    ]
    bits = grid_side.bit_length() - 1
    row_start = pl.multiple_of((tile >> bits) * side, side)
    col_start = pl.multiple_of((tile & (grid_side - 1)) * side, side)

    def inputs_from(start):
        planes = [signal_ref[plane, pl.ds(start, side), :] for plane in range(2 * HALVES)]
        return jnp.concatenate(planes, axis=1).astype(jnp.bfloat16)

    rows, cols = inputs_from(row_start), inputs_from(col_start)
    turned = jnp.concatenate([-rows[:, SPECTRA_SUMMED:], rows[:, :SPECTRA_SUMMED]], axis=1)
    product = lax.dot_general(
        jnp.concatenate([rows, turned], axis=0), cols, (((1,), (1,)), ((), ())),
        preferred_element_type=jnp.float32,
    )
    visible = (product * (1.0 / SPECTRA_SUMMED)).astype(jnp.bfloat16)
    for part in range(2):
        out_ref[0, 0, part] = visible[part * side : (part + 1) * side]


def on_device(voltages, fir_taps, channels, input_good_mask, tile_map):
    own = voltages.shape[1]
    chans = channels.shape[0]
    n_chan = lax.axis_size("chan")
    n_tile = lax.axis_size("tile")
    assert chans == n_chan and 2 * chans <= LANES and n_chan & (n_chan - 1) == 0
    chips = n_chan // 2
    order = [n_tile * chips - 1] + list(range(n_tile * chips - 1))
    groups = [[2 * place + (parity(place) ^ group) for place in order] for group in range(2)]
    x = voltages.reshape(own, FRAMES, BLOCKS, LANES).transpose(1, 2, 0, 3)
    operands = (channels.reshape(1, chans), input_good_mask, fir_taps, x)
    hbm = pl.BlockSpec(memory_space=pltpu.HBM)
    vmem = pl.BlockSpec(memory_space=pltpu.VMEM)
    per_block = 2 * HALVES * own
    kinds = 2 * chans
    folded_rows = SPECTRA_SUMMED + (LANES if kinds < LANES else 0)
    spectra = pl.pallas_call(
        functools.partial(front_kernel, own, chans, n_tile),
        out_shape=pltpu.VMEM((n_tile, chans * per_block, LANES), jnp.bfloat16),
        in_specs=[hbm, hbm, hbm, hbm],
        out_specs=vmem,
        scratch_shapes=[
            pltpu.VMEM((1, chans), jnp.int32),
            pltpu.VMEM(input_good_mask.shape, jnp.int32),
            pltpu.VMEM(fir_taps.shape, jnp.float32),
            pltpu.VMEM((DIRECT, ROWS, own, LANES), jnp.bfloat16),
            pltpu.VMEM((ROWS, BLOCKS - DIRECT, own, LANES), jnp.bfloat16),
            pltpu.VMEM((BLOCKS - DIRECT, ROWS * own, LANES), jnp.bfloat16),
            pltpu.VMEM((FILTER_TAPS * kinds, TRANSFORM_LENGTH), jnp.bfloat16),
            pltpu.VMEM((own * folded_rows, LANES), jnp.float32),
            pltpu.VMEM((chans * per_block, LANES), jnp.float32),
            pltpu.SemaphoreType.DMA((DIRECT + 2,)),
            pltpu.SemaphoreType.DMA((3,)),
        ],
        compiler_params=pltpu.CompilerParams(vmem_limit_bytes=32 << 20),
        name="front",
    )(*(pltpu.with_memory_space_constraint(v, pltpu.HBM) for v in operands))
    spectra = spectra.reshape(n_tile * chips, 2 * per_block, LANES)
    mine = lax.all_to_all(
        spectra, ("tile", "chan"), split_axis=0, concat_axis=0, axis_index_groups=groups, tiled=True
    )
    other = lax.ppermute(mine, "chan", [(c, c ^ 1) for c in range(n_chan)])
    grid_side = n_tile // 8 + 2
    inputs = n_tile * n_chan * own
    side = inputs // grid_side
    return pl.pallas_call(
        functools.partial(back_kernel, own, grid_side),
        out_shape=jax.ShapeDtypeStruct((1, 1, 2, side, side), jnp.bfloat16),
        in_specs=[vmem, vmem, vmem],
        out_specs=vmem,
        scratch_shapes=[
            pltpu.VMEM((2, n_tile * chips * (per_block + 1), LANES), jnp.float32),
            pltpu.VMEM((2 * HALVES, inputs, LANES), jnp.float32),
        ],
        compiler_params=pltpu.CompilerParams(vmem_limit_bytes=(4 << 20) + 60 * inputs * LANES * own),
        name="back",
    )(tile_map.T, mine, other)


def solution(mesh):
    in_specs = (P("tile", "chan", None), P(), P(), P("tile", "chan"), P())
    out_specs = P("chan", "tile", None, None, None)
    return jax.shard_map(
        on_device, mesh=mesh, in_specs=in_specs, out_specs=out_specs, check_vma=False
    )
```

```python
import functools
import math

import jax
import jax.numpy as jnp
from jax import lax
from jax.experimental import pallas as pl
from jax.experimental.pallas import tpu as pltpu
from jax.sharding import PartitionSpec as P

TRANSFORM_LENGTH = 2048
FILTER_TAPS = 16
SPECTRA_SUMMED = 256
FRAMES = SPECTRA_SUMMED + FILTER_TAPS - 1
ROWS = 272
LANES = 128
BLOCKS = TRANSFORM_LENGTH // LANES
DIRECT = 12
HALVES = SPECTRA_SUMMED // LANES
OCTANT = TRANSFORM_LENGTH // 8


def cos_sin(phase):
    turns = (phase + OCTANT) >> (OCTANT.bit_length())
    angle = (phase - (turns << OCTANT.bit_length())).astype(jnp.float32) * (2.0 * math.pi / TRANSFORM_LENGTH)
    square = angle * angle
    cosine, sine = jnp.zeros_like(angle), jnp.zeros_like(angle)
    for power in range(10, -1, -2):
        sign = -1.0 if power % 4 else 1.0
        cosine = cosine * square + sign / math.factorial(power)
        sine = sine * square + sign / math.factorial(power + 1)
    sine = sine * angle
    odd = (turns & 1) == 1
    first, second = jnp.where(odd, sine, cosine), jnp.where(odd, cosine, sine)
    first = jnp.where(((turns + 1) & 2) == 2, -first, first)
    second = jnp.where((turns & 2) == 2, -second, second)
    return first, second


def parity(place):
    return (place ^ (place >> 1) ^ (place >> 2)) & 1


def dft_blocks(chans, channels_ref):
    lane = lax.broadcasted_iota(jnp.int32, (chans, LANES), 1)
    place = lax.broadcasted_iota(jnp.int32, (chans, chans), 0)
    source = lax.broadcasted_iota(jnp.int32, (chans, chans), 1)
    turned = jnp.where(source == ((place + chans - 2) & (chans - 1)), channels_ref[...], 0)
    channel = jnp.sum(turned.astype(jnp.float32), axis=1, keepdims=True).astype(jnp.int32)
    channel = jnp.broadcast_to(channel, (chans, LANES))

    def unit(phase):
        return cos_sin(phase & (TRANSFORM_LENGTH - 1))

    factor = 1.0 / math.sqrt(TRANSFORM_LENGTH)
    cos0, sin0 = unit(channel * lane)
    blocks = [(cos0 * factor, sin0 * factor)]
    for bit in range(BLOCKS.bit_length() - 1):
        cos1, sin1 = unit(channel * (LANES << bit))
        blocks += [(c * cos1 - s * sin1, s * cos1 + c * sin1) for c, s in blocks]
    return [jnp.concatenate([cosine, -sine], axis=0) for cosine, sine in blocks]


def build_table(blocks, taps_ref, table_ref):
    for nb, dft in enumerate(blocks):
        columns = slice(nb * LANES, (nb + 1) * LANES)
        scaled = [dft * taps_ref[tap : tap + 1, columns] for tap in range(FILTER_TAPS)]
        table_ref[columns, :] = jnp.concatenate(scaled, axis=0).astype(jnp.bfloat16).T


def front_kernel(
    own, chans, copies, channels_hbm, mask_hbm, taps_hbm, x_hbm, out_ref,
    channels_ref, mask_ref, taps_ref, x_ref, rest_ref, sorted_ref, table_ref, fold_ref, block_ref,
    sems, small_sems,
):
    small = [
        pltpu.make_async_copy(source, target, small_sems.at[place])
        for place, (source, target) in enumerate(
            ((taps_hbm, taps_ref), (channels_hbm, channels_ref), (mask_hbm, mask_ref))
        )
    ]
    transfers = [
        pltpu.make_async_copy(x_hbm.at[:, nb], x_ref.at[nb, pl.ds(0, FRAMES)], sems.at[nb])
        for nb in range(DIRECT)
    ]
    halves = ((0, ROWS // 2), (ROWS // 2, FRAMES))
    rest = [
        pltpu.make_async_copy(
            x_hbm.at[pl.ds(start, stop - start), pl.ds(DIRECT, BLOCKS - DIRECT)],
            rest_ref.at[pl.ds(start, stop - start)],
            sems.at[DIRECT + part],
        )
        for part, (start, stop) in enumerate(halves)
    ]
    for transfer in small:
        transfer.start()
    for place, transfer in enumerate(rest + transfers):
        transfer.start(priority=place % 2)
    small[1].wait()
    blocks = dft_blocks(chans, channels_ref)
    small[0].wait()
    small[2].wait()
    build_table(blocks, taps_ref, table_ref)
    for part, transfer in enumerate(rest):
        transfer.wait()
        frames = pl.ds(part * (ROWS // 2), ROWS // 2)
        lines = pl.ds(part * (ROWS // 2) * own, ROWS // 2 * own)
        for place in range(BLOCKS - DIRECT):
            sorted_ref[place, lines, :] = rest_ref[frames, place].reshape(ROWS // 2 * own, LANES)
    rows_ref = x_ref.reshape(DIRECT, ROWS * own, LANES)
    for transfer in transfers:
        transfer.wait()
    product = lax.dot_general(
        jnp.concatenate(
            [rows_ref[nb] for nb in range(DIRECT)]
            + [sorted_ref[place] for place in range(BLOCKS - DIRECT)],
            axis=1,
        ),
        table_ref[...],
        (((1,), (0,)), ((), ())),
        preferred_element_type=jnp.float32,
    )
    kinds = 2 * chans
    together = LANES // kinds
    kept = -(-(SPECTRA_SUMMED + together - 1) // 8) * 8
    folded = product[: kept * own, :LANES]
    for group in range(1, FILTER_TAPS // together):
        start = group * together * own
        folded = folded + product[
            start : start + kept * own, group * LANES : (group + 1) * LANES
        ]
    fold_ref[: kept * own, :] = folded
    for i in range(own):
        turned = fold_ref[pl.ds(i, fold_ref.shape[0] // own, stride=own), :].T
        spectra = turned[:kinds, :SPECTRA_SUMMED]
        for tap in range(1, together):
            shifted = pltpu.roll(
                turned[tap * kinds : (tap + 1) * kinds, :], turned.shape[1] - tap, axis=1
            )
            spectra = spectra + shifted[:, :SPECTRA_SUMMED]
        spectra = spectra * mask_ref[:, i : i + 1].astype(jnp.float32)
        for half in range(HALVES):
            for q in range(2):
                block_ref[pl.ds((i * HALVES + half) * 2 + q, chans, stride=4 * own), :] = spectra[
                    q * chans : (q + 1) * chans, half * LANES : (half + 1) * LANES
                ]
    block = block_ref[...].astype(jnp.bfloat16)
    for copy in range(copies):
        out_ref[copy] = block


def back_kernel(
    own, grid_side, tile_map_ref, mine_ref, other_ref, out_ref, wide_ref, signal_ref
):
    slot = lax.broadcasted_iota(jnp.int32, tile_map_ref.shape, 0)
    owner = lax.broadcasted_iota(jnp.int32, tile_map_ref.shape, 1)
    wanted = (slot == lax.axis_index("tile")) & (owner == lax.axis_index("chan"))
    tile = jnp.sum(jnp.where(wanted, tile_map_ref[...].astype(jnp.float32), 0.0)).astype(jnp.int32)
    sources = mine_ref.shape[0]
    inputs = sources * 2 * own
    side = inputs // grid_side
    lines = mine_ref.shape[1] // 2
    pitch = lines + 1
    chan = lax.axis_index("chan")
    core_here = chan & 1
    place_here = lax.axis_index("tile") * (lax.axis_size("chan") // 2) + (chan >> 1)
    group_here = core_here ^ parity(place_here)

    def my_channel(blocks_ref, block):
        both = blocks_ref[block].astype(jnp.float32)
        return jnp.where(core_here == 0, both[:lines], both[lines:])

    for block in range(sources):
        place = (block - 1) % sources
        first_is_mine = group_here == parity(place)
        mine, other = my_channel(mine_ref, block), my_channel(other_ref, block)
        target = pl.ds(place * pitch, lines)
        wide_ref[0, target, :] = jnp.where(first_is_mine, mine, other)
        wide_ref[1, target, :] = jnp.where(first_is_mine, other, mine)
    for core in range(2):
        for i in range(own):
            for half in range(HALVES):
                for q in range(2):
                    line = (i * HALVES + half) * 2 + q
                    target = pl.ds(core * own + i, sources, stride=2 * own)
                    signal_ref[q * HALVES + half, target, :] = wide_ref[
                        core, pl.ds(line, sources, stride=pitch), :
                    ]
    bits = grid_side.bit_length() - 1
    row_start = pl.multiple_of((tile >> bits) * side, side)
    col_start = pl.multiple_of((tile & (grid_side - 1)) * side, side)

    def inputs_from(start):
        planes = [signal_ref[plane, pl.ds(start, side), :] for plane in range(2 * HALVES)]
        return jnp.concatenate(planes, axis=1).astype(jnp.bfloat16)

    rows, cols = inputs_from(row_start), inputs_from(col_start)
    turned = jnp.concatenate([-rows[:, SPECTRA_SUMMED:], rows[:, :SPECTRA_SUMMED]], axis=1)
    product = lax.dot_general(
        jnp.concatenate([rows, turned], axis=0), cols, (((1,), (1,)), ((), ())),
        preferred_element_type=jnp.float32,
    )
    visible = (product * (1.0 / SPECTRA_SUMMED)).astype(jnp.bfloat16)
    for part in range(2):
        out_ref[0, 0, part] = visible[part * side : (part + 1) * side]


def on_device(voltages, fir_taps, channels, input_good_mask, tile_map):
    own = voltages.shape[1]
    chans = channels.shape[0]
    n_chan = lax.axis_size("chan")
    n_tile = lax.axis_size("tile")
    assert chans == n_chan and 2 * chans <= LANES and n_chan & (n_chan - 1) == 0
    chips = n_chan // 2
    order = [n_tile * chips - 1] + list(range(n_tile * chips - 1))
    groups = [[2 * place + (parity(place) ^ group) for place in order] for group in range(2)]
    x = voltages.reshape(own, FRAMES, BLOCKS, LANES).transpose(1, 2, 0, 3)
    operands = (channels.reshape(1, chans), input_good_mask, fir_taps, x)
    hbm = pl.BlockSpec(memory_space=pltpu.HBM)
    vmem = pl.BlockSpec(memory_space=pltpu.VMEM)
    per_block = 2 * HALVES * own
    kinds = 2 * chans
    folded_rows = SPECTRA_SUMMED + (LANES if kinds < LANES else 0)
    spectra = pl.pallas_call(
        functools.partial(front_kernel, own, chans, n_tile),
        out_shape=pltpu.VMEM((n_tile, chans * per_block, LANES), jnp.bfloat16),
        in_specs=[hbm, hbm, hbm, hbm],
        out_specs=vmem,
        scratch_shapes=[
            pltpu.VMEM((1, chans), jnp.int32),
            pltpu.VMEM(input_good_mask.shape, jnp.int32),
            pltpu.VMEM(fir_taps.shape, jnp.float32),
            pltpu.VMEM((DIRECT, ROWS, own, LANES), jnp.bfloat16),
            pltpu.VMEM((ROWS, BLOCKS - DIRECT, own, LANES), jnp.bfloat16),
            pltpu.VMEM((BLOCKS - DIRECT, ROWS * own, LANES), jnp.bfloat16),
            pltpu.VMEM((TRANSFORM_LENGTH, FILTER_TAPS * kinds), jnp.bfloat16),
            pltpu.VMEM((own * folded_rows, LANES), jnp.float32),
            pltpu.VMEM((chans * per_block, LANES), jnp.float32),
            pltpu.SemaphoreType.DMA((DIRECT + 2,)),
            pltpu.SemaphoreType.DMA((3,)),
        ],
        compiler_params=pltpu.CompilerParams(vmem_limit_bytes=32 << 20),
        name="front",
    )(*(pltpu.with_memory_space_constraint(v, pltpu.HBM) for v in operands))
    spectra = spectra.reshape(n_tile * chips, 2 * per_block, LANES)
    mine = lax.all_to_all(
        spectra, ("tile", "chan"), split_axis=0, concat_axis=0, axis_index_groups=groups, tiled=True
    )
    other = lax.ppermute(mine, "chan", [(c, c ^ 1) for c in range(n_chan)])
    grid_side = n_tile // 8 + 2
    inputs = n_tile * n_chan * own
    side = inputs // grid_side
    return pl.pallas_call(
        functools.partial(back_kernel, own, grid_side),
        out_shape=jax.ShapeDtypeStruct((1, 1, 2, side, side), jnp.bfloat16),
        in_specs=[vmem, vmem, vmem],
        out_specs=vmem,
        scratch_shapes=[
            pltpu.VMEM((2, n_tile * chips * (per_block + 1), LANES), jnp.float32),
            pltpu.VMEM((2 * HALVES, inputs, LANES), jnp.float32),
        ],
        compiler_params=pltpu.CompilerParams(vmem_limit_bytes=(4 << 20) + 60 * inputs * LANES * own),
        name="back",
    )(tile_map.T, mine, other)


def solution(mesh):
    in_specs = (P("tile", "chan", None), P(), P(), P("tile", "chan"), P())
    out_specs = P("chan", "tile", None, None, None)
    return jax.shard_map(
        on_device, mesh=mesh, in_specs=in_specs, out_specs=out_specs, check_vma=False
    )
```
